256 devices in a mesh: tm: 32 (over z, x_hi, core), tok: 8 (over x_lo, y).
Axes of the slice: x: 4 (x_hi: 2, x_lo: 2; x = x_hi * 2 + x_lo), y: 4, z: 8, core: 2. Of those that a mesh axis runs over, the one named last changes fastest.
Arguments:
- latents: bfloat16 [64, 1024, 1536], P('tm', 'tok'), may hold values from -6 to 6
- fresh_noise: bfloat16 [1024, 1536], P('tok'), may hold values from -6 to 6
- noise_levels: int32 [64], replicated, may hold values from 0 to 31
- offset: int32 [1], replicated, may hold values from 0 to 63
- block_ids: int32 [64], replicated, may hold values from 0 to 31, never falling along the last dimension, each value on 1 to 4 neighbouring positions
- mod_table: float32 [32, 3, 1536], replicated, may hold values from -4 to 4
- step_sizes: float32 [32], replicated, may hold values from 0.25 to 1
- w_query: bfloat16 [1536, 768], replicated, as said below
- w_key: bfloat16 [1536, 768], replicated, as said below
- w_value: bfloat16 [1536, 768], replicated, may hold values from -0.15625 to 0.15625
- w_out: bfloat16 [768, 1536], replicated, may hold values from -0.21875 to 0.21875
Outputs:
- velocity: bfloat16 [64, 1024, 1536], P('tm', 'tok')
- next_window: bfloat16 [64, 1024, 1536], P('tm', 'tok')
The draws below stay inside these ranges and needn't reach their ends.
Inputs may be any that keep to these rules, and one draw needn't show every extreme that they name: `block_ids`: never falling along the window; each block holds 1 to 4 consecutive frames. `w_query`: entries lie within 20 over the square root of 1536 in magnitude. `w_key`: entries lie within 20 over the square root of 1536 in magnitude.
All inputs are finite; a program needn't handle non-finite values.
Results may differ from the reference program's by a relative error of at most 0.008.
Values may be sent and summed in bfloat16 or wider, within the bound.
No kernel may reach another device: no remote copies, remote signals or barrier semaphores. Data moves between devices by JAX's collectives and lax.ppermute only.
A program may use at most 128 MiB of HBM per device.

```python
import math
import jax
import jax.numpy as jnp
import numpy as np
from jax import lax

D = 1536
HEAD_DIM = 128
HEADS = 6
LEVELS = 32
FRAMES = 64
FRAME_TOK = 1024


def shared_base(key):
    return jax.random.normal(key, (D, HEADS * HEAD_DIM), jnp.float32)


def head_levels(key, strong_level, weak_level):
    head_order = jax.random.permutation(jax.random.fold_in(key, 7), HEADS)
    per_head = jnp.where(head_order < (HEADS + 1) // 2, strong_level, weak_level).astype(jnp.float32)
    return jnp.repeat(per_head, HEAD_DIM)[None, :]


def finish_weight(values):
    bound_value = 20.0 / math.sqrt(D)
    return jnp.clip(values, -bound_value, bound_value).astype(jnp.bfloat16)


def draw_latents(key, part):
    key = jax.random.fold_in(key, 21)
    static_key, frame_key = jax.random.split(key, 2)
    static = jax.random.normal(static_key, (FRAME_TOK, D), jnp.float32)
    moving = jax.random.normal(frame_key, (FRAMES, FRAME_TOK, D), jnp.float32)
    mixing = jnp.full((FRAME_TOK, 1), 0.32, jnp.float32)
    values = jnp.sqrt(1.0 - mixing * mixing)[None] * static[None] + mixing[None] * moving
    return jnp.clip(values, -6.0, 6.0).astype(jnp.bfloat16)


def draw_w_query(key, part):
    shared = shared_base(key)
    factors = head_levels(key, 0.72, 0.72)
    key = jax.random.fold_in(key, 11)
    own_part = jax.random.normal(key, (D, HEADS * HEAD_DIM), jnp.float32)
    return finish_weight(factors * (shared + 0.2 * own_part) / math.sqrt(D))


def draw_w_key(key, part):
    shared = shared_base(key)
    factors = head_levels(key, 0.72, 0.72)
    key = jax.random.fold_in(key, 12)
    own_part = jax.random.normal(key, (D, HEADS * HEAD_DIM), jnp.float32)
    return finish_weight(factors * (shared + 0.2 * own_part) / math.sqrt(D))


def plant(result, rng, low, high):
    dims = result.shape
    place = [jax.random.randint(jax.random.fold_in(rng, axis), (), 0, dims[axis]) for axis in range(len(dims))]
    result = result.at[tuple(place)].set(low)
    longest = dims.index(max(dims))
    place[longest] = (place[longest] + 1) % dims[longest]
    return result.at[tuple(place)].set(high)


def block_levels(key, dims, shards, low, largest):
    def one(position, shards_of):
        steps = jax.random.uniform(jax.random.fold_in(jax.random.fold_in(key, 6), position), (shards_of,), jnp.float32, low / len(shards), largest / len(shards))
        return jnp.repeat(jnp.exp(steps), dims[position] // shards_of).reshape((-1,) + (1,) * (len(dims) - position - 1))

    level = one(*shards[0])
    for cut in shards[1:]:
        level = level * one(*cut)
    return level


def split_up(count, total, limit, lean):
    portions = [(1 << 20) // math.isqrt(rank ** lean) + 1 for rank in range(2, count + 1)]
    spare, counts = total - limit - (count - 1), [1] * (count - 1)
    while spare > 0:
        free = [i for i in range(count - 1) if counts[i] < limit]
        mass, left = sum([portions[i] for i in free]), spare
        for i in free:
            more = min(limit - counts[i], max(1, left * portions[i] // mass), spare)
            counts[i] = counts[i] + more
            spare = spare - more
    return np.array([limit] + counts)


def ragged(key, amount, total, reach, skew):
    if amount == 2:
        one = jax.random.randint(key, (), max(1, total - reach), min(reach, total - 1) + 1)
        return jnp.stack([one, total - one])
    tallies = jnp.asarray(split_up(amount, total, reach, skew), jnp.int32)
    couples = (amount - 1) // 2
    giver, sink = tallies[1:1 + 2 * couples:2], tallies[2:2 + 2 * couples:2]
    room = jnp.minimum(giver - 1, reach - sink)
    passed = jax.random.randint(jax.random.fold_in(key, 1), (couples,), 0, 1 << 20) % (room + 1)
    tallies = tallies.at[1:1 + 2 * couples:2].set(giver - passed).at[2:2 + 2 * couples:2].set(sink + passed)
    return tallies[jax.random.permutation(jax.random.fold_in(key, 2), amount)]


def centred(rng, extent, scale, reach, shards=(), kind=jnp.bfloat16):
    entries = jax.random.normal(rng, extent, jnp.float32) * scale
    if len(shards) > 0:
        entries = block_levels(rng, extent, shards, -0.22, 0.18) * entries
    return jnp.clip(entries, min=-reach, max=reach).astype(kind)


def setup_inputs(seed: int = 0) -> dict:
    streams_of = jax.random.split(jax.random.key(seed), 12)
    return {
        "latents": draw_latents(jax.random.fold_in(streams_of[11], 71), 0),
        "fresh_noise": centred(streams_of[1], (FRAME_TOK, D), 1.0, 6.0, ((0, 8),)),
        "noise_levels": plant(jax.random.randint(streams_of[2], (FRAMES,), 0, LEVELS), jax.random.fold_in(streams_of[2], 1), 0, LEVELS - 1).astype(jnp.int32),
        "offset": jax.random.randint(streams_of[3], (1,), 0, FRAMES).astype(jnp.int32),
        "block_ids": jnp.searchsorted(jnp.cumsum(ragged(streams_of[4], FRAMES // 2, FRAMES, 4, 0)), jnp.arange(FRAMES), side="right").astype(jnp.int32),
        "mod_table": centred(streams_of[5], (LEVELS, 3, D), 0.6, 4.0, (), jnp.float32),
        "step_sizes": jnp.clip(jnp.exp(jax.random.uniform(streams_of[6], (LEVELS,), jnp.float32, math.log(0.25), math.log(1.0))), 0.25, 1.0),
        "w_query": draw_w_query(jax.random.fold_in(streams_of[11], 71), 0),
        "w_key": draw_w_key(jax.random.fold_in(streams_of[11], 71), 0),
        "w_value": centred(streams_of[9], (D, HEADS * HEAD_DIM), D ** -0.5, 0.15625),
        "w_out": centred(streams_of[10], (HEADS * HEAD_DIM, D), (HEADS * HEAD_DIM) ** -0.5, 0.21875),
    }


NEG_FILL = -1e+30

def modulation(frame_ids, noise_levels, offset, mod_table, step_sizes):
    total_frames = noise_levels.shape[0]
    slots = (frame_ids + offset[0]) % total_frames
    slot_hits = slots[:, None] == jnp.arange(total_frames, dtype=jnp.int32)[None, :]
    level_ids = lax.optimization_barrier(jnp.sum(jnp.where(slot_hits, noise_levels[None, :], 0), axis=1))
    level_count = mod_table.shape[0]
    one_hot = (level_ids[:, None] == jnp.arange(level_count, dtype=jnp.int32)[None, :]).astype(jnp.float32)
    mods = jnp.dot(one_hot, mod_table.reshape(level_count, -1), precision=lax.Precision.HIGHEST)
    mods = mods.reshape(frame_ids.shape[0], 3, mod_table.shape[2])
    steps_now = jnp.dot(one_hot, step_sizes[:, None], precision=lax.Precision.HIGHEST)[:, 0]
    return (mods[:, 0], mods[:, 1], mods[:, 2], steps_now)

def project(latents, shift, scale, w_query, w_key, w_value):
    values = latents.astype(jnp.float32)
    center = lax.optimization_barrier(jnp.mean(values, axis=-1, keepdims=True))
    spread = lax.optimization_barrier(jnp.mean(jnp.square(values - center), axis=-1, keepdims=True))
    normed = (values - center) * lax.rsqrt(spread + 1e-06) * (1.0 + scale[:, None, :]) + shift[:, None, :]
    normed = normed.astype(jnp.bfloat16)
    flattened = normed.reshape(-1, normed.shape[-1])
    projected = [jnp.dot(flattened, weight, preferred_element_type=jnp.float32).astype(jnp.bfloat16) for weight in (w_query, w_key, w_value)]
    return (values, projected)

def rounded(weights):
    return lax.optimization_barrier(weights.astype(jnp.bfloat16)).astype(jnp.float32)

def reference(latents, fresh_noise, noise_levels, offset, block_ids, mod_table, step_sizes, w_query, w_key, w_value, w_out):
    total_frames, frame_tokens, width = latents.shape
    frame_ids = jnp.arange(total_frames, dtype=jnp.int32)
    shift, scale, gate, steps_now = modulation(frame_ids, noise_levels, offset, mod_table, step_sizes)
    values, projected = project(latents, shift, scale, w_query, w_key, w_value)
    shaped = [part.astype(jnp.float32).reshape(total_frames, frame_tokens, HEADS, HEAD_DIM) for part in projected]
    queries, key_rows, value_rows = shaped
    score_scale = HEAD_DIM ** (-0.5)
    allowed = (block_ids[None, :] <= block_ids[:, None]) & (frame_ids[None, :] != frame_ids[:, None])
    temporal = jnp.einsum('fphd,gphd->fphg', queries, key_rows) * score_scale
    temporal = jnp.where(allowed[:, None, None, :], temporal, NEG_FILL)

    def per_frame(inputs):
        query_frame, key_frame, value_frame, temporal_frame, allowed_row = inputs
        spatial = jnp.einsum('phd,khd->phk', query_frame, key_frame) * score_scale
        row_max = jnp.maximum(lax.optimization_barrier(jnp.max(spatial, axis=-1)), lax.optimization_barrier(jnp.max(temporal_frame, axis=-1)))
        spatial_w = jnp.exp(spatial - row_max[..., None])
        temporal_w = jnp.where(allowed_row[None, None, :], jnp.exp(temporal_frame - row_max[..., None]), 0.0)
        row_sum = lax.optimization_barrier(jnp.sum(spatial_w, axis=-1)) + lax.optimization_barrier(jnp.sum(temporal_w, axis=-1))
        mixed = jnp.einsum('phk,khd->phd', rounded(spatial_w), value_frame) + jnp.einsum('phg,gphd->phd', rounded(temporal_w), value_rows)
        return (mixed / row_sum[..., None]).astype(jnp.bfloat16)
    attended = lax.map(per_frame, (queries, key_rows, value_rows, temporal, allowed))
    flat_attended = attended.reshape(-1, HEADS * HEAD_DIM)
    projected_out = jnp.dot(flat_attended, w_out, preferred_element_type=jnp.float32).reshape(total_frames, frame_tokens, width)
    moving = gate[:, None, :] * projected_out
    advanced = (values + steps_now[:, None, None] * moving).astype(jnp.bfloat16)
    next_window = jnp.concatenate([advanced[1:], fresh_noise[None]], axis=0)
    return (moving.astype(jnp.bfloat16), next_window)
```

```python
import math

import jax
import jax.numpy as jnp
from jax import lax
from jax.experimental import pallas as pl
from jax.experimental.pallas import tpu as pltpu
from jax.sharding import PartitionSpec as P

HEAD_DIM = 128
HEADS = 6
FULL = 4
BASE2 = HEAD_DIM ** (-0.5) * math.log2(math.e)
MASKED = -1e30
FLOOR = -1e29
MIB = 1 << 20
STAT_ROWS = 16


def whole():
    return pl.BlockSpec(memory_space=pltpu.VMEM)


def normalise(x, scale1, shift):
    values = x.astype(jnp.float32)
    center = jnp.mean(values, axis=-1, keepdims=True)
    values = values - center
    spread = jnp.mean(values * values, axis=-1, keepdims=True)
    return (values * lax.rsqrt(spread + 1e-06) * scale1 + shift).astype(jnp.bfloat16)


def matmul(a, b):
    return jnp.dot(a, b, preferred_element_type=jnp.float32)


def attend(q, k, v, bias=None):
    scores = lax.dot_general(q, k, (((1,), (1,)), ((), ())), preferred_element_type=jnp.float32)
    if bias is not None:
        scores = scores + bias
    top = jnp.max(scores, axis=-1, keepdims=True)
    if bias is not None:
        top = jnp.maximum(top, FLOOR)
    weights = jnp.exp2((scores - top) * BASE2)
    total = jnp.sum(weights, axis=-1, keepdims=True)
    mixed = matmul(weights.astype(jnp.bfloat16), v)
    if bias is None:
        return mixed / total, top * BASE2 + jnp.log2(total)
    some = total > 0.0
    safe = jnp.where(some, total, 1.0)
    return mixed / safe, jnp.where(some, top * BASE2 + jnp.log2(safe), MASKED)


def split3(x):
    one = x.astype(jnp.bfloat16).astype(jnp.float32)
    rest = x - one
    two = rest.astype(jnp.bfloat16).astype(jnp.float32)
    return one, two, rest - two


def home_kernel(x_ref, mods_ref, wq_ref, wk_ref, wv_ref, out_ref):
    frames, tokens, _ = x_ref.shape
    rows = []
    for f in range(frames):
        rows.append(normalise(x_ref[f], mods_ref[f, 1:2, :] + 1.0, mods_ref[f, 0:1, :]))
    normed = jnp.concatenate(rows, axis=0)
    half = tokens // 2
    q, k, v = [matmul(normed, w[...]).astype(jnp.bfloat16) for w in (wq_ref, wk_ref, wv_ref)]
    for j in range(2 * FULL):
        f, unit = j // FULL, j % FULL
        r = slice(f * tokens, (f + 1) * tokens)
        own = slice(unit * HEAD_DIM, (unit + 1) * HEAD_DIM)
        pair = FULL + unit // 2
        shared = slice(pair * HEAD_DIM, (pair + 1) * HEAD_DIM)
        out_ref[j, 0:tokens] = q[r, own]
        out_ref[j, tokens : 2 * tokens] = k[r, own]
        out_ref[j, 2 * tokens : 3 * tokens] = v[r, own]
        out_ref[j, 3 * tokens : 4 * tokens] = k[r, shared]
        out_ref[j, 4 * tokens : 5 * tokens] = v[r, shared]
        begin = f * tokens + (unit % 2) * half
        out_ref[j, 5 * tokens : 5 * tokens + half] = q[begin : begin + half, shared]


def spatial_kernel(in_ref, out_ref):
    count = in_ref.shape[0]
    tokens, half = HEAD_DIM, HEAD_DIM // 2

    def part(first, rows):
        return in_ref[:, first : first + rows, :].reshape(count * rows, HEAD_DIM)

    keys, vals = part(tokens, tokens), part(2 * tokens, tokens)
    shared_keys, shared_vals = part(3 * tokens, tokens), part(4 * tokens, tokens)
    lane = lax.broadcasted_iota(jnp.int32, (tokens, HEAD_DIM), 1)
    for s in range(0, count, 2):
        q = in_ref[s : s + 2, 0:tokens, :].reshape(2 * tokens, HEAD_DIM)
        mixed, logs = attend(q, keys, vals)
        q2 = in_ref[s : s + 2, 5 * tokens : 5 * tokens + half, :].reshape(2 * half, HEAD_DIM)
        mixed2, logs2 = attend(q2, shared_keys, shared_vals)
        mixed, mixed2 = mixed.astype(jnp.bfloat16), mixed2.astype(jnp.bfloat16)
        for d in range(2):
            out_ref[s + d, 0:tokens] = mixed[d * tokens : (d + 1) * tokens]
            out_ref[s + d, tokens : tokens + half] = mixed2[d * half : (d + 1) * half]
            stats = jnp.zeros((tokens, HEAD_DIM), jnp.float32)
            for n, piece in enumerate(split3(logs[d * tokens : (d + 1) * tokens])):
                stats = jnp.where(lane == n, piece, stats)
            own = logs2[d * half : (d + 1) * half]
            for n, piece in enumerate(split3(jnp.concatenate([own, own], axis=0))):
                stats = jnp.where(lane == 3 + n, piece, stats)
            turned = jnp.transpose(stats)[0:STAT_ROWS]
            out_ref[s + d, tokens + half : tokens + half + STAT_ROWS] = turned.astype(jnp.bfloat16)


def temporal_kernel(x_ref, scale_ref, shift_ref, bias_ref, wq_ref, wk_ref, wv_ref, out_ref):
    normed = normalise(x_ref[...], scale_ref[...] + 1.0, shift_ref[...])
    q, k, v = [matmul(normed, w[...]).astype(jnp.bfloat16) for w in (wq_ref, wk_ref, wv_ref)]
    bias = bias_ref[...]
    rows = x_ref.shape[0]
    lane = lax.broadcasted_iota(jnp.int32, (rows, HEAD_DIM), 1)
    stats = jnp.zeros((rows, HEAD_DIM), jnp.float32)
    for h in range(HEADS):
        own = slice(h * HEAD_DIM, (h + 1) * HEAD_DIM)
        mixed, logs = attend(q[:, own], k[:, own], v[:, own], bias)
        out_ref[:, own] = mixed.astype(jnp.bfloat16)
        for n, piece in enumerate(split3(logs)):
            stats = jnp.where(lane == 8 * n + h, piece, stats)
    out_ref[:, HEADS * HEAD_DIM :] = stats.astype(jnp.bfloat16)


def merge_kernel(steps_ref, x_ref, gate_ref, space_ref, time_ref, wout_ref, vel_ref, next_ref, first_ref):
    frames, tokens, _ = x_ref.shape
    half = tokens // 2
    width = time_ref.shape[1]
    turned = time_ref[...].astype(jnp.float32).reshape(tokens // 8, 2, 8, width)
    low = lax.broadcasted_iota(jnp.int32, (tokens // 8, 8, width), 1) < 4
    even, odd = turned[:, 0], turned[:, 1]
    by_frame = [
        jnp.where(low, even, pltpu.roll(odd, 4, 1)).reshape(tokens, width),
        jnp.where(low, pltpu.roll(even, 4, 1), odd).reshape(tokens, width),
    ]
    lane = lax.broadcasted_iota(jnp.int32, (1, HEAD_DIM), 1)
    attended = []
    for f in range(frames):
        stats = by_frame[f][:, HEADS * HEAD_DIM :]
        time_log = stats[:, 0:8] + stats[:, 8:16] + stats[:, 16:24]
        log_rows = []
        for h in range(FULL):
            log_rows.append(log_row(space_ref, f * FULL + h, 0))
        for h in range(HEADS - FULL):
            j = f * FULL + 2 * h
            log_rows.append(jnp.where(lane < half, log_row(space_ref, j, 3), log_row(space_ref, j + 1, 3)))
        log_rows.append(jnp.zeros((8 - HEADS, HEAD_DIM), jnp.float32))
        space_log = jnp.transpose(jnp.concatenate(log_rows, axis=0))
        of_space = 1.0 / (1.0 + jnp.exp2(time_log - space_log))
        of_time = 1.0 / (1.0 + jnp.exp2(space_log - time_log))
        parts = []
        for h in range(HEADS):
            if h < FULL:
                near = space_ref[f * FULL + h, 0:tokens]
            else:
                j = f * FULL + 2 * (h - FULL)
                near = jnp.concatenate(
                    [space_ref[j + side, tokens : tokens + half] for side in range(2)], axis=0
                )
            far = by_frame[f][:, h * HEAD_DIM : (h + 1) * HEAD_DIM]
            mixed = of_space[:, h : h + 1] * near.astype(jnp.float32) + of_time[:, h : h + 1] * far
            parts.append(mixed.astype(jnp.bfloat16))
        attended.append(jnp.concatenate(parts, axis=1))
    projected = matmul(jnp.concatenate(attended, axis=0), wout_ref[...])
    for f in range(frames):
        moving = projected[f * tokens : (f + 1) * tokens] * gate_ref[f : f + 1, :]
        vel_ref[f] = moving.astype(jnp.bfloat16)
        advanced = (x_ref[f].astype(jnp.float32) + steps_ref[f] * moving).astype(jnp.bfloat16)
        if f == 0:
            first_ref[...] = advanced
        else:
            next_ref[f - 1] = advanced


def log_row(space_ref, j, first):
    begin = space_ref.shape[1] - STAT_ROWS
    st = space_ref[j, begin : begin + STAT_ROWS].astype(jnp.float32)
    return st[first : first + 1] + st[first + 1 : first + 2] + st[first + 2 : first + 3]


def kernel_call(kernel, out_shapes, flops, nbytes, vmem=32, smem_first=False):
    def call(*args):
        specs = [whole() for _ in args]
        if smem_first:
            specs[0] = pl.BlockSpec(memory_space=pltpu.SMEM)
        single = not isinstance(out_shapes, tuple)
        return pl.pallas_call(
            kernel,
            out_shape=out_shapes,
            in_specs=specs,
            out_specs=whole() if single else tuple(whole() for _ in out_shapes),
            compiler_params=pltpu.CompilerParams(vmem_limit_bytes=vmem * MIB),
            cost_estimate=pl.CostEstimate(flops=flops, bytes_accessed=nbytes, transcendentals=0),
        )(*args)

    return call


def modulation(noise_levels, offset, mod_table, step_sizes):
    total = noise_levels.shape[0]
    frame_ids = jnp.arange(total, dtype=jnp.int32)
    slots = (frame_ids + offset[0]) % total
    slot_hits = slots[:, None] == frame_ids[None, :]
    level_ids = jnp.sum(jnp.where(slot_hits, noise_levels[None, :], 0), axis=1)
    count = mod_table.shape[0]
    one_hot = (level_ids[:, None] == jnp.arange(count, dtype=jnp.int32)[None, :]).astype(jnp.float32)
    mods = jnp.dot(one_hot, mod_table.reshape(count, -1), precision=lax.Precision.HIGHEST)
    steps = jnp.sum(one_hot * step_sizes[None, :], axis=1)
    return mods.reshape(total, 3, -1), steps


def body(
    latents,
    fresh_noise,
    noise_levels,
    offset,
    block_ids,
    mod_table,
    step_sizes,
    w_query,
    w_key,
    w_value,
    w_out,
):
    frames, tokens, width = latents.shape
    times = lax.axis_size("tm")
    share = tokens // times
    total = frames * times
    inner = HEADS * HEAD_DIM
    sds = jax.ShapeDtypeStruct
    bf16 = jnp.bfloat16
    half = tokens // 2

    outgoing = latents.reshape(frames, times, share, width).transpose(1, 0, 2, 3)
    outgoing = outgoing.reshape(times, frames * share, width)
    column = lax.all_to_all(outgoing, "tm", 0, 0)

    mods, steps = modulation(noise_levels, offset, mod_table, step_sizes)
    first_frame = lax.axis_index("tm") * frames
    my_mods = lax.dynamic_slice_in_dim(mods, first_frame, frames)
    my_steps = lax.dynamic_slice_in_dim(steps, first_frame, frames)

    units = kernel_call(
        home_kernel,
        sds((2 * FULL, 5 * tokens + half, HEAD_DIM), bf16),
        2 * frames * tokens * width * 3 * inner,
        10 * MIB,
    )(latents, my_mods, w_query, w_key, w_value)
    units = lax.all_to_all(units, "tok", 0, 0)

    row = jnp.arange(total * share, dtype=jnp.int32)
    row_frame, row_token = row // share, row % share
    row_block = jnp.repeat(block_ids, share)
    allowed = (
        (row_token[:, None] == row_token[None, :])
        & (row_block[None, :] <= row_block[:, None])
        & (row_frame[:, None] != row_frame[None, :])
    )
    bias = jnp.where(allowed, 0.0, MASKED).astype(jnp.float32)
    row_scale = jnp.repeat(mods[:, 1], share, axis=0)
    row_shift = jnp.repeat(mods[:, 0], share, axis=0)

    back = kernel_call(
        temporal_kernel,
        sds((total * share, inner + HEAD_DIM), bf16),
        2 * total * share * width * 3 * inner,
        10 * MIB,
    )(column.reshape(total * share, width), row_scale, row_shift, bias, w_query, w_key, w_value)
    back = lax.all_to_all(back.reshape(times, frames * share, inner + HEAD_DIM), "tm", 0, 0)

    near = kernel_call(
        spatial_kernel,
        sds((2 * FULL, tokens + half + STAT_ROWS, HEAD_DIM), bf16),
        3 * 2 * 1024 * 1024 * HEAD_DIM,
        3 * MIB,
    )(units)
    near = lax.all_to_all(near, "tok", 0, 0)

    velocity, following, first = kernel_call(
        merge_kernel,
        (
            sds((frames, tokens, width), bf16),
            sds((frames, tokens, width), bf16),
            sds((tokens, width), bf16),
        ),
        2 * frames * tokens * width * inner,
        7 * MIB,
        smem_first=True,
    )(
        my_steps,
        latents,
        my_mods[:, 2],
        near,
        back.reshape(times * frames * share, inner + HEAD_DIM),
        w_out,
    )
    received = lax.ppermute(first, "tm", [(i, i - 1) for i in range(1, times)])
    is_last = lax.axis_index("tm") == times - 1
    incoming = jnp.where(is_last, fresh_noise, received)
    return velocity, lax.dynamic_update_slice(following, incoming[None], (frames - 1, 0, 0))


def solution(mesh):
    in_specs = (P("tm", "tok", None), P("tok", None), P(), P(), P(), P(), P(), P(), P(), P(), P())
    out_specs = (P("tm", "tok", None), P("tm", "tok", None))
    return jax.shard_map(body, mesh=mesh, in_specs=in_specs, out_specs=out_specs, check_vma=False)
```

```python
import math

import jax
import jax.numpy as jnp
from jax import lax
from jax.experimental import pallas as pl
from jax.experimental.pallas import tpu as pltpu
from jax.sharding import PartitionSpec as P

HEAD_DIM = 128
HEADS = 6
SPAN = 3
RANKS = 4
BASE2 = HEAD_DIM ** (-0.5) * math.log2(math.e)
MASKED = -1e30
FLOOR = -1e29
MIB = 1 << 20
STAT_ROWS = 16
LONG = 60_000_000_000
BF16 = jnp.bfloat16
F32 = jnp.float32


def normalise(x, scale1, shift):
    values = x.astype(F32)
    center = jnp.mean(values, axis=-1, keepdims=True)
    values = values - center
    spread = jnp.mean(values * values, axis=-1, keepdims=True)
    return (values * lax.rsqrt(spread + 1e-06) * scale1 + shift).astype(BF16)


def matmul(a, b):
    return jnp.dot(a, b, preferred_element_type=F32)


def attend(q, k, v, bias=None):
    scores = lax.dot_general(q, k, (((1,), (1,)), ((), ())), preferred_element_type=F32)
    if bias is not None:
        scores = scores + bias
    top = jnp.max(scores, axis=-1, keepdims=True)
    if bias is not None:
        top = jnp.maximum(top, FLOOR)
    weights = jnp.exp2((scores - top) * BASE2)
    total = jnp.sum(weights, axis=-1, keepdims=True)
    mixed = matmul(weights.astype(BF16), v)
    if bias is None:
        return mixed / total, top * BASE2 + jnp.log2(total)
    some = total > 0.0
    safe = jnp.where(some, total, 1.0)
    return mixed / safe, jnp.where(some, top * BASE2 + jnp.log2(safe), MASKED)


def split3(x):
    one = x.astype(BF16).astype(F32)
    rest = x - one
    two = rest.astype(BF16).astype(F32)
    return one, two, rest - two


def swap_halves(even, odd):
    low = lax.broadcasted_iota(jnp.int32, even.shape, 1) < 4
    return jnp.where(low, even, pltpu.roll(odd, 4, 1)), jnp.where(low, pltpu.roll(even, 4, 1), odd)


def shuffle_kernel(x_hbm, out_hbm, x_ref, mixed_ref, in_sems, out_sems):
    _, tokens, width = x_ref.shape
    chunks = in_sems.shape[0]
    rows = tokens // chunks
    pairs = rows // 8
    ins, outs = [], []
    for c in range(chunks):
        r = pl.ds(c * rows, rows)
        ins.append(pltpu.make_async_copy(x_hbm.at[:, r], x_ref.at[:, r], in_sems.at[c]))
        ins[c].start()
    for c in range(chunks):
        ins[c].wait()
        first, second = [
            x_ref[f, c * rows : (c + 1) * rows].astype(F32).reshape(pairs, 8, width) for f in range(2)
        ]
        even, odd = swap_halves(first, second)
        mixed_ref[c * pairs : (c + 1) * pairs, 0] = even.astype(BF16)
        mixed_ref[c * pairs : (c + 1) * pairs, 1] = odd.astype(BF16)
        r = pl.ds(c * pairs, pairs)
        outs.append(pltpu.make_async_copy(mixed_ref.at[r], out_hbm.at[r], out_sems.at[c]))
        outs[c].start()
    for c in range(chunks):
        outs[c].wait()


def home_kernel(
    noise_ref,
    offset_ref,
    step_ref,
    blocks_ref,
    place_ref,
    x_ref,
    table_hbm,
    wq_hbm,
    wk_hbm,
    wv_hbm,
    size_ref,
    own_hbm,
    shift_hbm,
    scale_hbm,
    bias_hbm,
    *refs,
):
    kv_outs, q_outs = refs[:RANKS], refs[RANKS : 2 * RANKS]
    table_ref, q_ref, k_ref, v_ref, wq_ref, wk_ref, wv_ref, *refs = refs[2 * RANKS :]
    own_ref, shift_ref, scale_ref, bias_ref, sems, out_sems = refs
    loads = [
        pltpu.make_async_copy(src, dst, sems.at[n])
        for n, (src, dst) in enumerate(
            (
                (table_hbm, table_ref),
                (wq_hbm, wq_ref),
                (wk_hbm, wk_ref),
                (wv_hbm, wv_ref),
            )
        )
    ]
    for load in loads:
        load.start()
    frames, tokens, _ = x_ref.shape
    total = noise_ref.shape[0]
    share = bias_ref.shape[0] // total
    place, rank = place_ref[0], place_ref[1]

    wide = (8, total * share)
    lane = lax.broadcasted_iota(jnp.int32, wide, 1)
    block = jnp.zeros(wide, F32)
    for f in range(total):
        block = jnp.where(lane // share == f, blocks_ref[f].astype(F32), block)
    block = jnp.broadcast_to(block[0:1], bias_ref.shape)
    down = lax.broadcasted_iota(jnp.int32, bias_ref.shape, 0)
    along = lax.broadcasted_iota(jnp.int32, bias_ref.shape, 1)
    allowed = (down % share == along % share) & (down != along) & (block <= jnp.transpose(block))
    bias_ref[...] = jnp.where(allowed, 0.0, MASKED)
    stores = [
        pltpu.make_async_copy(src, dst, out_sems.at[n])
        for n, (src, dst) in enumerate(
            (
                (bias_ref, bias_hbm),
                (own_ref, own_hbm),
                (shift_ref, shift_hbm),
                (scale_ref, scale_hbm),
            )
        )
    ]
    stores[0].start()

    def level_of(frame):
        return noise_ref[lax.rem(frame + offset_ref[0], total)]

    loads[0].wait()
    for n in range(frames + 1):
        level = level_of(jnp.minimum(place * frames + n, total - 1))
        size_ref[n] = step_ref[level]
        own_ref[n : n + 1, :] = table_ref[0, pl.ds(level, 1), :]
        own_ref[n + 3 : n + 4, :] = table_ref[1, pl.ds(level, 1), :] + 1.0
        own_ref[n + 6 : n + 7, :] = table_ref[2, pl.ds(level, 1), :]
    stores[1].start()
    rows = []
    for f in range(frames):
        rows.append(normalise(x_ref[f], own_ref[f + 3 : f + 4, :], own_ref[f : f + 1, :]))
    normed = jnp.concatenate(rows, axis=0)
    for n, (ref, w) in enumerate(((q_ref, wq_ref), (k_ref, wk_ref), (v_ref, wv_ref))):
        loads[1 + n].wait()
        ref[...] = matmul(normed, w[...]).astype(BF16)
    for d in range(RANKS):
        other = rank ^ d
        r = pl.ds(pl.multiple_of((other // 2) * tokens, tokens), tokens)
        for u in range(SPAN):
            c = pl.ds(pl.multiple_of((other % 2) * SPAN * HEAD_DIM + u * HEAD_DIM, HEAD_DIM), HEAD_DIM)
            kv_outs[d][u * tokens : (u + 1) * tokens] = k_ref[r, c]
            kv_outs[d][(SPAN + u) * tokens : (SPAN + u + 1) * tokens] = v_ref[r, c]
            q_outs[d][u * tokens : (u + 1) * tokens] = q_ref[r, c]
    for f in range(total):
        level = level_of(f)
        shift_ref[f // frames, f % frames : f % frames + 1, :] = table_ref[0, pl.ds(level, 1), :]
        scale_ref[f // frames, f % frames : f % frames + 1, :] = table_ref[1, pl.ds(level, 1), :] + 1.0
    stores[2].start()
    stores[3].start()
    for store in stores:
        store.wait()


def spatial_kernel(*refs):
    kvs, qs, outs = refs[: 2 * RANKS], refs[2 * RANKS : 3 * RANKS], refs[3 * RANKS :]
    tokens = HEAD_DIM
    lane = lax.broadcasted_iota(jnp.int32, (tokens, HEAD_DIM), 1)
    stats = [jnp.zeros((tokens, HEAD_DIM), F32)] * RANKS
    for u in range(SPAN):
        r = slice(u * tokens, (u + 1) * tokens)
        keys = jnp.concatenate([ref[u * tokens : (u + 1) * tokens] for ref in kvs], axis=0)
        vals = jnp.concatenate([ref[(SPAN + u) * tokens : (SPAN + u + 1) * tokens] for ref in kvs], axis=0)
        for s in range(0, RANKS, 2):
            q = jnp.concatenate([qs[s][r], qs[s + 1][r]], axis=0)
            mixed, logs = attend(q, keys, vals)
            mixed = mixed.astype(BF16)
            for d in range(2):
                half = slice(d * tokens, (d + 1) * tokens)
                outs[s + d][r] = mixed[half]
                for n, piece in enumerate(split3(logs[half])):
                    stats[s + d] = jnp.where(lane == SPAN * u + n, piece, stats[s + d])
    for d in range(RANKS):
        turned = jnp.transpose(stats[d])[0:STAT_ROWS]
        outs[d][SPAN * tokens : SPAN * tokens + STAT_ROWS] = turned.astype(BF16)


def temporal_kernel(x_ref, *refs):
    sources, out_hbm, held, (out_ref, load_sems, sems) = refs[:6], refs[6], refs[7:13], refs[13:]
    loads = []
    for n, (src, dst) in enumerate(zip(sources, held)):
        loads.append(pltpu.make_async_copy(src, dst, load_sems.at[n]))
        loads[n].start()
    scale_ref, shift_ref, wq_ref, wk_ref, wv_ref, bias_ref = held
    groups, rows, width = x_ref.shape
    low = lax.broadcasted_iota(jnp.int32, (groups, rows, width), 1) < rows // 2

    def spread(ref):
        first = jnp.broadcast_to(ref[:, 0:1, :], low.shape)
        return jnp.where(low, first, jnp.broadcast_to(ref[:, 1:2, :], low.shape))

    loads[0].wait()
    loads[1].wait()
    normed = normalise(x_ref[...].astype(F32), spread(scale_ref), spread(shift_ref))
    normed = normed.reshape(groups * rows, width)
    projected = []
    for n, w in enumerate((wq_ref, wk_ref, wv_ref)):
        loads[2 + n].wait()
        projected.append(matmul(normed, w[...]).astype(BF16))
    q, k, v = projected
    loads[5].wait()
    bias = bias_ref[...]
    lane = lax.broadcasted_iota(jnp.int32, (groups * rows, HEAD_DIM), 1)
    stats = jnp.zeros((groups * rows, HEAD_DIM), F32)
    copies = []

    def send(n):
        c = pl.ds(n * HEAD_DIM, HEAD_DIM)
        copies.append(pltpu.make_async_copy(out_ref.at[:, c], out_hbm.at[:, c], sems.at[n]))
        copies[-1].start()

    for h in range(HEADS):
        own = slice(h * HEAD_DIM, (h + 1) * HEAD_DIM)
        mixed, logs = attend(q[:, own], k[:, own], v[:, own], bias)
        out_ref[:, own] = mixed.astype(BF16)
        send(h)
        for n, piece in enumerate(split3(logs)):
            stats = jnp.where(lane == 8 * n + h, piece, stats)
    out_ref[:, HEADS * HEAD_DIM :] = stats.astype(BF16)
    send(HEADS)
    for copy in copies:
        copy.wait()


def merged(f, rank, near_refs, time_ref, space_ref, out_ref):
    for d, ref in enumerate(near_refs):
        space_ref[rank ^ d] = ref[...]
    tokens = out_ref.shape[0]
    width = time_ref.shape[1]
    turned = time_ref[...].astype(F32).reshape(tokens // 8, 2, 8, width)
    far_rows = swap_halves(turned[:, 0], turned[:, 1])[f].reshape(tokens, width)
    stats = far_rows[:, HEADS * HEAD_DIM :]
    time_log = stats[:, 0:8] + stats[:, 8:16] + stats[:, 16:24]
    log_rows = []
    for h in range(HEADS):
        st = space_ref[2 * f + h // SPAN, SPAN * tokens : SPAN * tokens + STAT_ROWS].astype(F32)
        b = SPAN * (h % SPAN)
        log_rows.append(st[b : b + 1] + st[b + 1 : b + 2] + st[b + 2 : b + 3])
    log_rows.append(jnp.zeros((8 - HEADS, HEAD_DIM), F32))
    space_log = jnp.transpose(jnp.concatenate(log_rows, axis=0))
    of_space = 1.0 / (1.0 + jnp.exp2(time_log - space_log))
    of_time = 1.0 / (1.0 + jnp.exp2(space_log - time_log))
    for h in range(HEADS):
        own = slice(h * HEAD_DIM, (h + 1) * HEAD_DIM)
        u = h % SPAN
        near = space_ref[2 * f + h // SPAN, u * tokens : (u + 1) * tokens].astype(F32)
        mixed = of_space[:, h : h + 1] * near + of_time[:, h : h + 1] * far_rows[:, own]
        out_ref[:, own] = mixed.astype(BF16)


def first_kernel(place_ref, *refs):
    near_refs, (time_ref, sent_ref, first_ref, space_ref) = refs[:RANKS], refs[RANKS:]
    merged(0, place_ref[1], near_refs, time_ref, space_ref, first_ref)
    sent_ref[...] = first_ref[...]


def project_kernel(place_ref, size_ref, *refs):
    near_refs = refs[:RANKS]
    time_ref, first_ref, own_hbm, x_hbm, wo_hbm, vel_ref, next_ref, wo_ref = refs[RANKS : RANKS + 8]
    space_ref, second_ref, own_ref, x_ref, sems = refs[RANKS + 8 :]
    frames, tokens, _ = x_ref.shape
    loads = []
    for n, (src, dst) in enumerate(((wo_hbm, wo_ref), (x_hbm, x_ref), (own_hbm, own_ref))):
        loads.append(pltpu.make_async_copy(src, dst, sems.at[n]))
        loads[n].start()

    merged(1, place_ref[1], near_refs, time_ref, space_ref, second_ref)
    attended = jnp.concatenate([first_ref[...], second_ref[...]], axis=0)
    for load in loads:
        load.wait()
    projected = matmul(attended, wo_ref[...])
    for f in range(frames):
        moving = projected[f * tokens : (f + 1) * tokens] * own_ref[6 + f : 7 + f, :]
        vel_ref[f] = moving.astype(BF16)
        if f > 0:
            next_ref[f - 1] = (x_ref[f].astype(F32) + size_ref[f] * moving).astype(BF16)


def last_kernel(
    place_ref,
    size_ref,
    x_ref,
    att_ref,
    wo_ref,
    own_hbm,
    fresh_hbm,
    kept_ref,
    next_ref,
    out_ref,
    own_ref,
    sems,
):
    del kept_ref
    slot = next_ref.shape[0] - 1
    chunks = sems.shape[0]
    width = out_ref.shape[1] // chunks
    at_end = place_ref[0] == place_ref[2]

    @pl.when(at_end)
    def _():
        copy = pltpu.make_async_copy(fresh_hbm, next_ref.at[slot], sems.at[0])
        copy.start()
        copy.wait()

    @pl.when(jnp.logical_not(at_end))
    def _():
        load = pltpu.make_async_copy(own_hbm, own_ref, sems.at[0])
        load.start()
        load.wait()
        copies = []
        for n in range(chunks):
            c = slice(n * width, (n + 1) * width)
            moving = matmul(att_ref[...], wo_ref[:, c]) * own_ref[8:9, c]
            out_ref[:, c] = (x_ref[:, c].astype(F32) + size_ref[2] * moving).astype(BF16)
            d = pl.ds(n * width, width)
            copies.append(pltpu.make_async_copy(out_ref.at[:, d], next_ref.at[slot, :, d], sems.at[n]))
            copies[n].start()
        for copy in copies:
            copy.wait()


def whole():
    return pl.BlockSpec(memory_space=pltpu.VMEM)


def scalar():
    return pl.BlockSpec(memory_space=pltpu.SMEM)


def anywhere():
    return pl.BlockSpec(memory_space=pl.ANY)


def pinned(x):
    return pltpu.with_memory_space_constraint(x, pltpu.VMEM)


def in_hbm(x):
    return pltpu.with_memory_space_constraint(x, pltpu.HBM)


def call(kernel, args, in_specs, outs, out_specs, flops=0, nbytes=0, vmem=20, **more):
    return pl.pallas_call(
        kernel,
        out_shape=outs,
        in_specs=in_specs,
        out_specs=out_specs,
        compiler_params=pltpu.CompilerParams(vmem_limit_bytes=vmem * MIB),
        cost_estimate=pl.CostEstimate(flops=flops, bytes_accessed=nbytes, transcendentals=0),
        **more,
    )(*args)


def body(
    latents,
    fresh_noise,
    noise_levels,
    offset,
    block_ids,
    mod_table,
    step_sizes,
    w_query,
    w_key,
    w_value,
    w_out,
):
    frames, tokens, width = latents.shape
    times = lax.axis_size("tm")
    ranks = lax.axis_size("tok")
    share = tokens // times
    total = frames * times
    inner = HEADS * HEAD_DIM
    sds = jax.ShapeDtypeStruct
    dma = pltpu.SemaphoreType.DMA
    back_perm = [(i, i - 1) for i in range(1, times)]
    project_flops = 2 * frames * tokens * width * inner

    def over_y(x, d):
        return lax.ppermute(x, "tok", [(j, j ^ d) for j in range(ranks)]) if d else x

    def over_x(x):
        return lax.ppermute(x, "tok", [(j, j ^ RANKS) for j in range(ranks)])

    outgoing, x = call(
        shuffle_kernel,
        (in_hbm(latents),),
        [anywhere()],
        (pltpu.HBM((tokens // 8, 2, 8, width), BF16), pltpu.VMEM((frames, tokens, width), BF16)),
        (anywhere(), whole()),
        nbytes=2 * MIB,
        scratch_shapes=[pltpu.VMEM((tokens // 8, 2, 8, width), BF16), dma((4,)), dma((4,))],
    )
    column = lax.all_to_all(outgoing.reshape(times, frames * share, width), "tm", 0, 0)

    small = (
        pltpu.VMEM((16, width), F32),
        pltpu.VMEM((times, frames, width), F32),
        pltpu.VMEM((times, frames, width), F32),
        pltpu.VMEM((total * share, total * share), F32),
    )
    place = lax.axis_index("tm").astype(jnp.int32)
    rank = lax.axis_index("tok").astype(jnp.int32) % RANKS
    place = jnp.stack([place, rank, jnp.int32(times - 1)])
    sizes, own, shifts, scales, bias, *parts = call(
        home_kernel,
        (
            noise_levels,
            offset,
            step_sizes,
            block_ids,
            place,
            pinned(x),
            in_hbm(mod_table.transpose(1, 0, 2)),
            in_hbm(w_query),
            in_hbm(w_key),
            in_hbm(w_value),
        ),
        [scalar()] * 5 + [whole()] + [anywhere()] * 4,
        (
            sds((frames + 1,), F32),
            pltpu.HBM((16, width), F32),
            pltpu.HBM((times, frames, width), F32),
            pltpu.HBM((times, frames, width), F32),
            pltpu.HBM((total * share, total * share), F32),
            *[sds((2 * SPAN * tokens, HEAD_DIM), BF16)] * RANKS,
            *[sds((SPAN * tokens, HEAD_DIM), BF16)] * RANKS,
        ),
        (scalar(), *[anywhere()] * 4, *[whole()] * (2 * RANKS)),
        flops=LONG,
        nbytes=10 * MIB,
        scratch_shapes=[
            pltpu.VMEM((3, mod_table.shape[0], width), F32),
            *[pltpu.VMEM((frames * tokens, inner), BF16)] * 3,
            *[pltpu.VMEM((width, inner), BF16)] * 3,
            *small,
            dma((4,)),
            dma((4,)),
        ],
    )
    kvs, qs = parts[:RANKS], parts[RANKS:]
    near_kvs = [over_y(kv, d) for d, kv in enumerate(kvs)]
    far_kvs = [over_x(kv) for kv in near_kvs]
    qs = [over_y(q, d) for d, q in enumerate(qs)]
    next_latents = lax.ppermute(latents[0], "tm", back_perm)

    back = call(
        temporal_kernel,
        (column, *[in_hbm(a) for a in (scales, shifts, w_query, w_key, w_value, bias)]),
        [whole()] + [anywhere()] * 6,
        pltpu.HBM((total * share, inner + HEAD_DIM), BF16),
        anywhere(),
        flops=LONG,
        nbytes=10 * MIB,
        scratch_shapes=[
            *small[1:3],
            *[pltpu.VMEM((width, inner), BF16)] * 3,
            small[3],
            pltpu.VMEM((total * share, inner + HEAD_DIM), BF16),
            dma((6,)),
            dma((HEADS + 1,)),
        ],
    )
    back = lax.all_to_all(back.reshape(times, frames * share, inner + HEAD_DIM), "tm", 0, 0)
    back = back.reshape(times * frames * share, inner + HEAD_DIM)

    near = call(
        spatial_kernel,
        (*near_kvs, *far_kvs, *qs),
        [whole()] * (3 * RANKS),
        [sds((SPAN * tokens + STAT_ROWS, HEAD_DIM), BF16)] * RANKS,
        [whole()] * RANKS,
        flops=2 * LONG,
        nbytes=3 * MIB,
    )
    near = [over_y(part, d) for d, part in enumerate(near)]

    space = pltpu.VMEM((RANKS, SPAN * tokens + STAT_ROWS, HEAD_DIM), BF16)
    sent, first = call(
        first_kernel,
        (place, *near, back),
        [scalar()] + [whole()] * (RANKS + 1),
        (sds((tokens, inner), BF16), pltpu.VMEM((tokens, inner), BF16)),
        (whole(), whole()),
        nbytes=2 * MIB,
        scratch_shapes=[space],
    )
    next_first = lax.ppermute(sent, "tm", back_perm)
    velocity, following, wo = call(
        project_kernel,
        (place, sizes, *near, back, pinned(first), in_hbm(own), in_hbm(latents), in_hbm(w_out)),
        [scalar()] * 2 + [whole()] * (RANKS + 2) + [anywhere()] * 3,
        (
            sds((frames, tokens, width), BF16),
            sds((frames, tokens, width), BF16),
            pltpu.VMEM((inner, width), BF16),
        ),
        (whole(), whole(), whole()),
        flops=project_flops,
        nbytes=6 * MIB,
        scratch_shapes=[
            space,
            pltpu.VMEM((tokens, inner), BF16),
            small[0],
            pltpu.VMEM((frames, tokens, width), BF16),
            dma((3,)),
        ],
    )
    following = call(
        last_kernel,
        (place, sizes, next_latents, next_first, pinned(wo), in_hbm(own), in_hbm(fresh_noise), following),
        [scalar()] * 2 + [whole()] * 3 + [anywhere()] * 3,
        sds((frames, tokens, width), BF16),
        anywhere(),
        flops=project_flops // 2,
        nbytes=4 * MIB,
        scratch_shapes=[pltpu.VMEM((tokens, width), BF16), small[0], dma((3,))],
        input_output_aliases={7: 0},
    )
    return velocity, following


def solution(mesh):
    in_specs = (P("tm", "tok", None), P("tok", None), P(), P(), P(), P(), P(), P(), P(), P(), P())
    out_specs = (P("tm", "tok", None), P("tm", "tok", None))
    return jax.shard_map(body, mesh=mesh, in_specs=in_specs, out_specs=out_specs, check_vma=False)
```

```python
import math

import jax
import jax.numpy as jnp
from jax import lax
from jax.experimental import pallas as pl
from jax.experimental.pallas import tpu as pltpu
from jax.sharding import PartitionSpec as P

HEAD_DIM = 128
HEADS = 6
SPAN = 3
RANKS = 4
BASE2 = HEAD_DIM ** (-0.5) * math.log2(math.e)
MASKED = -1e30
FLOOR = -1e29
MIB = 1 << 20
STAT_ROWS = 16
LONG = 60_000_000_000
BF16 = jnp.bfloat16
F32 = jnp.float32


def normalise(x, scale1, shift):
    values = x.astype(F32)
    center = jnp.mean(values, axis=-1, keepdims=True)
    values = values - center
    spread = jnp.mean(values * values, axis=-1, keepdims=True)
    return (values * lax.rsqrt(spread + 1e-06) * scale1 + shift).astype(BF16)


def matmul(a, b):
    return jnp.dot(a, b, preferred_element_type=F32)


def softmax_parts(q, k, bias=None):
    scores = lax.dot_general(q, k, (((1,), (1,)), ((), ())), preferred_element_type=F32)
    if bias is not None:
        scores = scores + bias
    top = jnp.max(scores, axis=-1, keepdims=True)
    if bias is not None:
        top = jnp.maximum(top, FLOOR)
    weights = jnp.exp2((scores - top) * BASE2)
    return weights.astype(BF16), jnp.sum(weights, axis=-1, keepdims=True), top


def finish(weights, total, top, v, may_be_empty):
    mixed = matmul(weights, v)
    if not may_be_empty:
        return mixed / total, top * BASE2 + jnp.log2(total)
    some = total > 0.0
    safe = jnp.where(some, total, 1.0)
    return mixed / safe, jnp.where(some, top * BASE2 + jnp.log2(safe), MASKED)


def attend(q, k, v):
    return finish(*softmax_parts(q, k), v, False)


def split3(x):
    one = x.astype(BF16).astype(F32)
    rest = x - one
    two = rest.astype(BF16).astype(F32)
    return one, two, rest - two


def swap_halves(even, odd):
    low = lax.broadcasted_iota(jnp.int32, even.shape, 1) < 4
    return jnp.where(low, even, pltpu.roll(odd, 4, 1)), jnp.where(low, pltpu.roll(even, 4, 1), odd)


def shuffle_kernel(x_hbm, out_hbm, x_ref, mixed_ref, in_sems, out_sems):
    _, tokens, width = x_ref.shape
    chunks = in_sems.shape[0]
    rows = tokens // chunks
    pairs = rows // 8
    ins, outs = [], []
    for c in range(chunks):
        r = pl.ds(c * rows, rows)
        ins.append(pltpu.make_async_copy(x_hbm.at[:, r], x_ref.at[:, r], in_sems.at[c]))
        ins[c].start()
    for c in range(chunks):
        ins[c].wait()
        first, second = [
            x_ref[f, c * rows : (c + 1) * rows].astype(F32).reshape(pairs, 8, width) for f in range(2)
        ]
        even, odd = swap_halves(first, second)
        mixed_ref[c * pairs : (c + 1) * pairs, 0] = even.astype(BF16)
        mixed_ref[c * pairs : (c + 1) * pairs, 1] = odd.astype(BF16)
        r = pl.ds(c * pairs, pairs)
        outs.append(pltpu.make_async_copy(mixed_ref.at[r], out_hbm.at[r], out_sems.at[c]))
        outs[c].start()
    for c in range(chunks):
        outs[c].wait()


def home_kernel(
    noise_ref, offset_ref, step_ref, place_ref, x_ref, table_hbm, wq_hbm, wk_hbm, wv_hbm, size_ref, own_hbm, *refs
):
    outs = refs[:RANKS]
    table_ref, q_ref, k_ref, v_ref, wq_ref, wk_ref, wv_ref, own_ref, sems, own_sem = refs[RANKS:]
    loads = []
    for n, (src, dst) in enumerate(
        ((table_hbm, table_ref), (wq_hbm, wq_ref), (wk_hbm, wk_ref), (wv_hbm, wv_ref))
    ):
        loads.append(pltpu.make_async_copy(src, dst, sems.at[n]))
        loads[n].start()
    frames, tokens, _ = x_ref.shape
    total = noise_ref.shape[0]
    loads[0].wait()
    for n in range(frames + 1):
        frame = jnp.minimum(place_ref[0] * frames + n, total - 1)
        level = noise_ref[lax.rem(frame + offset_ref[0], total)]
        size_ref[n] = step_ref[level]
        own_ref[n : n + 1, :] = table_ref[0, pl.ds(level, 1), :]
        own_ref[n + 3 : n + 4, :] = table_ref[1, pl.ds(level, 1), :] + 1.0
        own_ref[n + 6 : n + 7, :] = table_ref[2, pl.ds(level, 1), :]
    own_store = pltpu.make_async_copy(own_ref, own_hbm, own_sem)
    own_store.start()
    normed = []
    for f in range(frames):
        normed.append(normalise(x_ref[f], own_ref[f + 3 : f + 4, :], own_ref[f : f + 1, :]))
    normed = jnp.concatenate(normed, axis=0)
    for n, (ref, w) in enumerate(((q_ref, wq_ref), (k_ref, wk_ref), (v_ref, wv_ref))):
        loads[1 + n].wait()
        ref[...] = matmul(normed, w[...]).astype(BF16)
    for d in range(RANKS):
        other = place_ref[1] ^ d
        r = pl.ds(pl.multiple_of((other // 2) * tokens, tokens), tokens)
        for u in range(SPAN):
            c = pl.ds(pl.multiple_of((other % 2) * SPAN * HEAD_DIM + u * HEAD_DIM, HEAD_DIM), HEAD_DIM)
            for n, ref in enumerate((k_ref, v_ref, q_ref)):
                block = slice((n * SPAN + u) * tokens, (n * SPAN + u + 1) * tokens)
                outs[d][block] = ref[r, c]
    own_store.wait()


def column_kernel(noise_ref, offset_ref, blocks_ref, table_ref, shift_hbm, scale_hbm, bias_hbm, *refs):
    shift_ref, scale_ref, bias_ref, sems = refs
    total = noise_ref.shape[0]
    frames = shift_ref.shape[1]
    share = bias_ref.shape[0] // total
    stores = [
        pltpu.make_async_copy(src, dst, sems.at[n])
        for n, (src, dst) in enumerate(
            ((shift_ref, shift_hbm), (scale_ref, scale_hbm), (bias_ref, bias_hbm))
        )
    ]
    for f in range(total):
        level = noise_ref[lax.rem(f + offset_ref[0], total)]
        shift_ref[f // frames, f % frames : f % frames + 1, :] = table_ref[0, pl.ds(level, 1), :]
        scale_ref[f // frames, f % frames : f % frames + 1, :] = table_ref[1, pl.ds(level, 1), :] + 1.0
    stores[0].start()
    stores[1].start()
    wide = (8, total * share)
    lane = lax.broadcasted_iota(jnp.int32, wide, 1) // share
    block = jnp.zeros(wide, F32)
    for f in range(total):
        block = jnp.where(lane == f, blocks_ref[f].astype(F32), block)
    block = jnp.broadcast_to(block[0:1], bias_ref.shape)
    down = lax.broadcasted_iota(jnp.int32, bias_ref.shape, 0)
    along = lax.broadcasted_iota(jnp.int32, bias_ref.shape, 1)
    allowed = (down % share == along % share) & (down != along) & (block <= jnp.transpose(block))
    bias_ref[...] = jnp.where(allowed, 0.0, MASKED)
    stores[2].start()
    for store in stores:
        store.wait()


def spatial_kernel(*refs):
    kvs, qs, outs = refs[: 2 * RANKS], refs[:RANKS], refs[2 * RANKS :]
    tokens = HEAD_DIM
    lane = lax.broadcasted_iota(jnp.int32, (tokens, HEAD_DIM), 1)
    stats = [jnp.zeros((tokens, HEAD_DIM), F32)] * RANKS
    for u in range(SPAN):
        r = slice(u * tokens, (u + 1) * tokens)
        block = slice((2 * SPAN + u) * tokens, (2 * SPAN + u + 1) * tokens)
        keys = jnp.concatenate([ref[u * tokens : (u + 1) * tokens] for ref in kvs], axis=0)
        vals = jnp.concatenate([ref[(SPAN + u) * tokens : (SPAN + u + 1) * tokens] for ref in kvs], axis=0)
        for s in range(0, RANKS, 2):
            q = jnp.concatenate([qs[s][block], qs[s + 1][block]], axis=0)
            mixed, logs = attend(q, keys, vals)
            mixed = mixed.astype(BF16)
            for d in range(2):
                half = slice(d * tokens, (d + 1) * tokens)
                outs[s + d][r] = mixed[half]
                for n, piece in enumerate(split3(logs[half])):
                    stats[s + d] = jnp.where(lane == SPAN * u + n, piece, stats[s + d])
    for d in range(RANKS):
        turned = jnp.transpose(stats[d])[0:STAT_ROWS]
        outs[d][SPAN * tokens : SPAN * tokens + STAT_ROWS] = turned.astype(BF16)


def temporal_kernel(x_ref, *refs):
    scale_hbm, shift_hbm, wq_hbm, wk_hbm, bias_hbm, wv_hbm, out_hbm = refs[:7]
    scale_ref, shift_ref, wq_ref, wk_ref, bias_ref, wv_ref, out_ref, sems, out_sems = refs[7:]
    held = (scale_ref, shift_ref, wq_ref, wk_ref, bias_ref, wv_ref)
    loads = []
    for n, (src, dst) in enumerate(zip(refs[:6], held)):
        loads.append(pltpu.make_async_copy(src, dst, sems.at[n]))
        loads[n].start()
    groups, rows, width = x_ref.shape
    low = lax.broadcasted_iota(jnp.int32, (groups, rows, width), 1) < rows // 2

    def spread(ref):
        first = jnp.broadcast_to(ref[:, 0:1, :], low.shape)
        return jnp.where(low, first, jnp.broadcast_to(ref[:, 1:2, :], low.shape))

    loads[0].wait()
    loads[1].wait()
    normed = normalise(x_ref[...].astype(F32), spread(scale_ref), spread(shift_ref))
    normed = normed.reshape(groups * rows, width)
    loads[2].wait()
    q = matmul(normed, wq_ref[...]).astype(BF16)
    loads[3].wait()
    k = matmul(normed, wk_ref[...]).astype(BF16)
    loads[4].wait()
    lane = lax.broadcasted_iota(jnp.int32, (groups * rows, HEAD_DIM), 1)
    stats = jnp.zeros((groups * rows, HEAD_DIM), F32)
    heads = [slice(h * HEAD_DIM, (h + 1) * HEAD_DIM) for h in range(HEADS)]
    parts = [softmax_parts(q[:, own], k[:, own], bias_ref[...]) for own in heads]
    loads[5].wait()
    v = matmul(normed, wv_ref[...]).astype(BF16)
    copies = []

    def send(n):
        c = pl.ds(n * HEAD_DIM, HEAD_DIM)
        copies.append(pltpu.make_async_copy(out_ref.at[:, c], out_hbm.at[:, c], out_sems.at[n]))
        copies[n].start()

    for h, (own, (weights, total, top)) in enumerate(zip(heads, parts)):
        mixed, logs = finish(weights, total, top, v[:, own], True)
        out_ref[:, own] = mixed.astype(BF16)
        send(h)
        for m, piece in enumerate(split3(logs)):
            stats = jnp.where(lane == 8 * m + h, piece, stats)
    out_ref[:, HEADS * HEAD_DIM :] = stats.astype(BF16)
    send(HEADS)
    for copy in copies:
        copy.wait()


def merged(f, rank, near_refs, time_ref, space_ref, out_ref):
    for d, ref in enumerate(near_refs):
        space_ref[rank ^ d] = ref[...]
    tokens = out_ref.shape[0]
    width = time_ref.shape[1]
    turned = time_ref[...].astype(F32).reshape(tokens // 8, 2, 8, width)
    far_rows = swap_halves(turned[:, 0], turned[:, 1])[f].reshape(tokens, width)
    stats = far_rows[:, HEADS * HEAD_DIM :]
    time_log = stats[:, 0:8] + stats[:, 8:16] + stats[:, 16:24]
    log_rows = []
    for h in range(HEADS):
        st = space_ref[2 * f + h // SPAN, SPAN * tokens : SPAN * tokens + STAT_ROWS].astype(F32)
        b = SPAN * (h % SPAN)
        log_rows.append(st[b : b + 1] + st[b + 1 : b + 2] + st[b + 2 : b + 3])
    log_rows.append(jnp.zeros((8 - HEADS, HEAD_DIM), F32))
    space_log = jnp.transpose(jnp.concatenate(log_rows, axis=0))
    of_space = 1.0 / (1.0 + jnp.exp2(time_log - space_log))
    of_time = 1.0 / (1.0 + jnp.exp2(space_log - time_log))
    for h in range(HEADS):
        own = slice(h * HEAD_DIM, (h + 1) * HEAD_DIM)
        u = h % SPAN
        near = space_ref[2 * f + h // SPAN, u * tokens : (u + 1) * tokens].astype(F32)
        mixed = of_space[:, h : h + 1] * near + of_time[:, h : h + 1] * far_rows[:, own]
        out_ref[:, own] = mixed.astype(BF16)


def first_kernel(place_ref, *refs):
    near_refs, (time_ref, sent_ref, first_ref, space_ref) = refs[:RANKS], refs[RANKS:]
    merged(0, place_ref[1], near_refs, time_ref, space_ref, first_ref)
    sent_ref[...] = first_ref[...]


def project_kernel(place_ref, size_ref, *refs):
    near_refs = refs[:RANKS]
    time_ref, first_ref, wo_hbm, own_hbm, x_hbm, fresh_hbm, in_hbm_ref = refs[RANKS : RANKS + 7]
    vel_hbm, next_hbm, wo_ref, own_ref, base_ref = refs[RANKS + 7 : RANKS + 12]
    space_ref, second_ref, x_ref, fresh_ref, vel_ref, next_ref, sems, vel_sems, next_sems = refs[RANKS + 12 :]
    frames, tokens, _ = x_ref.shape
    loads = []
    for n, (src, dst) in enumerate(
        (
            (wo_hbm, wo_ref),
            (own_hbm, own_ref),
            (x_hbm, x_ref),
            (in_hbm_ref, base_ref),
            (fresh_hbm, fresh_ref),
        )
    ):
        loads.append(pltpu.make_async_copy(src, dst, sems.at[n]))
        loads[n].start()

    merged(1, place_ref[1], near_refs, time_ref, space_ref, second_ref)
    attended = jnp.concatenate([first_ref[...], second_ref[...]], axis=0)
    for load in loads:
        load.wait()

    @pl.when(place_ref[0] == place_ref[2])
    def _():
        base_ref[...] = fresh_ref[...]

    chunks = vel_sems.shape[0]
    width = vel_ref.shape[2] // chunks
    copies = []
    for n in range(chunks):
        c, d = slice(n * width, (n + 1) * width), pl.ds(n * width, width)
        projected = matmul(attended, wo_ref[:, c])
        for f in range(frames):
            moving = projected[f * tokens : (f + 1) * tokens] * own_ref[6 + f : 7 + f, c]
            vel_ref[f, :, c] = moving.astype(BF16)
            if f > 0:
                advanced = x_ref[f, :, c].astype(F32) + size_ref[f] * moving
                next_ref[f - 1, :, c] = advanced.astype(BF16)
        copies.append(pltpu.make_async_copy(vel_ref.at[:, :, d], vel_hbm.at[:, :, d], vel_sems.at[n]))
        copies[-1].start()
        filled = next_hbm.at[pl.ds(0, frames - 1), :, d]
        copies.append(pltpu.make_async_copy(next_ref.at[:, :, d], filled, next_sems.at[n]))
        copies[-1].start()
    for copy in copies:
        copy.wait()


def last_kernel(size_ref, att_ref, wo_ref, own_ref, base_ref, kept_ref, next_ref, out_ref, sems):
    del kept_ref
    slot = next_ref.shape[0] - 1
    chunks = sems.shape[0]
    width = out_ref.shape[1] // chunks
    copies = []
    for n in range(chunks):
        c, d = slice(n * width, (n + 1) * width), pl.ds(n * width, width)
        moving = matmul(att_ref[...], wo_ref[:, c]) * own_ref[8:9, c]
        out_ref[:, c] = (base_ref[:, c].astype(F32) + size_ref[2] * moving).astype(BF16)
        copies.append(pltpu.make_async_copy(out_ref.at[:, d], next_ref.at[slot, :, d], sems.at[n]))
        copies[n].start()
    for copy in copies:
        copy.wait()


def whole():
    return pl.BlockSpec(memory_space=pltpu.VMEM)


def scalar():
    return pl.BlockSpec(memory_space=pltpu.SMEM)


def anywhere():
    return pl.BlockSpec(memory_space=pl.ANY)


def pinned(x):
    return pltpu.with_memory_space_constraint(x, pltpu.VMEM)


def in_hbm(x):
    return pltpu.with_memory_space_constraint(x, pltpu.HBM)


def call(kernel, args, in_specs, outs, out_specs, flops=0, nbytes=0, vmem=20, **more):
    return pl.pallas_call(
        kernel,
        out_shape=outs,
        in_specs=in_specs,
        out_specs=out_specs,
        compiler_params=pltpu.CompilerParams(vmem_limit_bytes=vmem * MIB),
        cost_estimate=pl.CostEstimate(flops=flops, bytes_accessed=nbytes, transcendentals=0),
        **more,
    )(*args)


def body(
    latents,
    fresh_noise,
    noise_levels,
    offset,
    block_ids,
    mod_table,
    step_sizes,
    w_query,
    w_key,
    w_value,
    w_out,
):
    frames, tokens, width = latents.shape
    times = lax.axis_size("tm")
    ranks = lax.axis_size("tok")
    share = tokens // times
    total = frames * times
    inner = HEADS * HEAD_DIM
    sds = jax.ShapeDtypeStruct
    dma = pltpu.SemaphoreType.DMA
    back_perm = [(i, i - 1) for i in range(1, times)]
    project_flops = 2 * frames * tokens * width * inner

    def exchange(x, d):
        pairs = []
        for tm in range(times):
            for tok in range(ranks):
                side, y, core = tok // RANKS, tok % RANKS, tm % 2
                pairs.append((tm * ranks + tok, (tm - core + side) * ranks + core * RANKS + (y ^ d)))
        return lax.ppermute(x, ("tm", "tok"), pairs)

    outgoing, x = call(
        shuffle_kernel,
        (in_hbm(latents),),
        [anywhere()],
        (pltpu.HBM((tokens // 8, 2, 8, width), BF16), pltpu.VMEM((frames, tokens, width), BF16)),
        (anywhere(), whole()),
        nbytes=2 * MIB,
        scratch_shapes=[pltpu.VMEM((tokens // 8, 2, 8, width), BF16), dma((4,)), dma((4,))],
    )
    column = lax.all_to_all(outgoing.reshape(times, frames * share, width), "tm", 0, 0)

    place = lax.axis_index("tm").astype(jnp.int32)
    rank = lax.axis_index("tok").astype(jnp.int32) % RANKS
    place = jnp.stack([place, rank, jnp.int32(times - 1)])
    table = mod_table.transpose(1, 0, 2)
    sizes, own, *parts = call(
        home_kernel,
        (
            noise_levels,
            offset,
            step_sizes,
            place,
            pinned(x),
            *[in_hbm(a) for a in (table, w_query, w_key, w_value)],
        ),
        [scalar()] * 4 + [whole()] + [anywhere()] * 4,
        (
            sds((frames + 1,), F32),
            pltpu.HBM((16, width), F32),
            *[sds((3 * SPAN * tokens, HEAD_DIM), BF16)] * RANKS,
        ),
        (scalar(), anywhere(), *[whole()] * RANKS),
        flops=LONG,
        nbytes=10 * MIB,
        scratch_shapes=[
            pltpu.VMEM(table.shape, F32),
            *[pltpu.VMEM((frames * tokens, inner), BF16)] * 3,
            *[pltpu.VMEM((width, inner), BF16)] * 3,
            pltpu.VMEM((16, width), F32),
            dma((4,)),
            dma,
        ],
    )
    units = [exchange(part, d) for d, part in enumerate(parts)]

    small = (
        pltpu.VMEM((16, width), F32),
        pltpu.VMEM((times, frames, width), F32),
        pltpu.VMEM((times, frames, width), F32),
        pltpu.VMEM((total * share, total * share), F32),
    )
    table, noise_levels, sizes = lax.optimization_barrier((table, noise_levels, sizes))
    shifts, scales, bias = call(
        column_kernel,
        (noise_levels, offset, block_ids, table),
        [scalar()] * 3 + [whole()],
        tuple(pltpu.HBM(a.inner_aval.shape, F32) for a in small[1:]),
        (anywhere(),) * 3,
        nbytes=MIB // 4,
        scratch_shapes=[*small[1:], dma((3,))],
    )
    incoming, sizes = lax.optimization_barrier((latents[0], sizes))
    next_latents = lax.ppermute(incoming, "tm", back_perm)

    back = call(
        temporal_kernel,
        (column, *[in_hbm(a) for a in (scales, shifts, w_query, w_key, bias, w_value)]),
        [whole()] + [anywhere()] * 6,
        pltpu.HBM((total * share, inner + HEAD_DIM), BF16),
        anywhere(),
        flops=LONG,
        nbytes=10 * MIB,
        scratch_shapes=[
            *small[1:3],
            *[pltpu.VMEM((width, inner), BF16)] * 2,
            small[3],
            pltpu.VMEM((width, inner), BF16),
            pltpu.VMEM((total * share, inner + HEAD_DIM), BF16),
            dma((6,)),
            dma((HEADS + 1,)),
        ],
    )
    back, next_latents, *units = lax.optimization_barrier((back, next_latents, *units))
    sibling = [lax.ppermute(part, "tm", [(i, i ^ 1) for i in range(times)]) for part in units]
    back = lax.all_to_all(back.reshape(times, frames * share, inner + HEAD_DIM), "tm", 0, 0)
    back = back.reshape(times * frames * share, inner + HEAD_DIM)

    near = call(
        spatial_kernel,
        (*units, *sibling),
        [whole()] * (2 * RANKS),
        [sds((SPAN * tokens + STAT_ROWS, HEAD_DIM), BF16)] * RANKS,
        [whole()] * RANKS,
        flops=2 * LONG,
        nbytes=3 * MIB,
    )
    near = [exchange(part, d) for d, part in enumerate(near)]

    space = pltpu.VMEM((RANKS, SPAN * tokens + STAT_ROWS, HEAD_DIM), BF16)
    sent, first = call(
        first_kernel,
        (place, *near, back),
        [scalar()] + [whole()] * (RANKS + 1),
        (sds((tokens, inner), BF16), pltpu.VMEM((tokens, inner), BF16)),
        (whole(), whole()),
        nbytes=2 * MIB,
        scratch_shapes=[space],
    )
    next_first = lax.ppermute(sent, "tm", back_perm)
    velocity, following, wo, own, base = call(
        project_kernel,
        (
            place,
            sizes,
            *near,
            back,
            pinned(first),
            *[in_hbm(a) for a in (w_out, own, latents, fresh_noise, next_latents)],
        ),
        [scalar()] * 2 + [whole()] * (RANKS + 2) + [anywhere()] * 5,
        (
            pltpu.HBM((frames, tokens, width), BF16),
            pltpu.HBM((frames, tokens, width), BF16),
            pltpu.VMEM((inner, width), BF16),
            pltpu.VMEM((16, width), F32),
            pltpu.VMEM((tokens, width), BF16),
        ),
        (anywhere(), anywhere(), whole(), whole(), whole()),
        flops=project_flops,
        nbytes=6 * MIB,
        scratch_shapes=[
            space,
            pltpu.VMEM((tokens, inner), BF16),
            pltpu.VMEM((frames, tokens, width), BF16),
            pltpu.VMEM((tokens, width), BF16),
            pltpu.VMEM((frames, tokens, width), BF16),
            pltpu.VMEM((frames - 1, tokens, width), BF16),
            dma((5,)),
            *[dma((3,))] * 2,
        ],
    )
    following = call(
        last_kernel,
        (sizes, next_first, pinned(wo), pinned(own), pinned(base), following),
        [scalar()] + [whole()] * 4 + [anywhere()],
        sds((frames, tokens, width), BF16),
        anywhere(),
        flops=project_flops // 2,
        nbytes=4 * MIB,
        scratch_shapes=[pltpu.VMEM((tokens, width), BF16), dma((3,))],
        input_output_aliases={5: 0},
    )
    return velocity, following


def solution(mesh):
    in_specs = (P("tm", "tok", None), P("tok", None), P(), P(), P(), P(), P(), P(), P(), P(), P())
    out_specs = (P("tm", "tok", None), P("tm", "tok", None))
    return jax.shard_map(body, mesh=mesh, in_specs=in_specs, out_specs=out_specs, check_vma=False)
```

```python
import math

import jax
import jax.numpy as jnp
from jax import lax
from jax.experimental import pallas as pl
from jax.experimental.pallas import tpu as pltpu
from jax.sharding import PartitionSpec as P

HEAD_DIM = 128
HEADS = 6
SPAN = 3
RANKS = 4
BASE2 = HEAD_DIM ** (-0.5) * math.log2(math.e)
MASKED = -1e30
FLOOR = -1e29
MIB = 1 << 20
STAT_ROWS = 16
PAUSE = 3_500_000_000
LONG = 60_000_000_000
BF16 = jnp.bfloat16
F32 = jnp.float32


def normalise(x, scale1, shift):
    values = x.astype(F32)
    center = jnp.mean(values, axis=-1, keepdims=True)
    values = values - center
    spread = jnp.mean(values * values, axis=-1, keepdims=True)
    return (values * lax.rsqrt(spread + 1e-06) * scale1 + shift).astype(BF16)


def matmul(a, b):
    return jnp.dot(a, b, preferred_element_type=F32)


def softmax_parts(q, k, bias=None):
    scores = lax.dot_general(q, k, (((1,), (1,)), ((), ())), preferred_element_type=F32)
    if bias is not None:
        scores = scores + bias
    top = jnp.max(scores, axis=-1, keepdims=True)
    if bias is not None:
        top = jnp.maximum(top, FLOOR)
    weights = jnp.exp2((scores - top) * BASE2)
    return weights.astype(BF16), jnp.sum(weights, axis=-1, keepdims=True), top


def finish(weights, total, top, v, may_be_empty):
    mixed = matmul(weights, v)
    if not may_be_empty:
        return mixed / total, top * BASE2 + jnp.log2(total)
    some = total > 0.0
    safe = jnp.where(some, total, 1.0)
    return mixed / safe, jnp.where(some, top * BASE2 + jnp.log2(safe), MASKED)


def attend(q, k, v):
    return finish(*softmax_parts(q, k), v, False)


def split3(x):
    one = x.astype(BF16).astype(F32)
    rest = x - one
    two = rest.astype(BF16).astype(F32)
    return one, two, rest - two


def swap_halves(even, odd):
    low = lax.broadcasted_iota(jnp.int32, even.shape, 1) < 4
    return jnp.where(low, even, pltpu.roll(odd, 4, 1)), jnp.where(low, pltpu.roll(even, 4, 1), odd)


def shuffle_kernel(x_hbm, out_hbm, x_ref, mixed_ref, in_sems, out_sems):
    _, tokens, width = x_ref.shape
    chunks = in_sems.shape[0]
    rows = tokens // chunks
    pairs = rows // 8
    ins, outs = [], []
    for c in range(chunks):
        r = pl.ds(c * rows, rows)
        ins.append(pltpu.make_async_copy(x_hbm.at[:, r], x_ref.at[:, r], in_sems.at[c]))
        ins[c].start()
    for c in range(chunks):
        ins[c].wait()
        first, second = [
            x_ref[f, c * rows : (c + 1) * rows].astype(F32).reshape(pairs, 8, width) for f in range(2)
        ]
        even, odd = swap_halves(first, second)
        mixed_ref[c * pairs : (c + 1) * pairs, 0] = even.astype(BF16)
        mixed_ref[c * pairs : (c + 1) * pairs, 1] = odd.astype(BF16)
        r = pl.ds(c * pairs, pairs)
        outs.append(pltpu.make_async_copy(mixed_ref.at[r], out_hbm.at[r], out_sems.at[c]))
        outs[c].start()
    for c in range(chunks):
        outs[c].wait()


def home_kernel(
    noise_ref, offset_ref, step_ref, place_ref, x_ref, table_hbm, wq_hbm, wk_hbm, wv_hbm, size_ref, own_hbm, *refs
):
    outs = refs[:RANKS]
    table_ref, q_ref, k_ref, v_ref, wq_ref, wk_ref, wv_ref, own_ref, sems, own_sem = refs[RANKS:]
    loads = []
    for n, (src, dst) in enumerate(
        ((table_hbm, table_ref), (wq_hbm, wq_ref), (wk_hbm, wk_ref), (wv_hbm, wv_ref))
    ):
        loads.append(pltpu.make_async_copy(src, dst, sems.at[n]))
        loads[n].start()
    frames, tokens, _ = x_ref.shape
    total = noise_ref.shape[0]
    loads[0].wait()
    for n in range(frames + 1):
        frame = jnp.minimum(place_ref[0] * frames + n, total - 1)
        level = noise_ref[lax.rem(frame + offset_ref[0], total)]
        size_ref[n] = step_ref[level]
        own_ref[n : n + 1, :] = table_ref[0, pl.ds(level, 1), :]
        own_ref[n + 3 : n + 4, :] = table_ref[1, pl.ds(level, 1), :] + 1.0
        own_ref[n + 6 : n + 7, :] = table_ref[2, pl.ds(level, 1), :]
    own_store = pltpu.make_async_copy(own_ref, own_hbm, own_sem)
    own_store.start()
    normed = []
    for f in range(frames):
        normed.append(normalise(x_ref[f], own_ref[f + 3 : f + 4, :], own_ref[f : f + 1, :]))
    normed = jnp.concatenate(normed, axis=0)
    for n, (ref, w) in enumerate(((q_ref, wq_ref), (k_ref, wk_ref), (v_ref, wv_ref))):
        loads[1 + n].wait()
        ref[...] = matmul(normed, w[...]).astype(BF16)
    for d in range(RANKS):
        other = place_ref[1] ^ d
        r = pl.ds(pl.multiple_of((other // 2) * tokens, tokens), tokens)
        for u in range(SPAN):
            c = pl.ds(pl.multiple_of((other % 2) * SPAN * HEAD_DIM + u * HEAD_DIM, HEAD_DIM), HEAD_DIM)
            for n, ref in enumerate((k_ref, v_ref, q_ref)):
                block = slice((n * SPAN + u) * tokens, (n * SPAN + u + 1) * tokens)
                outs[d][block] = ref[r, c]
    own_store.wait()


def column_kernel(noise_ref, offset_ref, blocks_ref, table_ref, shift_hbm, scale_hbm, bias_hbm, *refs):
    shift_ref, scale_ref, bias_ref, sems = refs
    total = noise_ref.shape[0]
    frames = shift_ref.shape[1]
    share = bias_ref.shape[0] // total
    stores = [
        pltpu.make_async_copy(src, dst, sems.at[n])
        for n, (src, dst) in enumerate(
            ((shift_ref, shift_hbm), (scale_ref, scale_hbm), (bias_ref, bias_hbm))
        )
    ]
    for f in range(total):
        level = noise_ref[lax.rem(f + offset_ref[0], total)]
        shift_ref[f // frames, f % frames : f % frames + 1, :] = table_ref[0, pl.ds(level, 1), :]
        scale_ref[f // frames, f % frames : f % frames + 1, :] = table_ref[1, pl.ds(level, 1), :] + 1.0
    stores[0].start()
    stores[1].start()
    wide = (8, total * share)
    lane = lax.broadcasted_iota(jnp.int32, wide, 1) // share
    block = jnp.zeros(wide, F32)
    for f in range(total):
        block = jnp.where(lane == f, blocks_ref[f].astype(F32), block)
    block = jnp.broadcast_to(block[0:1], bias_ref.shape)
    down = lax.broadcasted_iota(jnp.int32, bias_ref.shape, 0)
    along = lax.broadcasted_iota(jnp.int32, bias_ref.shape, 1)
    allowed = (down % share == along % share) & (down != along) & (block <= jnp.transpose(block))
    bias_ref[...] = jnp.where(allowed, 0.0, MASKED)
    stores[2].start()
    for store in stores:
        store.wait()


def pass_kernel(in_ref, out_ref):
    out_ref[...] = in_ref[...]


def spatial_kernel(*refs):
    kvs, qs, outs = refs[: 2 * RANKS], refs[:RANKS], refs[2 * RANKS :]
    tokens = HEAD_DIM
    lane = lax.broadcasted_iota(jnp.int32, (tokens, HEAD_DIM), 1)
    stats = [jnp.zeros((tokens, HEAD_DIM), F32)] * RANKS
    for u in range(SPAN):
        r = slice(u * tokens, (u + 1) * tokens)
        block = slice((2 * SPAN + u) * tokens, (2 * SPAN + u + 1) * tokens)
        keys = jnp.concatenate([ref[u * tokens : (u + 1) * tokens] for ref in kvs], axis=0)
        vals = jnp.concatenate([ref[(SPAN + u) * tokens : (SPAN + u + 1) * tokens] for ref in kvs], axis=0)
        for s in range(0, RANKS, 2):
            q = jnp.concatenate([qs[s][block], qs[s + 1][block]], axis=0)
            mixed, logs = attend(q, keys, vals)
            mixed = mixed.astype(BF16)
            for d in range(2):
                half = slice(d * tokens, (d + 1) * tokens)
                outs[s + d][r] = mixed[half]
                for n, piece in enumerate(split3(logs[half])):
                    stats[s + d] = jnp.where(lane == SPAN * u + n, piece, stats[s + d])
    for d in range(RANKS):
        turned = jnp.transpose(stats[d])[0:STAT_ROWS]
        outs[d][SPAN * tokens : SPAN * tokens + STAT_ROWS] = turned.astype(BF16)


def temporal_kernel(x_ref, *refs):
    scale_hbm, shift_hbm, wq_hbm, wk_hbm, bias_hbm, wv_hbm, out_hbm = refs[:7]
    scale_ref, shift_ref, wq_ref, wk_ref, bias_ref, wv_ref, out_ref, sems, out_sems = refs[7:]
    held = (scale_ref, shift_ref, wq_ref, wk_ref, bias_ref, wv_ref)
    loads = []
    for n, (src, dst) in enumerate(zip(refs[:6], held)):
        loads.append(pltpu.make_async_copy(src, dst, sems.at[n]))
        loads[n].start()
    groups, rows, width = x_ref.shape
    low = lax.broadcasted_iota(jnp.int32, (groups, rows, width), 1) < rows // 2

    def spread(ref):
        first = jnp.broadcast_to(ref[:, 0:1, :], low.shape)
        return jnp.where(low, first, jnp.broadcast_to(ref[:, 1:2, :], low.shape))

    loads[0].wait()
    loads[1].wait()
    normed = normalise(x_ref[...].astype(F32), spread(scale_ref), spread(shift_ref))
    normed = normed.reshape(groups * rows, width)
    loads[2].wait()
    q = matmul(normed, wq_ref[...]).astype(BF16)
    loads[3].wait()
    k = matmul(normed, wk_ref[...]).astype(BF16)
    loads[4].wait()
    lane = lax.broadcasted_iota(jnp.int32, (groups * rows, HEAD_DIM), 1)
    stats = jnp.zeros((groups * rows, HEAD_DIM), F32)
    heads = [slice(h * HEAD_DIM, (h + 1) * HEAD_DIM) for h in range(HEADS)]
    parts = [softmax_parts(q[:, own], k[:, own], bias_ref[...]) for own in heads]
    loads[5].wait()
    v = matmul(normed, wv_ref[...]).astype(BF16)
    copies = []

    def send(n):
        c = pl.ds(n * HEAD_DIM, HEAD_DIM)
        copies.append(pltpu.make_async_copy(out_ref.at[:, c], out_hbm.at[:, c], out_sems.at[n]))
        copies[n].start()

    for h, (own, (weights, total, top)) in enumerate(zip(heads, parts)):
        mixed, logs = finish(weights, total, top, v[:, own], True)
        out_ref[:, own] = mixed.astype(BF16)
        send(h)
        for m, piece in enumerate(split3(logs)):
            stats = jnp.where(lane == 8 * m + h, piece, stats)
    out_ref[:, HEADS * HEAD_DIM :] = stats.astype(BF16)
    send(HEADS)
    for copy in copies:
        copy.wait()


def reorder_kernel(time_ref, far_ref, logs_ref):
    frames, tokens, inner = far_ref.shape
    width = time_ref.shape[1]
    turned = time_ref[...].astype(F32).reshape(tokens // 8, 2, 8, width)
    for f, rows in enumerate(swap_halves(turned[:, 0], turned[:, 1])):
        rows = rows.reshape(tokens, width)
        far_ref[f] = rows[:, :inner].astype(BF16)
        stats = rows[:, inner:]
        logs_ref[f, :, 0:8] = stats[:, 0:8] + stats[:, 8:16] + stats[:, 16:24]


def merged(f, rank, near_refs, far_ref, logs_ref, space_ref, out_ref):
    for d, ref in enumerate(near_refs):
        space_ref[rank ^ d] = ref[...]
    tokens = out_ref.shape[0]
    time_log = logs_ref[f, :, 0:8]
    log_rows = []
    for h in range(HEADS):
        st = space_ref[2 * f + h // SPAN, SPAN * tokens : SPAN * tokens + STAT_ROWS].astype(F32)
        b = SPAN * (h % SPAN)
        log_rows.append(st[b : b + 1] + st[b + 1 : b + 2] + st[b + 2 : b + 3])
    log_rows.append(jnp.zeros((8 - HEADS, HEAD_DIM), F32))
    space_log = jnp.transpose(jnp.concatenate(log_rows, axis=0))
    of_space = 1.0 / (1.0 + jnp.exp2(time_log - space_log))
    of_time = 1.0 / (1.0 + jnp.exp2(space_log - time_log))
    for h in range(HEADS):
        own = slice(h * HEAD_DIM, (h + 1) * HEAD_DIM)
        u = h % SPAN
        near = space_ref[2 * f + h // SPAN, u * tokens : (u + 1) * tokens].astype(F32)
        far = far_ref[f, :, own].astype(F32)
        mixed = of_space[:, h : h + 1] * near + of_time[:, h : h + 1] * far
        out_ref[:, own] = mixed.astype(BF16)


def first_kernel(place_ref, mark_ref, *refs):
    del mark_ref
    near_refs, (far_ref, logs_ref, sent_ref, first_ref, space_ref) = refs[:RANKS], refs[RANKS:]
    merged(0, place_ref[1], near_refs, far_ref, logs_ref, space_ref, first_ref)
    sent_ref[...] = first_ref[...]


def project_kernel(place_ref, size_ref, *refs):
    near_refs = refs[:RANKS]
    far_ref, logs_ref, first_ref, wo_hbm, own_hbm, x_hbm, fresh_hbm, in_hbm_ref = refs[RANKS : RANKS + 8]
    vel_hbm, next_hbm, wo_ref, own_ref, base_ref = refs[RANKS + 8 : RANKS + 13]
    space_ref, second_ref, x_ref, fresh_ref, vel_ref, next_ref, sems, vel_sems, next_sems = refs[RANKS + 13 :]
    frames, tokens, _ = x_ref.shape
    loads = []
    for n, (src, dst) in enumerate(
        (
            (wo_hbm, wo_ref),
            (own_hbm, own_ref),
            (x_hbm, x_ref),
            (in_hbm_ref, base_ref),
            (fresh_hbm, fresh_ref),
        )
    ):
        loads.append(pltpu.make_async_copy(src, dst, sems.at[n]))
        loads[n].start()

    merged(1, place_ref[1], near_refs, far_ref, logs_ref, space_ref, second_ref)
    attended = jnp.concatenate([first_ref[...], second_ref[...]], axis=0)
    for load in loads:
        load.wait()

    @pl.when(place_ref[0] == place_ref[2])
    def _():
        base_ref[...] = fresh_ref[...]

    chunks = vel_sems.shape[0]
    width = vel_ref.shape[2] // chunks
    copies = []
    for n in range(chunks):
        c, d = slice(n * width, (n + 1) * width), pl.ds(n * width, width)
        projected = matmul(attended, wo_ref[:, c])
        for f in range(frames):
            moving = projected[f * tokens : (f + 1) * tokens] * own_ref[6 + f : 7 + f, c]
            vel_ref[f, :, c] = moving.astype(BF16)
            if f > 0:
                advanced = x_ref[f, :, c].astype(F32) + size_ref[f] * moving
                next_ref[f - 1, :, c] = advanced.astype(BF16)
        copies.append(pltpu.make_async_copy(vel_ref.at[:, :, d], vel_hbm.at[:, :, d], vel_sems.at[n]))
        copies[-1].start()
        filled = next_hbm.at[pl.ds(0, frames - 1), :, d]
        copies.append(pltpu.make_async_copy(next_ref.at[:, :, d], filled, next_sems.at[n]))
        copies[-1].start()
    for copy in copies:
        copy.wait()


def last_kernel(size_ref, att_ref, wo_ref, own_ref, base_ref, kept_ref, next_ref, out_ref, sems):
    del kept_ref
    slot = next_ref.shape[0] - 1
    chunks = sems.shape[0]
    width = out_ref.shape[1] // chunks
    copies = []
    for n in range(chunks):
        c, d = slice(n * width, (n + 1) * width), pl.ds(n * width, width)
        moving = matmul(att_ref[...], wo_ref[:, c]) * own_ref[8:9, c]
        out_ref[:, c] = (base_ref[:, c].astype(F32) + size_ref[2] * moving).astype(BF16)
        copies.append(pltpu.make_async_copy(out_ref.at[:, d], next_ref.at[slot, :, d], sems.at[n]))
        copies[n].start()
    for copy in copies:
        copy.wait()


def whole():
    return pl.BlockSpec(memory_space=pltpu.VMEM)


def scalar():
    return pl.BlockSpec(memory_space=pltpu.SMEM)


def anywhere():
    return pl.BlockSpec(memory_space=pl.ANY)


def pinned(x):
    return pltpu.with_memory_space_constraint(x, pltpu.VMEM)


def in_hbm(x):
    return pltpu.with_memory_space_constraint(x, pltpu.HBM)


def call(kernel, args, in_specs, outs, out_specs, flops=0, nbytes=0, vmem=20, **more):
    return pl.pallas_call(
        kernel,
        out_shape=outs,
        in_specs=in_specs,
        out_specs=out_specs,
        compiler_params=pltpu.CompilerParams(vmem_limit_bytes=vmem * MIB),
        cost_estimate=pl.CostEstimate(flops=flops, bytes_accessed=nbytes, transcendentals=0),
        **more,
    )(*args)


def body(
    latents,
    fresh_noise,
    noise_levels,
    offset,
    block_ids,
    mod_table,
    step_sizes,
    w_query,
    w_key,
    w_value,
    w_out,
):
    frames, tokens, width = latents.shape
    times = lax.axis_size("tm")
    ranks = lax.axis_size("tok")
    share = tokens // times
    total = frames * times
    inner = HEADS * HEAD_DIM
    sds = jax.ShapeDtypeStruct
    dma = pltpu.SemaphoreType.DMA
    back_perm = [(i, i - 1) for i in range(1, times)]
    project_flops = 2 * frames * tokens * width * inner

    def exchange(x, d):
        pairs = []
        for tm in range(times):
            for tok in range(ranks):
                side, y, core = tok // RANKS, tok % RANKS, tm % 2
                pairs.append((tm * ranks + tok, (tm - core + side) * ranks + core * RANKS + (y ^ d)))
        return lax.ppermute(x, ("tm", "tok"), pairs)

    outgoing, x = call(
        shuffle_kernel,
        (in_hbm(latents),),
        [anywhere()],
        (pltpu.HBM((tokens // 8, 2, 8, width), BF16), pltpu.VMEM((frames, tokens, width), BF16)),
        (anywhere(), whole()),
        nbytes=2 * MIB,
        scratch_shapes=[pltpu.VMEM((tokens // 8, 2, 8, width), BF16), dma((4,)), dma((4,))],
    )
    column = lax.all_to_all(outgoing.reshape(times, frames * share, width), "tm", 0, 0)

    place = lax.axis_index("tm").astype(jnp.int32)
    rank = lax.axis_index("tok").astype(jnp.int32) % RANKS
    place = jnp.stack([place, rank, jnp.int32(times - 1)])
    table = mod_table.transpose(1, 0, 2)
    sizes, own, *parts = call(
        home_kernel,
        (
            noise_levels,
            offset,
            step_sizes,
            place,
            pinned(x),
            *[in_hbm(a) for a in (table, w_query, w_key, w_value)],
        ),
        [scalar()] * 4 + [whole()] + [anywhere()] * 4,
        (
            sds((frames + 1,), F32),
            pltpu.HBM((16, width), F32),
            *[sds((3 * SPAN * tokens, HEAD_DIM), BF16)] * RANKS,
        ),
        (scalar(), anywhere(), *[whole()] * RANKS),
        flops=LONG,
        nbytes=10 * MIB,
        scratch_shapes=[
            pltpu.VMEM(table.shape, F32),
            *[pltpu.VMEM((frames * tokens, inner), BF16)] * 3,
            *[pltpu.VMEM((width, inner), BF16)] * 3,
            pltpu.VMEM((16, width), F32),
            dma((4,)),
            dma,
        ],
    )
    units = [exchange(part, d) for d, part in enumerate(parts)]

    small = (
        pltpu.VMEM((16, width), F32),
        pltpu.VMEM((times, frames, width), F32),
        pltpu.VMEM((times, frames, width), F32),
        pltpu.VMEM((total * share, total * share), F32),
    )
    table, noise_levels, sizes = lax.optimization_barrier((table, noise_levels, sizes))
    shifts, scales, bias = call(
        column_kernel,
        (noise_levels, offset, block_ids, table),
        [scalar()] * 3 + [whole()],
        tuple(pltpu.HBM(a.inner_aval.shape, F32) for a in small[1:]),
        (anywhere(),) * 3,
        nbytes=MIB // 4,
        scratch_shapes=[*small[1:], dma((3,))],
    )
    incoming, sizes = lax.optimization_barrier((latents[0], sizes))
    next_latents = lax.ppermute(incoming, "tm", back_perm)

    back = call(
        temporal_kernel,
        (column, *[in_hbm(a) for a in (scales, shifts, w_query, w_key, bias, w_value)]),
        [whole()] + [anywhere()] * 6,
        pltpu.HBM((total * share, inner + HEAD_DIM), BF16),
        anywhere(),
        flops=LONG,
        nbytes=10 * MIB,
        scratch_shapes=[
            *small[1:3],
            *[pltpu.VMEM((width, inner), BF16)] * 2,
            small[3],
            pltpu.VMEM((width, inner), BF16),
            pltpu.VMEM((total * share, inner + HEAD_DIM), BF16),
            dma((6,)),
            dma((HEADS + 1,)),
        ],
    )
    mark = step_sizes.reshape(1, -1)
    _, next_latents, mark, *units = lax.optimization_barrier((back, next_latents, mark, *units))
    mark = call(pass_kernel, (mark,), [whole()], sds(mark.shape, F32), whole(), flops=PAUSE)
    mark, *units = lax.optimization_barrier((mark, *units))
    sibling = [lax.ppermute(part, "tm", [(i, i ^ 1) for i in range(times)]) for part in units]
    back = lax.all_to_all(back.reshape(times, frames * share, inner + HEAD_DIM), "tm", 0, 0)
    back = back.reshape(times * frames * share, inner + HEAD_DIM)

    near = call(
        spatial_kernel,
        (*units, *sibling),
        [whole()] * (2 * RANKS),
        [sds((SPAN * tokens + STAT_ROWS, HEAD_DIM), BF16)] * RANKS,
        [whole()] * RANKS,
        flops=4 * SPAN * RANKS * ranks * tokens * tokens * HEAD_DIM,
        nbytes=3 * MIB,
    )
    near = [exchange(part, d) for d, part in enumerate(near)]

    space = pltpu.VMEM((RANKS, SPAN * tokens + STAT_ROWS, HEAD_DIM), BF16)
    far, logs = call(
        reorder_kernel,
        (back,),
        [whole()],
        (pltpu.VMEM((frames, tokens, inner), BF16), pltpu.VMEM((frames, tokens, HEAD_DIM), F32)),
        (whole(), whole()),
        flops=LONG,
        nbytes=MIB,
    )
    sent, first = call(
        first_kernel,
        (place, mark, *near, pinned(far), pinned(logs)),
        [scalar()] + [whole()] * (RANKS + 3),
        (sds((tokens, inner), BF16), pltpu.VMEM((tokens, inner), BF16)),
        (whole(), whole()),
        nbytes=2 * MIB,
        scratch_shapes=[space],
    )
    next_first = lax.ppermute(sent, "tm", back_perm)
    velocity, following, wo, own, base = call(
        project_kernel,
        (
            place,
            sizes,
            *near,
            pinned(far),
            pinned(logs),
            pinned(first),
            *[in_hbm(a) for a in (w_out, own, latents, fresh_noise, next_latents)],
        ),
        [scalar()] * 2 + [whole()] * (RANKS + 3) + [anywhere()] * 5,
        (
            pltpu.HBM((frames, tokens, width), BF16),
            pltpu.HBM((frames, tokens, width), BF16),
            pltpu.VMEM((inner, width), BF16),
            pltpu.VMEM((16, width), F32),
            pltpu.VMEM((tokens, width), BF16),
        ),
        (anywhere(), anywhere(), whole(), whole(), whole()),
        flops=project_flops,
        nbytes=6 * MIB,
        scratch_shapes=[
            space,
            pltpu.VMEM((tokens, inner), BF16),
            pltpu.VMEM((frames, tokens, width), BF16),
            pltpu.VMEM((tokens, width), BF16),
            pltpu.VMEM((frames, tokens, width), BF16),
            pltpu.VMEM((frames - 1, tokens, width), BF16),
            dma((5,)),
            *[dma((3,))] * 2,
        ],
    )
    following = call(
        last_kernel,
        (sizes, next_first, pinned(wo), pinned(own), pinned(base), following),
        [scalar()] + [whole()] * 4 + [anywhere()],
        sds((frames, tokens, width), BF16),
        anywhere(),
        flops=project_flops // 2,
        nbytes=4 * MIB,
        scratch_shapes=[pltpu.VMEM((tokens, width), BF16), dma((3,))],
        input_output_aliases={5: 0},
    )
    return velocity, following


def solution(mesh):
    in_specs = (P("tm", "tok", None), P("tok", None), P(), P(), P(), P(), P(), P(), P(), P(), P())
    out_specs = (P("tm", "tok", None), P("tm", "tok", None))
    return jax.shard_map(body, mesh=mesh, in_specs=in_specs, out_specs=out_specs, check_vma=False)
```

```python
import math

import jax
import jax.numpy as jnp
from jax import lax
from jax.experimental import pallas as pl
from jax.experimental.pallas import tpu as pltpu
from jax.sharding import PartitionSpec as P

HEAD_DIM = 128
HEADS = 6
SPAN = 3
RANKS = 4
BASE2 = HEAD_DIM ** (-0.5) * math.log2(math.e)
MASKED = -1e30
FLOOR = -1e29
MIB = 1 << 20
STAT_ROWS = 16
PAUSE = 3_500_000_000
LONG = 60_000_000_000
BF16 = jnp.bfloat16
F32 = jnp.float32


def normalise(x, scale1, shift):
    values = x.astype(F32)
    center = jnp.mean(values, axis=-1, keepdims=True)
    values = values - center
    spread = jnp.mean(values * values, axis=-1, keepdims=True)
    return (values * lax.rsqrt(spread + 1e-06) * scale1 + shift).astype(BF16)


def matmul(a, b):
    return jnp.dot(a, b, preferred_element_type=F32)


def softmax_parts(q, k, bias=None):
    scores = lax.dot_general(q, k, (((1,), (1,)), ((), ())), preferred_element_type=F32)
    if bias is not None:
        scores = scores + bias
    top = jnp.max(scores, axis=-1, keepdims=True)
    if bias is not None:
        top = jnp.maximum(top, FLOOR)
    weights = jnp.exp2((scores - top) * BASE2)
    return weights.astype(BF16), jnp.sum(weights, axis=-1, keepdims=True), top


def finish(weights, total, top, v, may_be_empty):
    mixed = matmul(weights, v)
    if not may_be_empty:
        return mixed / total, top * BASE2 + jnp.log2(total)
    some = total > 0.0
    safe = jnp.where(some, total, 1.0)
    return mixed / safe, jnp.where(some, top * BASE2 + jnp.log2(safe), MASKED)


def attend(q, k, v):
    return finish(*softmax_parts(q, k), v, False)


def split3(x):
    one = x.astype(BF16).astype(F32)
    rest = x - one
    two = rest.astype(BF16).astype(F32)
    return one, two, rest - two


def swap_halves(even, odd):
    low = lax.broadcasted_iota(jnp.int32, even.shape, 1) < 4
    return jnp.where(low, even, pltpu.roll(odd, 4, 1)), jnp.where(low, pltpu.roll(even, 4, 1), odd)


def shuffle_kernel(x_hbm, out_hbm, x_ref, mixed_ref, in_sems, out_sems):
    _, tokens, width = x_ref.shape
    chunks = in_sems.shape[0]
    rows = tokens // chunks
    pairs = rows // 8
    ins, outs = [], []
    for c in range(chunks):
        r = pl.ds(c * rows, rows)
        ins.append(pltpu.make_async_copy(x_hbm.at[:, r], x_ref.at[:, r], in_sems.at[c]))
        ins[c].start()
    for c in range(chunks):
        ins[c].wait()
        first, second = [
            x_ref[f, c * rows : (c + 1) * rows].astype(F32).reshape(pairs, 8, width) for f in range(2)
        ]
        even, odd = swap_halves(first, second)
        mixed_ref[c * pairs : (c + 1) * pairs, 0] = even.astype(BF16)
        mixed_ref[c * pairs : (c + 1) * pairs, 1] = odd.astype(BF16)
        r = pl.ds(c * pairs, pairs)
        outs.append(pltpu.make_async_copy(mixed_ref.at[r], out_hbm.at[r], out_sems.at[c]))
        outs[c].start()
    for c in range(chunks):
        outs[c].wait()


def home_kernel(
    noise_ref, offset_ref, step_ref, place_ref, x_ref, table_hbm, wq_hbm, wk_hbm, wv_hbm, size_ref, own_hbm, *refs
):
    outs = refs[:RANKS]
    table_ref, q_ref, k_ref, v_ref, wq_ref, wk_ref, wv_ref, own_ref, sems, own_sem = refs[RANKS:]
    loads = []
    for n, (src, dst) in enumerate(
        ((table_hbm, table_ref), (wq_hbm, wq_ref), (wk_hbm, wk_ref), (wv_hbm, wv_ref))
    ):
        loads.append(pltpu.make_async_copy(src, dst, sems.at[n]))
        loads[n].start()
    frames, tokens, _ = x_ref.shape
    total = noise_ref.shape[0]
    loads[0].wait()
    for n in range(frames + 1):
        frame = jnp.minimum(place_ref[0] * frames + n, total - 1)
        level = noise_ref[lax.rem(frame + offset_ref[0], total)]
        size_ref[n] = step_ref[level]
        own_ref[n : n + 1, :] = table_ref[0, pl.ds(level, 1), :]
        own_ref[n + 3 : n + 4, :] = table_ref[1, pl.ds(level, 1), :] + 1.0
        own_ref[n + 6 : n + 7, :] = table_ref[2, pl.ds(level, 1), :]
    own_store = pltpu.make_async_copy(own_ref, own_hbm, own_sem)
    own_store.start()
    normed = []
    for f in range(frames):
        normed.append(normalise(x_ref[f], own_ref[f + 3 : f + 4, :], own_ref[f : f + 1, :]))
    normed = jnp.concatenate(normed, axis=0)
    for n, (ref, w) in enumerate(((q_ref, wq_ref), (k_ref, wk_ref), (v_ref, wv_ref))):
        loads[1 + n].wait()
        ref[...] = matmul(normed, w[...]).astype(BF16)
    for d in range(RANKS):
        other = place_ref[1] ^ d
        r = pl.ds(pl.multiple_of((other // 2) * tokens, tokens), tokens)
        for u in range(SPAN):
            c = pl.ds(pl.multiple_of((other % 2) * SPAN * HEAD_DIM + u * HEAD_DIM, HEAD_DIM), HEAD_DIM)
            for n, ref in enumerate((k_ref, v_ref, q_ref)):
                block = slice((n * SPAN + u) * tokens, (n * SPAN + u + 1) * tokens)
                outs[d][block] = ref[r, c]
    own_store.wait()


def column_kernel(noise_ref, offset_ref, blocks_ref, table_ref, *refs):
    count = 1
    sources, (shift_hbm, scale_hbm, bias_hbm), refs = refs[:count], refs[count : count + 3], refs[count + 3 :]
    held, (shift_ref, scale_ref, bias_ref, sems, load_sems) = refs[:count], refs[count:]
    loads = []
    for n, (src, dst) in enumerate(zip(sources, held)):
        loads.append(pltpu.make_async_copy(src, dst, load_sems.at[n]))
        loads[n].start()
    total = noise_ref.shape[0]
    frames = shift_ref.shape[1]
    share = bias_ref.shape[0] // total
    stores = [
        pltpu.make_async_copy(src, dst, sems.at[n])
        for n, (src, dst) in enumerate(
            ((shift_ref, shift_hbm), (scale_ref, scale_hbm), (bias_ref, bias_hbm))
        )
    ]
    for f in range(total):
        level = noise_ref[lax.rem(f + offset_ref[0], total)]
        shift_ref[f // frames, f % frames : f % frames + 1, :] = table_ref[0, pl.ds(level, 1), :]
        scale_ref[f // frames, f % frames : f % frames + 1, :] = table_ref[1, pl.ds(level, 1), :] + 1.0
    stores[0].start()
    stores[1].start()
    wide = (8, total * share)
    lane = lax.broadcasted_iota(jnp.int32, wide, 1) // share
    block = jnp.zeros(wide, F32)
    for f in range(total):
        block = jnp.where(lane == f, blocks_ref[f].astype(F32), block)
    block = jnp.broadcast_to(block[0:1], bias_ref.shape)
    down = lax.broadcasted_iota(jnp.int32, bias_ref.shape, 0)
    along = lax.broadcasted_iota(jnp.int32, bias_ref.shape, 1)
    allowed = (down % share == along % share) & (down != along) & (block <= jnp.transpose(block))
    bias_ref[...] = jnp.where(allowed, 0.0, MASKED)
    stores[2].start()
    for copy in stores + loads:
        copy.wait()


def pass_kernel(in_ref, out_ref):
    out_ref[...] = in_ref[...]


def spatial_kernel(*refs):
    kvs, qs, outs = refs[: 2 * RANKS], refs[:RANKS], refs[2 * RANKS :]
    tokens = HEAD_DIM
    lane = lax.broadcasted_iota(jnp.int32, (tokens, HEAD_DIM), 1)
    stats = [jnp.zeros((tokens, HEAD_DIM), F32)] * RANKS
    for u in range(SPAN):
        r = slice(u * tokens, (u + 1) * tokens)
        block = slice((2 * SPAN + u) * tokens, (2 * SPAN + u + 1) * tokens)
        keys = jnp.concatenate([ref[u * tokens : (u + 1) * tokens] for ref in kvs], axis=0)
        vals = jnp.concatenate([ref[(SPAN + u) * tokens : (SPAN + u + 1) * tokens] for ref in kvs], axis=0)
        for s in range(0, RANKS, 2):
            q = jnp.concatenate([qs[s][block], qs[s + 1][block]], axis=0)
            mixed, logs = attend(q, keys, vals)
            mixed = mixed.astype(BF16)
            for d in range(2):
                half = slice(d * tokens, (d + 1) * tokens)
                outs[s + d][r] = mixed[half]
                for n, piece in enumerate(split3(logs[half])):
                    stats[s + d] = jnp.where(lane == SPAN * u + n, piece, stats[s + d])
    for d in range(RANKS):
        turned = jnp.transpose(stats[d])[0:STAT_ROWS]
        outs[d][SPAN * tokens : SPAN * tokens + STAT_ROWS] = turned.astype(BF16)


def temporal_kernel(x_ref, wq_ref, *refs):
    scale_hbm, shift_hbm, wk_hbm, bias_hbm, wv_hbm, out_hbm = refs[:6]
    scale_ref, shift_ref, wk_ref, bias_ref, wv_ref, out_ref, sems, out_sems = refs[6:]
    loads = {}
    for n, (name, src, dst) in enumerate((
        ("scale", scale_hbm, scale_ref), ("shift", shift_hbm, shift_ref), ("wk", wk_hbm, wk_ref), ("bias", bias_hbm, bias_ref), ("wv", wv_hbm, wv_ref),
    )):
        loads[name] = pltpu.make_async_copy(src, dst, sems.at[n])
        loads[name].start()
    groups, rows, width = x_ref.shape
    low = lax.broadcasted_iota(jnp.int32, (groups, rows, width), 1) < rows // 2

    def spread(ref):
        first = jnp.broadcast_to(ref[:, 0:1, :], low.shape)
        return jnp.where(low, first, jnp.broadcast_to(ref[:, 1:2, :], low.shape))

    loads["scale"].wait()
    loads["shift"].wait()
    normed = normalise(x_ref[...].astype(F32), spread(scale_ref), spread(shift_ref))
    normed = normed.reshape(groups * rows, width)
    q = matmul(normed, wq_ref[...]).astype(BF16)
    loads["wk"].wait()
    k = matmul(normed, wk_ref[...]).astype(BF16)
    loads["bias"].wait()
    lane = lax.broadcasted_iota(jnp.int32, (groups * rows, HEAD_DIM), 1)
    stats = jnp.zeros((groups * rows, HEAD_DIM), F32)
    heads = [slice(h * HEAD_DIM, (h + 1) * HEAD_DIM) for h in range(HEADS)]
    parts = [softmax_parts(q[:, own], k[:, own], bias_ref[...]) for own in heads]
    loads["wv"].wait()
    v = matmul(normed, wv_ref[...]).astype(BF16)
    copies = []

    def send(n):
        c = pl.ds(n * HEAD_DIM, HEAD_DIM)
        copies.append(pltpu.make_async_copy(out_ref.at[:, c], out_hbm.at[:, c], out_sems.at[n]))
        copies[n].start()

    for h, (own, (weights, total, top)) in enumerate(zip(heads, parts)):
        mixed, logs = finish(weights, total, top, v[:, own], True)
        out_ref[:, own] = mixed.astype(BF16)
        send(h)
        for m, piece in enumerate(split3(logs)):
            stats = jnp.where(lane == 8 * m + h, piece, stats)
    out_ref[:, HEADS * HEAD_DIM :] = stats.astype(BF16)
    send(HEADS)
    for copy in copies:
        copy.wait()


def reorder_kernel(time_ref, wo_hbm, own_hbm, far_ref, logs_ref, wo_ref, own_ref, sems):
    loads = []
    for n, (src, dst) in enumerate(((wo_hbm, wo_ref), (own_hbm, own_ref))):
        loads.append(pltpu.make_async_copy(src, dst, sems.at[n]))
        loads[n].start()
    frames, tokens, inner = far_ref.shape
    width = time_ref.shape[1]
    turned = time_ref[...].astype(F32).reshape(tokens // 8, 2, 8, width)
    for f, rows in enumerate(swap_halves(turned[:, 0], turned[:, 1])):
        rows = rows.reshape(tokens, width)
        far_ref[f] = rows[:, :inner].astype(BF16)
        stats = rows[:, inner:]
        logs_ref[f, :, 0:8] = stats[:, 0:8] + stats[:, 8:16] + stats[:, 16:24]
    for load in loads:
        load.wait()


def merged(f, rank, near_refs, far_ref, logs_ref, space_ref, out_ref):
    for d, ref in enumerate(near_refs):
        space_ref[rank ^ d] = ref[...]
    tokens = out_ref.shape[0]
    time_log = logs_ref[f, :, 0:8]
    log_rows = []
    for h in range(HEADS):
        st = space_ref[2 * f + h // SPAN, SPAN * tokens : SPAN * tokens + STAT_ROWS].astype(F32)
        b = SPAN * (h % SPAN)
        log_rows.append(st[b : b + 1] + st[b + 1 : b + 2] + st[b + 2 : b + 3])
    log_rows.append(jnp.zeros((8 - HEADS, HEAD_DIM), F32))
    space_log = jnp.transpose(jnp.concatenate(log_rows, axis=0))
    of_space = 1.0 / (1.0 + jnp.exp2(time_log - space_log))
    of_time = 1.0 / (1.0 + jnp.exp2(space_log - time_log))
    for h in range(HEADS):
        own = slice(h * HEAD_DIM, (h + 1) * HEAD_DIM)
        u = h % SPAN
        near = space_ref[2 * f + h // SPAN, u * tokens : (u + 1) * tokens].astype(F32)
        far = far_ref[f, :, own].astype(F32)
        mixed = of_space[:, h : h + 1] * near + of_time[:, h : h + 1] * far
        out_ref[:, own] = mixed.astype(BF16)


def first_kernel(place_ref, mark_ref, *refs):
    del mark_ref
    near_refs, (far_ref, logs_ref, sent_ref, first_ref, space_ref) = refs[:RANKS], refs[RANKS:]
    merged(0, place_ref[1], near_refs, far_ref, logs_ref, space_ref, first_ref)
    sent_ref[...] = first_ref[...]


def project_kernel(place_ref, size_ref, *refs):
    near_refs = refs[:RANKS]
    far_ref, logs_ref, first_ref, wo_ref, own_ref, x_hbm, fresh_hbm, in_hbm_ref = refs[RANKS : RANKS + 8]
    vel_hbm, next_hbm, base_ref = refs[RANKS + 8 : RANKS + 11]
    space_ref, second_ref, x_ref, fresh_ref, vel_ref, next_ref, sems, vel_sems, next_sems = refs[RANKS + 11 :]
    frames, tokens, _ = x_ref.shape
    loads = []
    for n, (src, dst) in enumerate(
        (
            (x_hbm, x_ref),
            (in_hbm_ref, base_ref),
            (fresh_hbm, fresh_ref),
        )
    ):
        loads.append(pltpu.make_async_copy(src, dst, sems.at[n]))
        loads[n].start()

    merged(1, place_ref[1], near_refs, far_ref, logs_ref, space_ref, second_ref)
    attended = jnp.concatenate([first_ref[...], second_ref[...]], axis=0)
    for load in loads:
        load.wait()

    @pl.when(place_ref[0] == place_ref[2])
    def _():
        base_ref[...] = fresh_ref[...]

    chunks = vel_sems.shape[0]
    width = vel_ref.shape[2] // chunks
    copies = []
    for n in range(chunks):
        c, d = slice(n * width, (n + 1) * width), pl.ds(n * width, width)
        projected = matmul(attended, wo_ref[:, c])
        for f in range(frames):
            moving = projected[f * tokens : (f + 1) * tokens] * own_ref[6 + f : 7 + f, c]
            vel_ref[f, :, c] = moving.astype(BF16)
            if f > 0:
                advanced = x_ref[f, :, c].astype(F32) + size_ref[f] * moving
                next_ref[f - 1, :, c] = advanced.astype(BF16)
        copies.append(pltpu.make_async_copy(vel_ref.at[:, :, d], vel_hbm.at[:, :, d], vel_sems.at[n]))
        copies[-1].start()
        filled = next_hbm.at[pl.ds(0, frames - 1), :, d]
        copies.append(pltpu.make_async_copy(next_ref.at[:, :, d], filled, next_sems.at[n]))
        copies[-1].start()
    for copy in copies:
        copy.wait()


def last_kernel(size_ref, att_ref, wo_ref, own_ref, base_ref, kept_ref, next_ref, out_ref, sems):
    del kept_ref
    slot = next_ref.shape[0] - 1
    chunks = sems.shape[0]
    width = out_ref.shape[1] // chunks
    copies = []
    for n in range(chunks):
        c, d = slice(n * width, (n + 1) * width), pl.ds(n * width, width)
        moving = matmul(att_ref[...], wo_ref[:, c]) * own_ref[8:9, c]
        out_ref[:, c] = (base_ref[:, c].astype(F32) + size_ref[2] * moving).astype(BF16)
        copies.append(pltpu.make_async_copy(out_ref.at[:, d], next_ref.at[slot, :, d], sems.at[n]))
        copies[n].start()
    for copy in copies:
        copy.wait()


def whole():
    return pl.BlockSpec(memory_space=pltpu.VMEM)


def scalar():
    return pl.BlockSpec(memory_space=pltpu.SMEM)


def anywhere():
    return pl.BlockSpec(memory_space=pl.ANY)


def pinned(x):
    return pltpu.with_memory_space_constraint(x, pltpu.VMEM)


def in_hbm(x):
    return pltpu.with_memory_space_constraint(x, pltpu.HBM)


def call(kernel, args, in_specs, outs, out_specs, flops=0, nbytes=0, vmem=20, **more):
    return pl.pallas_call(
        kernel,
        out_shape=outs,
        in_specs=in_specs,
        out_specs=out_specs,
        compiler_params=pltpu.CompilerParams(vmem_limit_bytes=vmem * MIB),
        cost_estimate=pl.CostEstimate(flops=flops, bytes_accessed=nbytes, transcendentals=0),
        **more,
    )(*args)


def body(
    latents,
    fresh_noise,
    noise_levels,
    offset,
    block_ids,
    mod_table,
    step_sizes,
    w_query,
    w_key,
    w_value,
    w_out,
):
    frames, tokens, width = latents.shape
    times = lax.axis_size("tm")
    ranks = lax.axis_size("tok")
    share = tokens // times
    total = frames * times
    inner = HEADS * HEAD_DIM
    sds = jax.ShapeDtypeStruct
    dma = pltpu.SemaphoreType.DMA
    back_perm = [(i, i - 1) for i in range(1, times)]
    project_flops = 2 * frames * tokens * width * inner

    def exchange(x, d):
        pairs = []
        for tm in range(times):
            for tok in range(ranks):
                side, y, core = tok // RANKS, tok % RANKS, tm % 2
                pairs.append((tm * ranks + tok, (tm - core + side) * ranks + core * RANKS + (y ^ d)))
        return lax.ppermute(x, ("tm", "tok"), pairs)

    outgoing, x = call(
        shuffle_kernel,
        (in_hbm(latents),),
        [anywhere()],
        (pltpu.HBM((tokens // 8, 2, 8, width), BF16), pltpu.VMEM((frames, tokens, width), BF16)),
        (anywhere(), whole()),
        nbytes=2 * MIB,
        scratch_shapes=[pltpu.VMEM((tokens // 8, 2, 8, width), BF16), dma((4,)), dma((4,))],
    )
    column = lax.all_to_all(outgoing.reshape(times, frames * share, width), "tm", 0, 0)

    place = lax.axis_index("tm").astype(jnp.int32)
    rank = lax.axis_index("tok").astype(jnp.int32) % RANKS
    place = jnp.stack([place, rank, jnp.int32(times - 1)])
    table = mod_table.transpose(1, 0, 2)
    sizes, own, *parts = call(
        home_kernel,
        (
            noise_levels,
            offset,
            step_sizes,
            place,
            pinned(x),
            *[in_hbm(a) for a in (table, w_query, w_key, w_value)],
        ),
        [scalar()] * 4 + [whole()] + [anywhere()] * 4,
        (
            sds((frames + 1,), F32),
            pltpu.HBM((16, width), F32),
            *[sds((3 * SPAN * tokens, HEAD_DIM), BF16)] * RANKS,
        ),
        (scalar(), anywhere(), *[whole()] * RANKS),
        flops=LONG,
        nbytes=10 * MIB,
        scratch_shapes=[
            pltpu.VMEM(table.shape, F32),
            *[pltpu.VMEM((frames * tokens, inner), BF16)] * 3,
            *[pltpu.VMEM((width, inner), BF16)] * 3,
            pltpu.VMEM((16, width), F32),
            dma((4,)),
            dma,
        ],
    )
    units = [exchange(part, d) for d, part in enumerate(parts)]

    small = (
        pltpu.VMEM((16, width), F32),
        pltpu.VMEM((times, frames, width), F32),
        pltpu.VMEM((times, frames, width), F32),
        pltpu.VMEM((total * share, total * share), F32),
    )
    table, noise_levels, sizes = lax.optimization_barrier((table, noise_levels, sizes))
    shifts, scales, bias, *fetched = call(
        column_kernel,
        (noise_levels, offset, block_ids, table, *[in_hbm(a) for a in (w_query, w_key, w_value)[:1]]),
        [scalar()] * 3 + [whole()] + [anywhere()] * 1,
        (
            *[pltpu.HBM(a.inner_aval.shape, F32) for a in small[1:]],
            *[pltpu.VMEM((width, inner), BF16)] * 1,
        ),
        (*[anywhere()] * 3, *[whole()] * 1),
        nbytes=MIB // 4,
        scratch_shapes=[*small[1:], dma((3,)), dma((1,))],
    )
    incoming, sizes = lax.optimization_barrier((latents[0], sizes))
    next_latents = lax.ppermute(incoming, "tm", back_perm)

    back = call(
        temporal_kernel,
        (column, *[pinned(a) for a in fetched], *[in_hbm(a) for a in (scales, shifts, w_key, bias, w_value)]),
        [whole()] * 2 + [anywhere()] * 5,
        pltpu.HBM((total * share, inner + HEAD_DIM), BF16),
        anywhere(),
        flops=LONG,
        nbytes=10 * MIB,
        scratch_shapes=[
            *small[1:3],
            *[pltpu.VMEM((width, inner), BF16)] * 1,
            small[3],
            *[pltpu.VMEM((width, inner), BF16)] * 1,
            pltpu.VMEM((total * share, inner + HEAD_DIM), BF16),
            dma((5,)),
            dma((HEADS + 1,)),
        ],
    )
    mark = step_sizes.reshape(1, -1)
    _, next_latents, mark, *units = lax.optimization_barrier((back, next_latents, mark, *units))
    mark = call(pass_kernel, (mark,), [whole()], sds(mark.shape, F32), whole(), flops=PAUSE)
    mark, *units = lax.optimization_barrier((mark, *units))
    sibling = [lax.ppermute(part, "tm", [(i, i ^ 1) for i in range(times)]) for part in units]
    back = lax.all_to_all(back.reshape(times, frames * share, inner + HEAD_DIM), "tm", 0, 0)
    back = back.reshape(times * frames * share, inner + HEAD_DIM)

    near = call(
        spatial_kernel,
        (*units, *sibling),
        [whole()] * (2 * RANKS),
        [sds((SPAN * tokens + STAT_ROWS, HEAD_DIM), BF16)] * RANKS,
        [whole()] * RANKS,
        flops=4 * SPAN * RANKS * ranks * tokens * tokens * HEAD_DIM,
        nbytes=3 * MIB,
    )
    near = [exchange(part, d) for d, part in enumerate(near)]

    space = pltpu.VMEM((RANKS, SPAN * tokens + STAT_ROWS, HEAD_DIM), BF16)
    far, logs, wo, own = call(
        reorder_kernel,
        (back, in_hbm(w_out), in_hbm(own)),
        [whole()] + [anywhere()] * 2,
        (
            pltpu.VMEM((frames, tokens, inner), BF16),
            pltpu.VMEM((frames, tokens, HEAD_DIM), F32),
            pltpu.VMEM((inner, width), BF16),
            pltpu.VMEM((16, width), F32),
        ),
        (whole(),) * 4,
        scratch_shapes=[dma((2,))],
        flops=LONG,
        nbytes=MIB,
    )
    sent, first = call(
        first_kernel,
        (place, mark, *near, pinned(far), pinned(logs)),
        [scalar()] + [whole()] * (RANKS + 3),
        (sds((tokens, inner), BF16), pltpu.VMEM((tokens, inner), BF16)),
        (whole(), whole()),
        nbytes=2 * MIB,
        scratch_shapes=[space],
    )
    next_first = lax.ppermute(sent, "tm", back_perm)
    velocity, following, base = call(
        project_kernel,
        (
            place,
            sizes,
            *near,
            pinned(far),
            pinned(logs),
            pinned(first),
            pinned(wo),
            pinned(own),
            *[in_hbm(a) for a in (latents, fresh_noise, next_latents)],
        ),
        [scalar()] * 2 + [whole()] * (RANKS + 5) + [anywhere()] * 3,
        (
            pltpu.HBM((frames, tokens, width), BF16),
            pltpu.HBM((frames, tokens, width), BF16),
            pltpu.VMEM((tokens, width), BF16),
        ),
        (anywhere(), anywhere(), whole()),
        flops=project_flops,
        nbytes=6 * MIB,
        scratch_shapes=[
            space,
            pltpu.VMEM((tokens, inner), BF16),
            pltpu.VMEM((frames, tokens, width), BF16),
            pltpu.VMEM((tokens, width), BF16),
            pltpu.VMEM((frames, tokens, width), BF16),
            pltpu.VMEM((frames - 1, tokens, width), BF16),
            dma((3,)),
            *[dma((3,))] * 2,
        ],
    )
    following = call(
        last_kernel,
        (sizes, next_first, pinned(wo), pinned(own), pinned(base), following),
        [scalar()] + [whole()] * 4 + [anywhere()],
        sds((frames, tokens, width), BF16),
        anywhere(),
        flops=project_flops // 2,
        nbytes=4 * MIB,
        scratch_shapes=[pltpu.VMEM((tokens, width), BF16), dma((3,))],
        input_output_aliases={5: 0},
    )
    return velocity, following


def solution(mesh):
    in_specs = (P("tm", "tok", None), P("tok", None), P(), P(), P(), P(), P(), P(), P(), P(), P())
    out_specs = (P("tm", "tok", None), P("tm", "tok", None))
    return jax.shard_map(body, mesh=mesh, in_specs=in_specs, out_specs=out_specs, check_vma=False)
```

```python
import math

import jax
import jax.numpy as jnp
from jax import lax
from jax.experimental import pallas as pl
from jax.experimental.pallas import tpu as pltpu
from jax.sharding import PartitionSpec as P

HEAD_DIM = 128
HEADS = 6
SPAN = 3
RANKS = 4
BASE2 = HEAD_DIM ** (-0.5) * math.log2(math.e)
MASKED = -1e30
FLOOR = -1e29
MIB = 1 << 20
STAT_ROWS = 16
PAUSE = 3_500_000_000
LONG = 60_000_000_000
BF16 = jnp.bfloat16
F32 = jnp.float32


def normalise(x, scale1, shift):
    values = x.astype(F32)
    center = jnp.mean(values, axis=-1, keepdims=True)
    values = values - center
    spread = jnp.mean(values * values, axis=-1, keepdims=True)
    return (values * lax.rsqrt(spread + 1e-06) * scale1 + shift).astype(BF16)


def matmul(a, b):
    return jnp.dot(a, b, preferred_element_type=F32)


def softmax_parts(q, k, bias=None):
    scores = lax.dot_general(q, k, (((1,), (1,)), ((), ())), preferred_element_type=F32)
    if bias is not None:
        scores = scores + bias
    top = jnp.max(scores, axis=-1, keepdims=True)
    if bias is not None:
        top = jnp.maximum(top, FLOOR)
    weights = jnp.exp2((scores - top) * BASE2)
    return weights.astype(BF16), jnp.sum(weights, axis=-1, keepdims=True), top


def finish(weights, total, top, v, may_be_empty):
    mixed = matmul(weights, v)
    if not may_be_empty:
        return mixed / total, top * BASE2 + jnp.log2(total)
    some = total > 0.0
    safe = jnp.where(some, total, 1.0)
    return mixed / safe, jnp.where(some, top * BASE2 + jnp.log2(safe), MASKED)


def attend(q, k, v):
    return finish(*softmax_parts(q, k), v, False)


def split3(x):
    one = x.astype(BF16).astype(F32)
    rest = x - one
    two = rest.astype(BF16).astype(F32)
    return one, two, rest - two


def swap_halves(even, odd):
    low = lax.broadcasted_iota(jnp.int32, even.shape, 1) < 4
    return jnp.where(low, even, pltpu.roll(odd, 4, 1)), jnp.where(low, pltpu.roll(even, 4, 1), odd)


def shuffle_kernel(x_hbm, out_hbm, first_hbm, x_ref, mixed_ref, in_sems, out_sems, first_sem):
    _, tokens, width = x_ref.shape
    chunks = in_sems.shape[0]
    rows = tokens // chunks
    pairs = rows // 8
    ins, outs = [], []
    for c in range(chunks):
        r = pl.ds(c * rows, rows)
        ins.append(pltpu.make_async_copy(x_hbm.at[:, r], x_ref.at[:, r], in_sems.at[c]))
        ins[c].start()
    for c in range(chunks):
        ins[c].wait()
        first, second = [
            x_ref[f, c * rows : (c + 1) * rows].astype(F32).reshape(pairs, 8, width) for f in range(2)
        ]
        even, odd = swap_halves(first, second)
        mixed_ref[c * pairs : (c + 1) * pairs, 0] = even.astype(BF16)
        mixed_ref[c * pairs : (c + 1) * pairs, 1] = odd.astype(BF16)
        r = pl.ds(c * pairs, pairs)
        outs.append(pltpu.make_async_copy(mixed_ref.at[r], out_hbm.at[r], out_sems.at[c]))
        outs[c].start()
    outs.append(pltpu.make_async_copy(x_ref.at[0], first_hbm, first_sem))
    outs[-1].start()
    for copy in outs:
        copy.wait()


def home_kernel(
    noise_ref,
    offset_ref,
    step_ref,
    blocks_ref,
    place_ref,
    x_ref,
    table_hbm,
    wq_hbm,
    wk_hbm,
    wv_hbm,
    size_ref,
    own_hbm,
    shift_hbm,
    scale_hbm,
    bias_hbm,
    *refs,
):
    outs = refs[:RANKS]
    table_ref, q_ref, k_ref, v_ref, wq_ref, wk_ref, wv_ref, *refs = refs[RANKS:]
    own_ref, shift_ref, scale_ref, bias_ref, sems, store_sems = refs
    loads = []
    for n, (src, dst) in enumerate(
        ((table_hbm, table_ref), (wq_hbm, wq_ref), (wk_hbm, wk_ref), (wv_hbm, wv_ref))
    ):
        loads.append(pltpu.make_async_copy(src, dst, sems.at[n]))
        loads[n].start()
    frames, tokens, _ = x_ref.shape
    total = noise_ref.shape[0]
    loads[0].wait()
    for n in range(frames + 1):
        frame = jnp.minimum(place_ref[0] * frames + n, total - 1)
        level = noise_ref[lax.rem(frame + offset_ref[0], total)]
        size_ref[n] = step_ref[level]
        own_ref[n : n + 1, :] = table_ref[0, pl.ds(level, 1), :]
        own_ref[n + 3 : n + 4, :] = table_ref[1, pl.ds(level, 1), :] + 1.0
        own_ref[n + 6 : n + 7, :] = table_ref[2, pl.ds(level, 1), :]
    stores = [
        pltpu.make_async_copy(src, dst, store_sems.at[n])
        for n, (src, dst) in enumerate(
            ((own_ref, own_hbm), (shift_ref, shift_hbm), (scale_ref, scale_hbm), (bias_ref, bias_hbm))
        )
    ]
    stores[0].start()
    share = bias_ref.shape[0] // total
    for f in range(total):
        level = noise_ref[lax.rem(f + offset_ref[0], total)]
        shift_ref[f // frames, f % frames : f % frames + 1, :] = table_ref[0, pl.ds(level, 1), :]
        scale_ref[f // frames, f % frames : f % frames + 1, :] = table_ref[1, pl.ds(level, 1), :] + 1.0
    stores[1].start()
    stores[2].start()
    wide = (8, total * share)
    lane = lax.broadcasted_iota(jnp.int32, wide, 1) // share
    block = jnp.zeros(wide, F32)
    for f in range(total):
        block = jnp.where(lane == f, blocks_ref[f].astype(F32), block)
    block = jnp.broadcast_to(block[0:1], bias_ref.shape)
    down = lax.broadcasted_iota(jnp.int32, bias_ref.shape, 0)
    along = lax.broadcasted_iota(jnp.int32, bias_ref.shape, 1)
    allowed = (down % share == along % share) & (down != along) & (block <= jnp.transpose(block))
    bias_ref[...] = jnp.where(allowed, 0.0, MASKED)
    stores[3].start()
    normed = []
    for f in range(frames):
        normed.append(normalise(x_ref[f], own_ref[f + 3 : f + 4, :], own_ref[f : f + 1, :]))
    normed = jnp.concatenate(normed, axis=0)
    for n, (ref, w) in enumerate(((q_ref, wq_ref), (k_ref, wk_ref), (v_ref, wv_ref))):
        loads[1 + n].wait()
        ref[...] = matmul(normed, w[...]).astype(BF16)
    for d in range(RANKS):
        other = place_ref[1] ^ d
        r = pl.ds(pl.multiple_of((other // 2) * tokens, tokens), tokens)
        for u in range(SPAN):
            c = pl.ds(pl.multiple_of((other % 2) * SPAN * HEAD_DIM + u * HEAD_DIM, HEAD_DIM), HEAD_DIM)
            for n, ref in enumerate((k_ref, v_ref, q_ref)):
                block = slice((n * SPAN + u) * tokens, (n * SPAN + u + 1) * tokens)
                outs[d][block] = ref[r, c]
    for store in stores:
        store.wait()


def pass_kernel(in_ref, out_ref):
    out_ref[...] = in_ref[...]


def spatial_kernel(*refs):
    kvs, qs, outs = refs[: 2 * RANKS], refs[:RANKS], refs[2 * RANKS :]
    tokens = HEAD_DIM
    lane = lax.broadcasted_iota(jnp.int32, (tokens, HEAD_DIM), 1)
    stats = [jnp.zeros((tokens, HEAD_DIM), F32)] * RANKS
    for u in range(SPAN):
        r = slice(u * tokens, (u + 1) * tokens)
        block = slice((2 * SPAN + u) * tokens, (2 * SPAN + u + 1) * tokens)
        keys = jnp.concatenate([ref[u * tokens : (u + 1) * tokens] for ref in kvs], axis=0)
        vals = jnp.concatenate([ref[(SPAN + u) * tokens : (SPAN + u + 1) * tokens] for ref in kvs], axis=0)
        for s in range(0, RANKS, 2):
            q = jnp.concatenate([qs[s][block], qs[s + 1][block]], axis=0)
            mixed, logs = attend(q, keys, vals)
            mixed = mixed.astype(BF16)
            for d in range(2):
                half = slice(d * tokens, (d + 1) * tokens)
                outs[s + d][r] = mixed[half]
                for n, piece in enumerate(split3(logs[half])):
                    stats[s + d] = jnp.where(lane == SPAN * u + n, piece, stats[s + d])
    for d in range(RANKS):
        turned = jnp.transpose(stats[d])[0:STAT_ROWS]
        outs[d][SPAN * tokens : SPAN * tokens + STAT_ROWS] = turned.astype(BF16)


def temporal_kernel(x_ref, *refs):
    scale_hbm, shift_hbm, wq_hbm, wk_hbm, bias_hbm, wv_hbm, out_hbm = refs[:7]
    scale_ref, shift_ref, wq_ref, wk_ref, bias_ref, wv_ref, out_ref, sems, out_sems = refs[7:]
    held = (scale_ref, shift_ref, wq_ref, wk_ref, bias_ref, wv_ref)
    loads = []
    for n, (src, dst) in enumerate(zip(refs[:6], held)):
        loads.append(pltpu.make_async_copy(src, dst, sems.at[n]))
        loads[n].start()
    groups, rows, width = x_ref.shape
    low = lax.broadcasted_iota(jnp.int32, (groups, rows, width), 1) < rows // 2

    def spread(ref):
        first = jnp.broadcast_to(ref[:, 0:1, :], low.shape)
        return jnp.where(low, first, jnp.broadcast_to(ref[:, 1:2, :], low.shape))

    loads[0].wait()
    loads[1].wait()
    normed = normalise(x_ref[...].astype(F32), spread(scale_ref), spread(shift_ref))
    normed = normed.reshape(groups * rows, width)
    loads[2].wait()
    q = matmul(normed, wq_ref[...]).astype(BF16)
    loads[3].wait()
    k = matmul(normed, wk_ref[...]).astype(BF16)
    loads[4].wait()
    lane = lax.broadcasted_iota(jnp.int32, (groups * rows, HEAD_DIM), 1)
    stats = jnp.zeros((groups * rows, HEAD_DIM), F32)
    heads = [slice(h * HEAD_DIM, (h + 1) * HEAD_DIM) for h in range(HEADS)]
    parts = [softmax_parts(q[:, own], k[:, own], bias_ref[...]) for own in heads]
    loads[5].wait()
    v = matmul(normed, wv_ref[...]).astype(BF16)
    copies = []

    def send(n):
        c = pl.ds(n * HEAD_DIM, HEAD_DIM)
        copies.append(pltpu.make_async_copy(out_ref.at[:, c], out_hbm.at[:, c], out_sems.at[n]))
        copies[n].start()

    for h, (own, (weights, total, top)) in enumerate(zip(heads, parts)):
        mixed, logs = finish(weights, total, top, v[:, own], True)
        out_ref[:, own] = mixed.astype(BF16)
        send(h)
        for m, piece in enumerate(split3(logs)):
            stats = jnp.where(lane == 8 * m + h, piece, stats)
    out_ref[:, HEADS * HEAD_DIM :] = stats.astype(BF16)
    send(HEADS)
    for copy in copies:
        copy.wait()


def reorder_kernel(time_ref, wo_hbm, own_hbm, far_ref, logs_ref, wo_ref, own_ref, sems):
    loads = []
    for n, (src, dst) in enumerate(((wo_hbm, wo_ref), (own_hbm, own_ref))):
        loads.append(pltpu.make_async_copy(src, dst, sems.at[n]))
        loads[n].start()
    frames, tokens, inner = far_ref.shape
    width = time_ref.shape[1]
    turned = time_ref[...].astype(F32).reshape(tokens // 8, 2, 8, width)
    for f, rows in enumerate(swap_halves(turned[:, 0], turned[:, 1])):
        rows = rows.reshape(tokens, width)
        far_ref[f] = rows[:, :inner].astype(BF16)
        stats = rows[:, inner:]
        logs_ref[f, :, 0:8] = stats[:, 0:8] + stats[:, 8:16] + stats[:, 16:24]
    for load in loads:
        load.wait()


def merged(f, rank, near_refs, far_ref, logs_ref, space_ref, out_ref):
    for d, ref in enumerate(near_refs):
        space_ref[rank ^ d] = ref[...]
    tokens = out_ref.shape[0]
    time_log = logs_ref[f, :, 0:8]
    log_rows = []
    for h in range(HEADS):
        st = space_ref[2 * f + h // SPAN, SPAN * tokens : SPAN * tokens + STAT_ROWS].astype(F32)
        b = SPAN * (h % SPAN)
        log_rows.append(st[b : b + 1] + st[b + 1 : b + 2] + st[b + 2 : b + 3])
    log_rows.append(jnp.zeros((8 - HEADS, HEAD_DIM), F32))
    space_log = jnp.transpose(jnp.concatenate(log_rows, axis=0))
    of_space = 1.0 / (1.0 + jnp.exp2(time_log - space_log))
    of_time = 1.0 / (1.0 + jnp.exp2(space_log - time_log))
    for h in range(HEADS):
        own = slice(h * HEAD_DIM, (h + 1) * HEAD_DIM)
        u = h % SPAN
        near = space_ref[2 * f + h // SPAN, u * tokens : (u + 1) * tokens].astype(F32)
        far = far_ref[f, :, own].astype(F32)
        mixed = of_space[:, h : h + 1] * near + of_time[:, h : h + 1] * far
        out_ref[:, own] = mixed.astype(BF16)


def first_kernel(place_ref, mark_ref, *refs):
    del mark_ref
    near_refs, (far_ref, logs_ref, sent_ref, first_ref, space_ref) = refs[:RANKS], refs[RANKS:]
    merged(0, place_ref[1], near_refs, far_ref, logs_ref, space_ref, first_ref)
    sent_ref[...] = first_ref[...]


def project_kernel(place_ref, size_ref, *refs):
    near_refs = refs[:RANKS]
    far_ref, logs_ref, first_ref, wo_ref, own_ref, in_ref, x_hbm, fresh_hbm = refs[RANKS : RANKS + 8]
    vel_hbm, next_hbm, base_ref = refs[RANKS + 8 : RANKS + 11]
    space_ref, second_ref, x_ref, fresh_ref, vel_ref, next_ref, sems, vel_sems, next_sems = refs[RANKS + 11 :]
    frames, tokens, _ = x_ref.shape
    loads = []
    for n, (src, dst) in enumerate(
        (
            (x_hbm, x_ref),
            (fresh_hbm, fresh_ref),
        )
    ):
        loads.append(pltpu.make_async_copy(src, dst, sems.at[n]))
        loads[n].start()

    merged(1, place_ref[1], near_refs, far_ref, logs_ref, space_ref, second_ref)
    attended = jnp.concatenate([first_ref[...], second_ref[...]], axis=0)
    for load in loads:
        load.wait()

    base_ref[...] = jnp.where(place_ref[0] == place_ref[2], fresh_ref[...], in_ref[...])
    chunks = vel_sems.shape[0]
    width = vel_ref.shape[2] // chunks
    copies = []
    for n in range(chunks):
        c, d = slice(n * width, (n + 1) * width), pl.ds(n * width, width)
        projected = matmul(attended, wo_ref[:, c])
        for f in range(frames):
            moving = projected[f * tokens : (f + 1) * tokens] * own_ref[6 + f : 7 + f, c]
            vel_ref[f, :, c] = moving.astype(BF16)
            if f > 0:
                advanced = x_ref[f, :, c].astype(F32) + size_ref[f] * moving
                next_ref[f - 1, :, c] = advanced.astype(BF16)
        copies.append(pltpu.make_async_copy(vel_ref.at[:, :, d], vel_hbm.at[:, :, d], vel_sems.at[n]))
        copies[-1].start()
        filled = next_hbm.at[pl.ds(0, frames - 1), :, d]
        copies.append(pltpu.make_async_copy(next_ref.at[:, :, d], filled, next_sems.at[n]))
        copies[-1].start()
    for copy in copies:
        copy.wait()


def last_kernel(size_ref, att_ref, wo_ref, own_ref, base_ref, kept_ref, next_ref, out_ref, sems):
    del kept_ref
    slot = next_ref.shape[0] - 1
    chunks = sems.shape[0]
    width = out_ref.shape[1] // chunks
    copies = []
    for n in range(chunks):
        c, d = slice(n * width, (n + 1) * width), pl.ds(n * width, width)
        moving = matmul(att_ref[...], wo_ref[:, c]) * own_ref[8:9, c]
        out_ref[:, c] = (base_ref[:, c].astype(F32) + size_ref[2] * moving).astype(BF16)
        copies.append(pltpu.make_async_copy(out_ref.at[:, d], next_ref.at[slot, :, d], sems.at[n]))
        copies[n].start()
    for copy in copies:
        copy.wait()


def whole():
    return pl.BlockSpec(memory_space=pltpu.VMEM)


def scalar():
    return pl.BlockSpec(memory_space=pltpu.SMEM)


def anywhere():
    return pl.BlockSpec(memory_space=pl.ANY)


def pinned(x):
    return pltpu.with_memory_space_constraint(x, pltpu.VMEM)


def in_hbm(x):
    return pltpu.with_memory_space_constraint(x, pltpu.HBM)


def call(kernel, args, in_specs, outs, out_specs, flops=0, nbytes=0, vmem=20, **more):
    return pl.pallas_call(
        kernel,
        out_shape=outs,
        in_specs=in_specs,
        out_specs=out_specs,
        compiler_params=pltpu.CompilerParams(vmem_limit_bytes=vmem * MIB),
        cost_estimate=pl.CostEstimate(flops=flops, bytes_accessed=nbytes, transcendentals=0),
        **more,
    )(*args)


def body(
    latents,
    fresh_noise,
    noise_levels,
    offset,
    block_ids,
    mod_table,
    step_sizes,
    w_query,
    w_key,
    w_value,
    w_out,
):
    frames, tokens, width = latents.shape
    times = lax.axis_size("tm")
    ranks = lax.axis_size("tok")
    share = tokens // times
    total = frames * times
    inner = HEADS * HEAD_DIM
    sds = jax.ShapeDtypeStruct
    dma = pltpu.SemaphoreType.DMA
    back_perm = [(i, i - 1) for i in range(1, times)]
    project_flops = 2 * frames * tokens * width * inner

    def exchange(x, d):
        pairs = []
        for tm in range(times):
            for tok in range(ranks):
                side, y, core = tok // RANKS, tok % RANKS, tm % 2
                pairs.append((tm * ranks + tok, (tm - core + side) * ranks + core * RANKS + (y ^ d)))
        return lax.ppermute(x, ("tm", "tok"), pairs)

    outgoing, incoming, x = call(
        shuffle_kernel,
        (in_hbm(latents),),
        [anywhere()],
        (
            pltpu.HBM((tokens // 8, 2, 8, width), BF16),
            pltpu.HBM((tokens, width), BF16),
            pltpu.VMEM((frames, tokens, width), BF16),
        ),
        (anywhere(), anywhere(), whole()),
        nbytes=2 * MIB,
        scratch_shapes=[pltpu.VMEM((tokens // 8, 2, 8, width), BF16), dma((4,)), dma((4,)), dma],
    )
    column = lax.all_to_all(outgoing.reshape(times, frames * share, width), "tm", 0, 0)

    place = lax.axis_index("tm").astype(jnp.int32)
    rank = lax.axis_index("tok").astype(jnp.int32) % RANKS
    place = jnp.stack([place, rank, jnp.int32(times - 1)])
    table = mod_table.transpose(1, 0, 2)
    small = (
        pltpu.VMEM((16, width), F32),
        pltpu.VMEM((times, frames, width), F32),
        pltpu.VMEM((times, frames, width), F32),
        pltpu.VMEM((total * share, total * share), F32),
    )
    sizes, own, shifts, scales, bias, *parts = call(
        home_kernel,
        (
            noise_levels,
            offset,
            step_sizes,
            block_ids,
            place,
            pinned(x),
            *[in_hbm(a) for a in (table, w_query, w_key, w_value)],
        ),
        [scalar()] * 5 + [whole()] + [anywhere()] * 4,
        (
            sds((frames + 1,), F32),
            *[pltpu.HBM(a.inner_aval.shape, F32) for a in small],
            *[sds((3 * SPAN * tokens, HEAD_DIM), BF16)] * RANKS,
        ),
        (scalar(), *[anywhere()] * 4, *[whole()] * RANKS),
        flops=LONG,
        nbytes=10 * MIB,
        scratch_shapes=[
            pltpu.VMEM(table.shape, F32),
            *[pltpu.VMEM((frames * tokens, inner), BF16)] * 3,
            *[pltpu.VMEM((width, inner), BF16)] * 3,
            *small,
            dma((4,)),
            dma((4,)),
        ],
    )
    units = [exchange(part, d) for d, part in enumerate(parts)]

    incoming, sizes = lax.optimization_barrier((incoming, sizes))
    next_latents = lax.ppermute(incoming, "tm", back_perm)

    back = call(
        temporal_kernel,
        (column, *[in_hbm(a) for a in (scales, shifts, w_query, w_key, bias, w_value)]),
        [whole()] + [anywhere()] * 6,
        pltpu.HBM((total * share, inner + HEAD_DIM), BF16),
        anywhere(),
        flops=LONG,
        nbytes=10 * MIB,
        scratch_shapes=[
            *small[1:3],
            *[pltpu.VMEM((width, inner), BF16)] * 2,
            small[3],
            pltpu.VMEM((width, inner), BF16),
            pltpu.VMEM((total * share, inner + HEAD_DIM), BF16),
            dma((6,)),
            dma((HEADS + 1,)),
        ],
    )
    mark = step_sizes.reshape(1, -1)
    _, next_latents, mark, *units = lax.optimization_barrier((back, next_latents, mark, *units))
    mark = call(pass_kernel, (mark,), [whole()], sds(mark.shape, F32), whole(), flops=PAUSE)
    mark, *units = lax.optimization_barrier((mark, *units))
    sibling = [lax.ppermute(part, "tm", [(i, i ^ 1) for i in range(times)]) for part in units]
    back = lax.all_to_all(back.reshape(times, frames * share, inner + HEAD_DIM), "tm", 0, 0)
    back = back.reshape(times * frames * share, inner + HEAD_DIM)

    near = call(
        spatial_kernel,
        (*units, *sibling),
        [whole()] * (2 * RANKS),
        [sds((SPAN * tokens + STAT_ROWS, HEAD_DIM), BF16)] * RANKS,
        [whole()] * RANKS,
        flops=4 * SPAN * RANKS * ranks * tokens * tokens * HEAD_DIM,
        nbytes=3 * MIB,
    )
    near = [exchange(part, d) for d, part in enumerate(near)]

    space = pltpu.VMEM((RANKS, SPAN * tokens + STAT_ROWS, HEAD_DIM), BF16)
    far, logs, wo, own = call(
        reorder_kernel,
        (back, in_hbm(w_out), in_hbm(own)),
        [whole()] + [anywhere()] * 2,
        (
            pltpu.VMEM((frames, tokens, inner), BF16),
            pltpu.VMEM((frames, tokens, HEAD_DIM), F32),
            pltpu.VMEM((inner, width), BF16),
            pltpu.VMEM((16, width), F32),
        ),
        (whole(),) * 4,
        scratch_shapes=[dma((2,))],
        flops=LONG,
        nbytes=MIB,
    )
    sent, first = call(
        first_kernel,
        (place, mark, *near, pinned(far), pinned(logs)),
        [scalar()] + [whole()] * (RANKS + 3),
        (sds((tokens, inner), BF16), pltpu.VMEM((tokens, inner), BF16)),
        (whole(), whole()),
        nbytes=2 * MIB,
        scratch_shapes=[space],
    )
    next_first = lax.ppermute(sent, "tm", back_perm)
    velocity, following, base = call(
        project_kernel,
        (
            place,
            sizes,
            *near,
            pinned(far),
            pinned(logs),
            pinned(first),
            pinned(wo),
            pinned(own),
            next_latents,
            in_hbm(latents),
            in_hbm(fresh_noise),
        ),
        [scalar()] * 2 + [whole()] * (RANKS + 6) + [anywhere()] * 2,
        (
            pltpu.HBM((frames, tokens, width), BF16),
            pltpu.HBM((frames, tokens, width), BF16),
            pltpu.VMEM((tokens, width), BF16),
        ),
        (anywhere(), anywhere(), whole()),
        flops=project_flops,
        nbytes=6 * MIB,
        scratch_shapes=[
            space,
            pltpu.VMEM((tokens, inner), BF16),
            pltpu.VMEM((frames, tokens, width), BF16),
            pltpu.VMEM((tokens, width), BF16),
            pltpu.VMEM((frames, tokens, width), BF16),
            pltpu.VMEM((frames - 1, tokens, width), BF16),
            dma((2,)),
            *[dma((3,))] * 2,
        ],
    )
    following = call(
        last_kernel,
        (sizes, next_first, pinned(wo), pinned(own), pinned(base), following),
        [scalar()] + [whole()] * 4 + [anywhere()],
        sds((frames, tokens, width), BF16),
        anywhere(),
        flops=project_flops // 2,
        nbytes=4 * MIB,
        scratch_shapes=[pltpu.VMEM((tokens, width), BF16), dma((3,))],
        input_output_aliases={5: 0},
    )
    return velocity, following


def solution(mesh):
    in_specs = (P("tm", "tok", None), P("tok", None), P(), P(), P(), P(), P(), P(), P(), P(), P())
    out_specs = (P("tm", "tok", None), P("tm", "tok", None))
    return jax.shard_map(body, mesh=mesh, in_specs=in_specs, out_specs=out_specs, check_vma=False)
```

```python
import math

import jax
import jax.numpy as jnp
from jax import lax
from jax.experimental import pallas as pl
from jax.experimental.pallas import tpu as pltpu
from jax.sharding import PartitionSpec as P

HEAD_DIM = 128
HEADS = 6
SPAN = 3
RANKS = 4
BASE2 = HEAD_DIM ** (-0.5) * math.log2(math.e)
MASKED = -1e30
FLOOR = -1e29
MIB = 1 << 20
STAT_ROWS = 16
PAUSE = 3_500_000_000
LONG = 60_000_000_000
BF16 = jnp.bfloat16
F32 = jnp.float32


def normalise(x, scale1, shift):
    values = x.astype(F32)
    center = jnp.mean(values, axis=-1, keepdims=True)
    values = values - center
    spread = jnp.mean(values * values, axis=-1, keepdims=True)
    return (values * lax.rsqrt(spread + 1e-06) * scale1 + shift).astype(BF16)


def matmul(a, b):
    return jnp.dot(a, b, preferred_element_type=F32)


def softmax_parts(q, k, bias=None):
    scores = lax.dot_general(q, k, (((1,), (1,)), ((), ())), preferred_element_type=F32)
    if bias is not None:
        scores = scores + bias
    top = jnp.max(scores, axis=-1, keepdims=True)
    if bias is not None:
        top = jnp.maximum(top, FLOOR)
    weights = jnp.exp2((scores - top) * BASE2)
    return weights.astype(BF16), jnp.sum(weights, axis=-1, keepdims=True), top


def finish(weights, total, top, v, may_be_empty):
    mixed = matmul(weights, v)
    if not may_be_empty:
        return mixed * (1.0 / total), top * BASE2 + jnp.log2(total)
    some = total > 0.0
    safe = jnp.where(some, total, 1.0)
    return mixed * (1.0 / safe), jnp.where(some, top * BASE2 + jnp.log2(safe), MASKED)


def attend(q, k, v):
    return finish(*softmax_parts(q, k), v, False)


def split3(x):
    one = x.astype(BF16).astype(F32)
    rest = x - one
    two = rest.astype(BF16).astype(F32)
    return one, two, rest - two


def packed(tile, step):
    one, two, three = split3(tile)
    return one + pltpu.roll(two, step, 1) + pltpu.roll(three, 2 * step, 1)


def swap_halves(even, odd):
    low = lax.broadcasted_iota(jnp.int32, even.shape, 1) < 4
    return jnp.where(low, even, pltpu.roll(odd, 4, 1)), jnp.where(low, pltpu.roll(even, 4, 1), odd)


def shuffle_kernel(x_hbm, out_hbm, first_hbm, x_ref, mixed_ref, in_sems, out_sems, first_sem):
    _, tokens, width = x_ref.shape
    chunks = in_sems.shape[0]
    rows = tokens // chunks
    pairs = rows // 8
    ins, outs = [], []
    for c in range(chunks):
        r = pl.ds(c * rows, rows)
        ins.append(pltpu.make_async_copy(x_hbm.at[:, r], x_ref.at[:, r], in_sems.at[c]))
        ins[c].start()
    for c in range(chunks):
        ins[c].wait()
        first, second = [
            x_ref[f, c * rows : (c + 1) * rows].astype(F32).reshape(pairs, 8, width) for f in range(2)
        ]
        even, odd = swap_halves(first, second)
        mixed_ref[c * pairs : (c + 1) * pairs, 0] = even.astype(BF16)
        mixed_ref[c * pairs : (c + 1) * pairs, 1] = odd.astype(BF16)
        r = pl.ds(c * pairs, pairs)
        outs.append(pltpu.make_async_copy(mixed_ref.at[r], out_hbm.at[r], out_sems.at[c]))
        outs[c].start()
    outs.append(pltpu.make_async_copy(x_ref.at[0], first_hbm, first_sem))
    outs[-1].start()
    for copy in outs:
        copy.wait()


def home_kernel(
    noise_ref,
    offset_ref,
    step_ref,
    blocks_ref,
    place_ref,
    x_ref,
    table_hbm,
    wq_hbm,
    wk_hbm,
    wv_hbm,
    size_ref,
    own_hbm,
    shift_hbm,
    scale_hbm,
    bias_hbm,
    *refs,
):
    outs = refs[:RANKS]
    table_ref, q_ref, k_ref, v_ref, wq_ref, wk_ref, wv_ref, *refs = refs[RANKS:]
    own_ref, shift_ref, scale_ref, bias_ref, sems, store_sems = refs
    loads = []
    for n, (src, dst) in enumerate(
        ((table_hbm, table_ref), (wq_hbm, wq_ref), (wk_hbm, wk_ref), (wv_hbm, wv_ref))
    ):
        loads.append(pltpu.make_async_copy(src, dst, sems.at[n]))
        loads[n].start()
    frames, tokens, _ = x_ref.shape
    total = noise_ref.shape[0]
    loads[0].wait()
    for n in range(frames + 1):
        frame = jnp.minimum(place_ref[0] * frames + n, total - 1)
        level = noise_ref[lax.rem(frame + offset_ref[0], total)]
        size_ref[n] = step_ref[level]
        own_ref[n : n + 1, :] = table_ref[0, pl.ds(level, 1), :]
        own_ref[n + 3 : n + 4, :] = table_ref[1, pl.ds(level, 1), :] + 1.0
        own_ref[n + 6 : n + 7, :] = table_ref[2, pl.ds(level, 1), :]
    stores = [
        pltpu.make_async_copy(src, dst, store_sems.at[n])
        for n, (src, dst) in enumerate(
            ((own_ref, own_hbm), (shift_ref, shift_hbm), (scale_ref, scale_hbm), (bias_ref, bias_hbm))
        )
    ]
    stores[0].start()
    share = bias_ref.shape[0] // total
    for f in range(total):
        level = noise_ref[lax.rem(f + offset_ref[0], total)]
        shift_ref[f // frames, f % frames : f % frames + 1, :] = table_ref[0, pl.ds(level, 1), :]
        scale_ref[f // frames, f % frames : f % frames + 1, :] = table_ref[1, pl.ds(level, 1), :] + 1.0
    stores[1].start()
    stores[2].start()
    wide = (8, total * share)
    lane = lax.broadcasted_iota(jnp.int32, wide, 1) // share
    block = jnp.zeros(wide, F32)
    for f in range(total):
        block = jnp.where(lane == f, blocks_ref[f].astype(F32), block)
    block = jnp.broadcast_to(block[0:1], bias_ref.shape)
    down = lax.broadcasted_iota(jnp.int32, bias_ref.shape, 0)
    along = lax.broadcasted_iota(jnp.int32, bias_ref.shape, 1)
    allowed = (down % share == along % share) & (down != along) & (block <= jnp.transpose(block))
    bias_ref[...] = jnp.where(allowed, 0.0, MASKED)
    stores[3].start()
    normed = []
    for f in range(frames):
        normed.append(normalise(x_ref[f], own_ref[f + 3 : f + 4, :], own_ref[f : f + 1, :]))
    normed = jnp.concatenate(normed, axis=0)
    for n, (ref, w) in enumerate(((q_ref, wq_ref), (k_ref, wk_ref), (v_ref, wv_ref))):
        loads[1 + n].wait()
        ref[...] = matmul(normed, w[...]).astype(BF16)
    for d in range(RANKS):
        other = place_ref[1] ^ d
        r = pl.ds(pl.multiple_of((other // 2) * tokens, tokens), tokens)
        for u in range(SPAN):
            c = pl.ds(pl.multiple_of((other % 2) * SPAN * HEAD_DIM + u * HEAD_DIM, HEAD_DIM), HEAD_DIM)
            for n, ref in enumerate((k_ref, v_ref, q_ref)):
                block = slice((n * SPAN + u) * tokens, (n * SPAN + u + 1) * tokens)
                outs[d][block] = ref[r, c]
    for store in stores:
        store.wait()


def pass_kernel(in_ref, out_ref):
    out_ref[...] = in_ref[...]


def spatial_kernel(*refs):
    kvs, qs, outs = refs[: 2 * RANKS], refs[:RANKS], refs[2 * RANKS :]
    tokens = HEAD_DIM
    lane = lax.broadcasted_iota(jnp.int32, (tokens, HEAD_DIM), 1)
    stats = [jnp.zeros((tokens, HEAD_DIM), F32)] * RANKS
    for u in range(SPAN):
        r = slice(u * tokens, (u + 1) * tokens)
        block = slice((2 * SPAN + u) * tokens, (2 * SPAN + u + 1) * tokens)
        keys = jnp.concatenate([ref[u * tokens : (u + 1) * tokens] for ref in kvs], axis=0)
        vals = jnp.concatenate([ref[(SPAN + u) * tokens : (SPAN + u + 1) * tokens] for ref in kvs], axis=0)
        for s in range(0, RANKS, 2):
            q = jnp.concatenate([qs[s][block], qs[s + 1][block]], axis=0)
            mixed, logs = attend(q, keys, vals)
            mixed = mixed.astype(BF16)
            for d in range(2):
                half = slice(d * tokens, (d + 1) * tokens)
                outs[s + d][r] = mixed[half]
                stats[s + d] = jnp.where(lane == u, logs[half], stats[s + d])
    for d in range(RANKS):
        turned = jnp.transpose(packed(stats[d], 4))[0:STAT_ROWS]
        outs[d][SPAN * tokens : SPAN * tokens + STAT_ROWS] = turned.astype(BF16)


def temporal_kernel(x_ref, *refs):
    scale_hbm, shift_hbm, wq_hbm, wk_hbm, bias_hbm, wv_hbm, out_hbm = refs[:7]
    scale_ref, shift_ref, wq_ref, wk_ref, bias_ref, wv_ref, out_ref, sems, out_sems = refs[7:]
    held = (scale_ref, shift_ref, wq_ref, wk_ref, bias_ref, wv_ref)
    loads = []
    for n, (src, dst) in enumerate(zip(refs[:6], held)):
        loads.append(pltpu.make_async_copy(src, dst, sems.at[n]))
        loads[n].start()
    groups, rows, width = x_ref.shape
    low = lax.broadcasted_iota(jnp.int32, (groups, rows, width), 1) < rows // 2

    def spread(ref):
        first = jnp.broadcast_to(ref[:, 0:1, :], low.shape)
        return jnp.where(low, first, jnp.broadcast_to(ref[:, 1:2, :], low.shape))

    loads[0].wait()
    loads[1].wait()
    normed = normalise(x_ref[...].astype(F32), spread(scale_ref), spread(shift_ref))
    normed = normed.reshape(groups * rows, width)
    loads[2].wait()
    q = matmul(normed, wq_ref[...]).astype(BF16)
    loads[3].wait()
    k = matmul(normed, wk_ref[...]).astype(BF16)
    loads[4].wait()
    lane = lax.broadcasted_iota(jnp.int32, (groups * rows, HEAD_DIM), 1)
    stats = jnp.zeros((groups * rows, HEAD_DIM), F32)
    heads = [slice(h * HEAD_DIM, (h + 1) * HEAD_DIM) for h in range(HEADS)]
    parts = [softmax_parts(q[:, own], k[:, own], bias_ref[...]) for own in heads]
    loads[5].wait()
    v = matmul(normed, wv_ref[...]).astype(BF16)
    copies = []

    def send(n):
        c = pl.ds(n * HEAD_DIM, HEAD_DIM)
        copies.append(pltpu.make_async_copy(out_ref.at[:, c], out_hbm.at[:, c], out_sems.at[n]))
        copies[n].start()

    for h, (own, (weights, total, top)) in enumerate(zip(heads, parts)):
        mixed, logs = finish(weights, total, top, v[:, own], True)
        out_ref[:, own] = mixed.astype(BF16)
        send(h)
        stats = jnp.where(lane == h, logs, stats)
    out_ref[:, HEADS * HEAD_DIM :] = packed(stats, 8).astype(BF16)
    send(HEADS)
    for copy in copies:
        copy.wait()


def reorder_kernel(time_ref, wo_hbm, own_hbm, far_ref, logs_ref, wo_ref, own_ref, sems):
    loads = []
    for n, (src, dst) in enumerate(((wo_hbm, wo_ref), (own_hbm, own_ref))):
        loads.append(pltpu.make_async_copy(src, dst, sems.at[n]))
        loads[n].start()
    frames, tokens, inner = far_ref.shape
    width = time_ref.shape[1]
    turned = time_ref[...].astype(F32).reshape(tokens // 8, 2, 8, width)
    for f, rows in enumerate(swap_halves(turned[:, 0], turned[:, 1])):
        rows = rows.reshape(tokens, width)
        far_ref[f] = rows[:, :inner].astype(BF16)
        stats = rows[:, inner:]
        logs_ref[f, :, 0:8] = stats[:, 0:8] + stats[:, 8:16] + stats[:, 16:24]
    for load in loads:
        load.wait()


def merged(f, rank, near_refs, far_ref, logs_ref, space_ref, out_ref):
    for d, ref in enumerate(near_refs):
        space_ref[rank ^ d] = ref[...]
    tokens = out_ref.shape[0]
    time_log = logs_ref[f, :, 0:8]
    log_rows = []
    for h in range(HEADS):
        st = space_ref[2 * f + h // SPAN, SPAN * tokens : SPAN * tokens + STAT_ROWS].astype(F32)
        b = h % SPAN
        log_rows.append(st[b : b + 1] + st[b + 4 : b + 5] + st[b + 8 : b + 9])
    log_rows.append(jnp.zeros((8 - HEADS, HEAD_DIM), F32))
    space_log = jnp.transpose(jnp.concatenate(log_rows, axis=0))
    of_space = 1.0 / (1.0 + jnp.exp2(time_log - space_log))
    of_time = 1.0 / (1.0 + jnp.exp2(space_log - time_log))
    for h in range(HEADS):
        own = slice(h * HEAD_DIM, (h + 1) * HEAD_DIM)
        u = h % SPAN
        near = space_ref[2 * f + h // SPAN, u * tokens : (u + 1) * tokens].astype(F32)
        far = far_ref[f, :, own].astype(F32)
        mixed = of_space[:, h : h + 1] * near + of_time[:, h : h + 1] * far
        out_ref[:, own] = mixed.astype(BF16)


def first_kernel(place_ref, mark_ref, *refs):
    del mark_ref
    near_refs, (far_ref, logs_ref, sent_ref, first_ref, space_ref) = refs[:RANKS], refs[RANKS:]
    merged(0, place_ref[1], near_refs, far_ref, logs_ref, space_ref, first_ref)
    sent_ref[...] = first_ref[...]


def project_kernel(place_ref, size_ref, *refs):
    near_refs = refs[:RANKS]
    far_ref, logs_ref, first_ref, wo_ref, own_ref, in_ref, x_hbm, fresh_hbm = refs[RANKS : RANKS + 8]
    vel_hbm, next_hbm, base_ref = refs[RANKS + 8 : RANKS + 11]
    space_ref, second_ref, x_ref, fresh_ref, vel_ref, next_ref, sems, vel_sems, next_sems = refs[RANKS + 11 :]
    frames, tokens, _ = x_ref.shape
    loads = []
    for n, (src, dst) in enumerate(
        (
            (x_hbm, x_ref),
            (fresh_hbm, fresh_ref),
        )
    ):
        loads.append(pltpu.make_async_copy(src, dst, sems.at[n]))
        loads[n].start()

    merged(1, place_ref[1], near_refs, far_ref, logs_ref, space_ref, second_ref)
    attended = jnp.concatenate([first_ref[...], second_ref[...]], axis=0)
    for load in loads:
        load.wait()

    base_ref[...] = jnp.where(place_ref[0] == place_ref[2], fresh_ref[...], in_ref[...])
    chunks = vel_sems.shape[0]
    width = vel_ref.shape[2] // chunks
    copies = []
    for n in range(chunks):
        c, d = slice(n * width, (n + 1) * width), pl.ds(n * width, width)
        projected = matmul(attended, wo_ref[:, c])
        for f in range(frames):
            moving = projected[f * tokens : (f + 1) * tokens] * own_ref[6 + f : 7 + f, c]
            vel_ref[f, :, c] = moving.astype(BF16)
            if f > 0:
                advanced = x_ref[f, :, c].astype(F32) + size_ref[f] * moving
                next_ref[f - 1, :, c] = advanced.astype(BF16)
        copies.append(pltpu.make_async_copy(vel_ref.at[:, :, d], vel_hbm.at[:, :, d], vel_sems.at[n]))
        copies[-1].start()
        filled = next_hbm.at[pl.ds(0, frames - 1), :, d]
        copies.append(pltpu.make_async_copy(next_ref.at[:, :, d], filled, next_sems.at[n]))
        copies[-1].start()
    for copy in copies:
        copy.wait()


def last_kernel(size_ref, att_ref, wo_ref, own_ref, base_ref, kept_ref, next_ref, out_ref, sems):
    del kept_ref
    slot = next_ref.shape[0] - 1
    chunks = sems.shape[0]
    width = out_ref.shape[1] // chunks
    copies = []
    for n in range(chunks):
        c, d = slice(n * width, (n + 1) * width), pl.ds(n * width, width)
        moving = matmul(att_ref[...], wo_ref[:, c]) * own_ref[8:9, c]
        out_ref[:, c] = (base_ref[:, c].astype(F32) + size_ref[2] * moving).astype(BF16)
        copies.append(pltpu.make_async_copy(out_ref.at[:, d], next_ref.at[slot, :, d], sems.at[n]))
        copies[n].start()
    for copy in copies:
        copy.wait()


def whole():
    return pl.BlockSpec(memory_space=pltpu.VMEM)


def scalar():
    return pl.BlockSpec(memory_space=pltpu.SMEM)


def anywhere():
    return pl.BlockSpec(memory_space=pl.ANY)


def pinned(x):
    return pltpu.with_memory_space_constraint(x, pltpu.VMEM)


def in_hbm(x):
    return pltpu.with_memory_space_constraint(x, pltpu.HBM)


def call(kernel, args, in_specs, outs, out_specs, flops=0, nbytes=0, vmem=20, **more):
    return pl.pallas_call(
        kernel,
        out_shape=outs,
        in_specs=in_specs,
        out_specs=out_specs,
        compiler_params=pltpu.CompilerParams(vmem_limit_bytes=vmem * MIB),
        cost_estimate=pl.CostEstimate(flops=flops, bytes_accessed=nbytes, transcendentals=0),
        **more,
    )(*args)


def body(
    latents,
    fresh_noise,
    noise_levels,
    offset,
    block_ids,
    mod_table,
    step_sizes,
    w_query,
    w_key,
    w_value,
    w_out,
):
    frames, tokens, width = latents.shape
    times = lax.axis_size("tm")
    ranks = lax.axis_size("tok")
    share = tokens // times
    total = frames * times
    inner = HEADS * HEAD_DIM
    sds = jax.ShapeDtypeStruct
    dma = pltpu.SemaphoreType.DMA
    back_perm = [(i, i - 1) for i in range(1, times)]
    project_flops = 2 * frames * tokens * width * inner

    def exchange(x, d):
        pairs = []
        for tm in range(times):
            for tok in range(ranks):
                side, y, core = tok // RANKS, tok % RANKS, tm % 2
                pairs.append((tm * ranks + tok, (tm - core + side) * ranks + core * RANKS + (y ^ d)))
        return lax.ppermute(x, ("tm", "tok"), pairs)

    outgoing, incoming, x = call(
        shuffle_kernel,
        (in_hbm(latents),),
        [anywhere()],
        (
            pltpu.HBM((tokens // 8, 2, 8, width), BF16),
            pltpu.HBM((tokens, width), BF16),
            pltpu.VMEM((frames, tokens, width), BF16),
        ),
        (anywhere(), anywhere(), whole()),
        nbytes=2 * MIB,
        scratch_shapes=[pltpu.VMEM((tokens // 8, 2, 8, width), BF16), dma((4,)), dma((4,)), dma],
    )
    column = lax.all_to_all(outgoing.reshape(times, frames * share, width), "tm", 0, 0)

    place = lax.axis_index("tm").astype(jnp.int32)
    rank = lax.axis_index("tok").astype(jnp.int32) % RANKS
    place = jnp.stack([place, rank, jnp.int32(times - 1)])
    table = mod_table.transpose(1, 0, 2)
    small = (
        pltpu.VMEM((16, width), F32),
        pltpu.VMEM((times, frames, width), F32),
        pltpu.VMEM((times, frames, width), F32),
        pltpu.VMEM((total * share, total * share), F32),
    )
    sizes, own, shifts, scales, bias, *parts = call(
        home_kernel,
        (
            noise_levels,
            offset,
            step_sizes,
            block_ids,
            place,
            pinned(x),
            *[in_hbm(a) for a in (table, w_query, w_key, w_value)],
        ),
        [scalar()] * 5 + [whole()] + [anywhere()] * 4,
        (
            sds((frames + 1,), F32),
            *[pltpu.HBM(a.inner_aval.shape, F32) for a in small],
            *[sds((3 * SPAN * tokens, HEAD_DIM), BF16)] * RANKS,
        ),
        (scalar(), *[anywhere()] * 4, *[whole()] * RANKS),
        flops=LONG,
        nbytes=10 * MIB,
        scratch_shapes=[
            pltpu.VMEM(table.shape, F32),
            *[pltpu.VMEM((frames * tokens, inner), BF16)] * 3,
            *[pltpu.VMEM((width, inner), BF16)] * 3,
            *small,
            dma((4,)),
            dma((4,)),
        ],
    )
    units = [exchange(part, d) for d, part in enumerate(parts)]

    incoming, sizes = lax.optimization_barrier((incoming, sizes))
    next_latents = lax.ppermute(incoming, "tm", back_perm)

    back = call(
        temporal_kernel,
        (column, *[in_hbm(a) for a in (scales, shifts, w_query, w_key, bias, w_value)]),
        [whole()] + [anywhere()] * 6,
        pltpu.HBM((total * share, inner + HEAD_DIM), BF16),
        anywhere(),
        flops=LONG,
        nbytes=10 * MIB,
        scratch_shapes=[
            *small[1:3],
            *[pltpu.VMEM((width, inner), BF16)] * 2,
            small[3],
            pltpu.VMEM((width, inner), BF16),
            pltpu.VMEM((total * share, inner + HEAD_DIM), BF16),
            dma((6,)),
            dma((HEADS + 1,)),
        ],
    )
    mark = step_sizes.reshape(1, -1)
    _, next_latents, mark, *units = lax.optimization_barrier((back, next_latents, mark, *units))
    mark = call(pass_kernel, (mark,), [whole()], sds(mark.shape, F32), whole(), flops=PAUSE)
    mark, *units = lax.optimization_barrier((mark, *units))
    sibling = [lax.ppermute(part, "tm", [(i, i ^ 1) for i in range(times)]) for part in units]
    back = lax.all_to_all(back.reshape(times, frames * share, inner + HEAD_DIM), "tm", 0, 0)
    back = back.reshape(times * frames * share, inner + HEAD_DIM)

    near = call(
        spatial_kernel,
        (*units, *sibling),
        [whole()] * (2 * RANKS),
        [sds((SPAN * tokens + STAT_ROWS, HEAD_DIM), BF16)] * RANKS,
        [whole()] * RANKS,
        flops=4 * SPAN * RANKS * ranks * tokens * tokens * HEAD_DIM,
        nbytes=3 * MIB,
    )
    near = [exchange(part, d) for d, part in enumerate(near)]

    space = pltpu.VMEM((RANKS, SPAN * tokens + STAT_ROWS, HEAD_DIM), BF16)
    far, logs, wo, own = call(
        reorder_kernel,
        (back, in_hbm(w_out), in_hbm(own)),
        [whole()] + [anywhere()] * 2,
        (
            pltpu.VMEM((frames, tokens, inner), BF16),
            pltpu.VMEM((frames, tokens, HEAD_DIM), F32),
            pltpu.VMEM((inner, width), BF16),
            pltpu.VMEM((16, width), F32),
        ),
        (whole(),) * 4,
        scratch_shapes=[dma((2,))],
        flops=LONG,
        nbytes=MIB,
    )
    sent, first = call(
        first_kernel,
        (place, mark, *near, pinned(far), pinned(logs)),
        [scalar()] + [whole()] * (RANKS + 3),
        (sds((tokens, inner), BF16), pltpu.VMEM((tokens, inner), BF16)),
        (whole(), whole()),
        nbytes=2 * MIB,
        scratch_shapes=[space],
    )
    next_first = lax.ppermute(sent, "tm", back_perm)
    velocity, following, base = call(
        project_kernel,
        (
            place,
            sizes,
            *near,
            pinned(far),
            pinned(logs),
            pinned(first),
            pinned(wo),
            pinned(own),
            next_latents,
            in_hbm(latents),
            in_hbm(fresh_noise),
        ),
        [scalar()] * 2 + [whole()] * (RANKS + 6) + [anywhere()] * 2,
        (
            pltpu.HBM((frames, tokens, width), BF16),
            pltpu.HBM((frames, tokens, width), BF16),
            pltpu.VMEM((tokens, width), BF16),
        ),
        (anywhere(), anywhere(), whole()),
        flops=project_flops,
        nbytes=6 * MIB,
        scratch_shapes=[
            space,
            pltpu.VMEM((tokens, inner), BF16),
            pltpu.VMEM((frames, tokens, width), BF16),
            pltpu.VMEM((tokens, width), BF16),
            pltpu.VMEM((frames, tokens, width), BF16),
            pltpu.VMEM((frames - 1, tokens, width), BF16),
            dma((2,)),
            *[dma((3,))] * 2,
        ],
    )
    following = call(
        last_kernel,
        (sizes, next_first, pinned(wo), pinned(own), pinned(base), following),
        [scalar()] + [whole()] * 4 + [anywhere()],
        sds((frames, tokens, width), BF16),
        anywhere(),
        flops=project_flops // 2,
        nbytes=4 * MIB,
        scratch_shapes=[pltpu.VMEM((tokens, width), BF16), dma((3,))],
        input_output_aliases={5: 0},
    )
    return velocity, following


def solution(mesh):
    in_specs = (P("tm", "tok", None), P("tok", None), P(), P(), P(), P(), P(), P(), P(), P(), P())
    out_specs = (P("tm", "tok", None), P("tm", "tok", None))
    return jax.shard_map(body, mesh=mesh, in_specs=in_specs, out_specs=out_specs, check_vma=False)
```

```python
import math

import jax
import jax.numpy as jnp
from jax import lax
from jax.experimental import pallas as pl
from jax.experimental.pallas import tpu as pltpu
from jax.sharding import PartitionSpec as P

HEAD_DIM = 128
HEADS = 6
SPAN = 3
RANKS = 4
BASE2 = HEAD_DIM ** (-0.5) * math.log2(math.e)
MASKED = -1e30
FLOOR = -1e29
MIB = 1 << 20
STAT_ROWS = 16
PAUSE = 3_500_000_000
LONG = 60_000_000_000
BF16 = jnp.bfloat16
F32 = jnp.float32


def normalise(x, scale1, shift):
    values = x.astype(F32)
    center = jnp.mean(values, axis=-1, keepdims=True)
    values = values - center
    spread = jnp.mean(values * values, axis=-1, keepdims=True)
    return (values * lax.rsqrt(spread + 1e-06) * scale1 + shift).astype(BF16)


def matmul(a, b):
    return jnp.dot(a, b, preferred_element_type=F32)


def softmax_parts(q, k, bias=None):
    scores = lax.dot_general(q, k, (((1,), (1,)), ((), ())), preferred_element_type=F32)
    if bias is not None:
        scores = scores + bias
    top = jnp.max(scores, axis=-1, keepdims=True)
    if bias is not None:
        top = jnp.maximum(top, FLOOR)
    weights = jnp.exp2((scores - top) * BASE2)
    return weights.astype(BF16), jnp.sum(weights, axis=-1, keepdims=True), top


def finish(weights, total, top, v, may_be_empty):
    mixed = matmul(weights, v)
    if not may_be_empty:
        return mixed * (1.0 / total), top * BASE2 + jnp.log2(total)
    some = total > 0.0
    safe = jnp.where(some, total, 1.0)
    return mixed * (1.0 / safe), jnp.where(some, top * BASE2 + jnp.log2(safe), MASKED)


def attend(q, k, v):
    return finish(*softmax_parts(q, k), v, False)


def split3(x):
    one = x.astype(BF16).astype(F32)
    rest = x - one
    two = rest.astype(BF16).astype(F32)
    return one, two, rest - two


def packed(tile, step):
    one, two, three = split3(tile)
    return one + pltpu.roll(two, step, 1) + pltpu.roll(three, 2 * step, 1)


def swap_halves(even, odd):
    low = lax.broadcasted_iota(jnp.int32, even.shape, 1) < 4
    return jnp.where(low, even, pltpu.roll(odd, 4, 1)), jnp.where(low, pltpu.roll(even, 4, 1), odd)


def shuffle_kernel(x_hbm, out_hbm, first_hbm, x_ref, mixed_ref, in_sems, out_sems, first_sem):
    _, tokens, width = x_ref.shape
    chunks = in_sems.shape[0]
    rows = tokens // chunks
    pairs = rows // 8
    ins, outs = [], []
    for c in range(chunks):
        r = pl.ds(c * rows, rows)
        ins.append(pltpu.make_async_copy(x_hbm.at[:, r], x_ref.at[:, r], in_sems.at[c]))
        ins[c].start()
    for c in range(chunks):
        ins[c].wait()
        first, second = [
            x_ref[f, c * rows : (c + 1) * rows].astype(F32).reshape(pairs, 8, width) for f in range(2)
        ]
        even, odd = swap_halves(first, second)
        mixed_ref[c * pairs : (c + 1) * pairs, 0] = even.astype(BF16)
        mixed_ref[c * pairs : (c + 1) * pairs, 1] = odd.astype(BF16)
        r = pl.ds(c * pairs, pairs)
        outs.append(pltpu.make_async_copy(mixed_ref.at[r], out_hbm.at[r], out_sems.at[c]))
        outs[c].start()
    outs.append(pltpu.make_async_copy(x_ref.at[0], first_hbm, first_sem))
    outs[-1].start()
    for copy in outs:
        copy.wait()


def home_kernel(
    noise_ref,
    offset_ref,
    step_ref,
    blocks_ref,
    place_ref,
    x_ref,
    table_hbm,
    wq_hbm,
    wk_hbm,
    wv_hbm,
    size_ref,
    own_hbm,
    shift_hbm,
    scale_hbm,
    bias_hbm,
    *refs,
):
    outs = refs[:RANKS]
    table_ref, q_ref, k_ref, v_ref, wq_ref, wk_ref, wv_ref, *refs = refs[RANKS:]
    own_ref, shift_ref, scale_ref, bias_ref, sems, store_sems = refs
    loads = []
    for n, (src, dst) in enumerate(
        ((table_hbm, table_ref), (wq_hbm, wq_ref), (wk_hbm, wk_ref), (wv_hbm, wv_ref))
    ):
        loads.append(pltpu.make_async_copy(src, dst, sems.at[n]))
        loads[n].start()
    frames, tokens, _ = x_ref.shape
    total = noise_ref.shape[0]
    loads[0].wait()
    for n in range(frames + 1):
        frame = jnp.minimum(place_ref[0] * frames + n, total - 1)
        level = noise_ref[lax.rem(frame + offset_ref[0], total)]
        size_ref[n] = step_ref[level]
        own_ref[n : n + 1, :] = table_ref[0, pl.ds(level, 1), :]
        own_ref[n + 3 : n + 4, :] = table_ref[1, pl.ds(level, 1), :] + 1.0
        own_ref[n + 6 : n + 7, :] = table_ref[2, pl.ds(level, 1), :]
    stores = [
        pltpu.make_async_copy(src, dst, store_sems.at[n])
        for n, (src, dst) in enumerate(
            ((own_ref, own_hbm), (shift_ref, shift_hbm), (scale_ref, scale_hbm), (bias_ref, bias_hbm))
        )
    ]
    stores[0].start()
    share = bias_ref.shape[0] // total
    for f in range(total):
        level = noise_ref[lax.rem(f + offset_ref[0], total)]
        shift_ref[f // frames, f % frames : f % frames + 1, :] = table_ref[0, pl.ds(level, 1), :]
        scale_ref[f // frames, f % frames : f % frames + 1, :] = table_ref[1, pl.ds(level, 1), :] + 1.0
    stores[1].start()
    stores[2].start()
    wide = (8, total * share)
    lane = lax.broadcasted_iota(jnp.int32, wide, 1) // share
    block = jnp.zeros(wide, F32)
    for f in range(total):
        block = jnp.where(lane == f, blocks_ref[f].astype(F32), block)
    block = jnp.broadcast_to(block[0:1], bias_ref.shape)
    down = lax.broadcasted_iota(jnp.int32, bias_ref.shape, 0)
    along = lax.broadcasted_iota(jnp.int32, bias_ref.shape, 1)
    allowed = (down % share == along % share) & (down != along) & (block <= jnp.transpose(block))
    bias_ref[...] = jnp.where(allowed, 0.0, MASKED)
    stores[3].start()
    normed = []
    for f in range(frames):
        normed.append(normalise(x_ref[f], own_ref[f + 3 : f + 4, :], own_ref[f : f + 1, :]))
    normed = jnp.concatenate(normed, axis=0)
    for n, (ref, w) in enumerate(((q_ref, wq_ref), (k_ref, wk_ref), (v_ref, wv_ref))):
        loads[1 + n].wait()
        ref[...] = matmul(normed, w[...]).astype(BF16)
    for d in range(RANKS):
        other = place_ref[1] ^ d
        r = pl.ds(pl.multiple_of((other // 2) * tokens, tokens), tokens)
        for u in range(SPAN):
            c = pl.ds(pl.multiple_of((other % 2) * SPAN * HEAD_DIM + u * HEAD_DIM, HEAD_DIM), HEAD_DIM)
            for n, ref in enumerate((k_ref, v_ref, q_ref)):
                block = slice((n * SPAN + u) * tokens, (n * SPAN + u + 1) * tokens)
                outs[d][block] = ref[r, c]
    for store in stores:
        store.wait()


def pass_kernel(in_ref, out_ref):
    out_ref[...] = in_ref[...]


def spatial_kernel(*refs):
    kvs, qs, outs = refs[: 2 * RANKS], refs[:RANKS], refs[2 * RANKS :]
    tokens = HEAD_DIM
    lane = lax.broadcasted_iota(jnp.int32, (tokens, HEAD_DIM), 1)
    stats = [jnp.zeros((tokens, HEAD_DIM), F32)] * RANKS
    for u in range(SPAN):
        r = slice(u * tokens, (u + 1) * tokens)
        block = slice((2 * SPAN + u) * tokens, (2 * SPAN + u + 1) * tokens)
        keys = jnp.concatenate([ref[u * tokens : (u + 1) * tokens] for ref in kvs], axis=0)
        vals = jnp.concatenate([ref[(SPAN + u) * tokens : (SPAN + u + 1) * tokens] for ref in kvs], axis=0)
        for s in range(0, RANKS, 2):
            q = jnp.concatenate([qs[s][block], qs[s + 1][block]], axis=0)
            mixed, logs = attend(q, keys, vals)
            mixed = mixed.astype(BF16)
            for d in range(2):
                half = slice(d * tokens, (d + 1) * tokens)
                outs[s + d][r] = mixed[half]
                stats[s + d] = jnp.where(lane == u, logs[half], stats[s + d])
    for d in range(RANKS):
        turned = jnp.transpose(packed(stats[d], 4))[0:STAT_ROWS]
        outs[d][SPAN * tokens : SPAN * tokens + STAT_ROWS] = turned.astype(BF16)


def temporal_kernel(x_ref, *refs):
    scale_hbm, shift_hbm, wq_hbm, wk_hbm, bias_hbm, wv_hbm, out_hbm = refs[:7]
    scale_ref, shift_ref, wq_ref, wk_ref, bias_ref, wv_ref, out_ref, sems, out_sems = refs[7:]
    held = (scale_ref, shift_ref, wq_ref, wk_ref, bias_ref, wv_ref)
    loads = []
    for n, (src, dst) in enumerate(zip(refs[:6], held)):
        loads.append(pltpu.make_async_copy(src, dst, sems.at[n]))
        loads[n].start()
    groups, rows, width = x_ref.shape
    low = lax.broadcasted_iota(jnp.int32, (groups, rows, width), 1) < rows // 2

    def spread(ref):
        first = jnp.broadcast_to(ref[:, 0:1, :], low.shape)
        return jnp.where(low, first, jnp.broadcast_to(ref[:, 1:2, :], low.shape))

    loads[0].wait()
    loads[1].wait()
    normed = normalise(x_ref[...].astype(F32), spread(scale_ref), spread(shift_ref))
    normed = normed.reshape(groups * rows, width)
    loads[2].wait()
    q = matmul(normed, wq_ref[...]).astype(BF16)
    loads[3].wait()
    k = matmul(normed, wk_ref[...]).astype(BF16)
    loads[4].wait()
    lane = lax.broadcasted_iota(jnp.int32, (groups * rows, HEAD_DIM), 1)
    stats = jnp.zeros((groups * rows, HEAD_DIM), F32)
    heads = [slice(h * HEAD_DIM, (h + 1) * HEAD_DIM) for h in range(HEADS)]
    loads[5].wait()
    v = matmul(normed, wv_ref[...]).astype(BF16)
    parts = [softmax_parts(q[:, own], k[:, own], bias_ref[...]) for own in heads]
    copies = []

    def send(n):
        c = pl.ds(n * HEAD_DIM, HEAD_DIM)
        copies.append(pltpu.make_async_copy(out_ref.at[:, c], out_hbm.at[:, c], out_sems.at[n]))
        copies[n].start()

    for h, (own, (weights, total, top)) in enumerate(zip(heads, parts)):
        mixed, logs = finish(weights, total, top, v[:, own], True)
        out_ref[:, own] = mixed.astype(BF16)
        send(h)
        stats = jnp.where(lane == h, logs, stats)
    out_ref[:, HEADS * HEAD_DIM :] = packed(stats, 8).astype(BF16)
    send(HEADS)
    for copy in copies:
        copy.wait()


def reorder_kernel(time_ref, wo_hbm, own_hbm, far_ref, logs_ref, wo_ref, own_ref, sems):
    loads = []
    for n, (src, dst) in enumerate(((wo_hbm, wo_ref), (own_hbm, own_ref))):
        loads.append(pltpu.make_async_copy(src, dst, sems.at[n]))
        loads[n].start()
    frames, tokens, inner = far_ref.shape
    width = time_ref.shape[1]
    turned = time_ref[...].astype(F32).reshape(tokens // 8, 2, 8, width)
    for f, rows in enumerate(swap_halves(turned[:, 0], turned[:, 1])):
        rows = rows.reshape(tokens, width)
        far_ref[f] = rows[:, :inner].astype(BF16)
        stats = rows[:, inner:]
        logs_ref[f, :, 0:8] = stats[:, 0:8] + stats[:, 8:16] + stats[:, 16:24]
    for load in loads:
        load.wait()


def merged(f, rank, near_refs, far_ref, logs_ref, space_ref, out_ref):
    for d, ref in enumerate(near_refs):
        space_ref[rank ^ d] = ref[...]
    tokens = out_ref.shape[0]
    time_log = logs_ref[f, :, 0:8]
    log_rows = []
    for h in range(HEADS):
        st = space_ref[2 * f + h // SPAN, SPAN * tokens : SPAN * tokens + STAT_ROWS].astype(F32)
        b = h % SPAN
        log_rows.append(st[b : b + 1] + st[b + 4 : b + 5] + st[b + 8 : b + 9])
    log_rows.append(jnp.zeros((8 - HEADS, HEAD_DIM), F32))
    space_log = jnp.transpose(jnp.concatenate(log_rows, axis=0))
    of_space = 1.0 / (1.0 + jnp.exp2(time_log - space_log))
    of_time = 1.0 / (1.0 + jnp.exp2(space_log - time_log))
    for h in range(HEADS):
        own = slice(h * HEAD_DIM, (h + 1) * HEAD_DIM)
        u = h % SPAN
        near = space_ref[2 * f + h // SPAN, u * tokens : (u + 1) * tokens].astype(F32)
        far = far_ref[f, :, own].astype(F32)
        mixed = of_space[:, h : h + 1] * near + of_time[:, h : h + 1] * far
        out_ref[:, own] = mixed.astype(BF16)


def first_kernel(place_ref, mark_ref, *refs):
    del mark_ref
    near_refs, (far_ref, logs_ref, sent_ref, first_ref, space_ref) = refs[:RANKS], refs[RANKS:]
    merged(0, place_ref[1], near_refs, far_ref, logs_ref, space_ref, first_ref)
    sent_ref[...] = first_ref[...]


def project_kernel(place_ref, size_ref, *refs):
    near_refs = refs[:RANKS]
    far_ref, logs_ref, first_ref, wo_ref, own_ref, in_ref, x_hbm, fresh_hbm = refs[RANKS : RANKS + 8]
    vel_hbm, next_hbm, base_ref = refs[RANKS + 8 : RANKS + 11]
    space_ref, second_ref, x_ref, fresh_ref, vel_ref, next_ref, sems, vel_sems, next_sems = refs[RANKS + 11 :]
    frames, tokens, _ = x_ref.shape
    loads = []
    for n, (src, dst) in enumerate(
        (
            (x_hbm, x_ref),
            (fresh_hbm, fresh_ref),
        )
    ):
        loads.append(pltpu.make_async_copy(src, dst, sems.at[n]))
        loads[n].start()

    merged(1, place_ref[1], near_refs, far_ref, logs_ref, space_ref, second_ref)
    attended = jnp.concatenate([first_ref[...], second_ref[...]], axis=0)
    for load in loads:
        load.wait()

    base_ref[...] = jnp.where(place_ref[0] == place_ref[2], fresh_ref[...], in_ref[...])
    chunks = vel_sems.shape[0]
    width = vel_ref.shape[2] // chunks
    copies = []
    for n in range(chunks):
        c, d = slice(n * width, (n + 1) * width), pl.ds(n * width, width)
        projected = matmul(attended, wo_ref[:, c])
        for f in range(frames):
            moving = projected[f * tokens : (f + 1) * tokens] * own_ref[6 + f : 7 + f, c]
            vel_ref[f, :, c] = moving.astype(BF16)
            if f > 0:
                advanced = x_ref[f, :, c].astype(F32) + size_ref[f] * moving
                next_ref[f - 1, :, c] = advanced.astype(BF16)
        copies.append(pltpu.make_async_copy(vel_ref.at[:, :, d], vel_hbm.at[:, :, d], vel_sems.at[n]))
        copies[-1].start()
        filled = next_hbm.at[pl.ds(0, frames - 1), :, d]
        copies.append(pltpu.make_async_copy(next_ref.at[:, :, d], filled, next_sems.at[n]))
        copies[-1].start()
    for copy in copies:
        copy.wait()


def last_kernel(size_ref, att_ref, wo_ref, own_ref, base_ref, kept_ref, next_ref, out_ref, sems):
    del kept_ref
    slot = next_ref.shape[0] - 1
    chunks = sems.shape[0]
    width = out_ref.shape[1] // chunks
    copies = []
    for n in range(chunks):
        c, d = slice(n * width, (n + 1) * width), pl.ds(n * width, width)
        moving = matmul(att_ref[...], wo_ref[:, c]) * own_ref[8:9, c]
        out_ref[:, c] = (base_ref[:, c].astype(F32) + size_ref[2] * moving).astype(BF16)
        copies.append(pltpu.make_async_copy(out_ref.at[:, d], next_ref.at[slot, :, d], sems.at[n]))
        copies[n].start()
    for copy in copies:
        copy.wait()


def whole():
    return pl.BlockSpec(memory_space=pltpu.VMEM)


def scalar():
    return pl.BlockSpec(memory_space=pltpu.SMEM)


def anywhere():
    return pl.BlockSpec(memory_space=pl.ANY)


def pinned(x):
    return pltpu.with_memory_space_constraint(x, pltpu.VMEM)


def in_hbm(x):
    return pltpu.with_memory_space_constraint(x, pltpu.HBM)


def call(kernel, args, in_specs, outs, out_specs, flops=0, nbytes=0, vmem=20, **more):
    return pl.pallas_call(
        kernel,
        out_shape=outs,
        in_specs=in_specs,
        out_specs=out_specs,
        compiler_params=pltpu.CompilerParams(vmem_limit_bytes=vmem * MIB),
        cost_estimate=pl.CostEstimate(flops=flops, bytes_accessed=nbytes, transcendentals=0),
        **more,
    )(*args)


def body(
    latents,
    fresh_noise,
    noise_levels,
    offset,
    block_ids,
    mod_table,
    step_sizes,
    w_query,
    w_key,
    w_value,
    w_out,
):
    frames, tokens, width = latents.shape
    times = lax.axis_size("tm")
    ranks = lax.axis_size("tok")
    share = tokens // times
    total = frames * times
    inner = HEADS * HEAD_DIM
    sds = jax.ShapeDtypeStruct
    dma = pltpu.SemaphoreType.DMA
    back_perm = [(i, i - 1) for i in range(1, times)]
    project_flops = 2 * frames * tokens * width * inner

    def exchange(x, d):
        pairs = []
        for tm in range(times):
            for tok in range(ranks):
                side, y, core = tok // RANKS, tok % RANKS, tm % 2
                pairs.append((tm * ranks + tok, (tm - core + side) * ranks + core * RANKS + (y ^ d)))
        return lax.ppermute(x, ("tm", "tok"), pairs)

    outgoing, incoming, x = call(
        shuffle_kernel,
        (in_hbm(latents),),
        [anywhere()],
        (
            pltpu.HBM((tokens // 8, 2, 8, width), BF16),
            pltpu.HBM((tokens, width), BF16),
            pltpu.VMEM((frames, tokens, width), BF16),
        ),
        (anywhere(), anywhere(), whole()),
        nbytes=2 * MIB,
        scratch_shapes=[pltpu.VMEM((tokens // 8, 2, 8, width), BF16), dma((8,)), dma((8,)), dma],
    )
    column = lax.all_to_all(outgoing.reshape(times, frames * share, width), "tm", 0, 0)

    place = lax.axis_index("tm").astype(jnp.int32)
    rank = lax.axis_index("tok").astype(jnp.int32) % RANKS
    place = jnp.stack([place, rank, jnp.int32(times - 1)])
    table = mod_table.transpose(1, 0, 2)
    small = (
        pltpu.VMEM((16, width), F32),
        pltpu.VMEM((times, frames, width), F32),
        pltpu.VMEM((times, frames, width), F32),
        pltpu.VMEM((total * share, total * share), F32),
    )
    sizes, own, shifts, scales, bias, *parts = call(
        home_kernel,
        (
            noise_levels,
            offset,
            step_sizes,
            block_ids,
            place,
            pinned(x),
            *[in_hbm(a) for a in (table, w_query, w_key, w_value)],
        ),
        [scalar()] * 5 + [whole()] + [anywhere()] * 4,
        (
            sds((frames + 1,), F32),
            *[pltpu.HBM(a.inner_aval.shape, F32) for a in small],
            *[sds((3 * SPAN * tokens, HEAD_DIM), BF16)] * RANKS,
        ),
        (scalar(), *[anywhere()] * 4, *[whole()] * RANKS),
        flops=LONG,
        nbytes=10 * MIB,
        scratch_shapes=[
            pltpu.VMEM(table.shape, F32),
            *[pltpu.VMEM((frames * tokens, inner), BF16)] * 3,
            *[pltpu.VMEM((width, inner), BF16)] * 3,
            *small,
            dma((4,)),
            dma((4,)),
        ],
    )
    units = [exchange(part, d) for d, part in enumerate(parts)]

    incoming, sizes = lax.optimization_barrier((incoming, sizes))
    next_latents = lax.ppermute(incoming, "tm", back_perm)

    back = call(
        temporal_kernel,
        (column, *[in_hbm(a) for a in (scales, shifts, w_query, w_key, bias, w_value)]),
        [whole()] + [anywhere()] * 6,
        pltpu.HBM((total * share, inner + HEAD_DIM), BF16),
        anywhere(),
        flops=LONG,
        nbytes=10 * MIB,
        scratch_shapes=[
            *small[1:3],
            *[pltpu.VMEM((width, inner), BF16)] * 2,
            small[3],
            pltpu.VMEM((width, inner), BF16),
            pltpu.VMEM((total * share, inner + HEAD_DIM), BF16),
            dma((6,)),
            dma((HEADS + 1,)),
        ],
    )
    mark = step_sizes.reshape(1, -1)
    _, next_latents, mark, *units = lax.optimization_barrier((back, next_latents, mark, *units))
    mark = call(pass_kernel, (mark,), [whole()], sds(mark.shape, F32), whole(), flops=PAUSE)
    mark, *units = lax.optimization_barrier((mark, *units))
    sibling = [lax.ppermute(part, "tm", [(i, i ^ 1) for i in range(times)]) for part in units]
    back = lax.all_to_all(back.reshape(times, frames * share, inner + HEAD_DIM), "tm", 0, 0)
    back = back.reshape(times * frames * share, inner + HEAD_DIM)

    near = call(
        spatial_kernel,
        (*units, *sibling),
        [whole()] * (2 * RANKS),
        [sds((SPAN * tokens + STAT_ROWS, HEAD_DIM), BF16)] * RANKS,
        [whole()] * RANKS,
        flops=4 * SPAN * RANKS * ranks * tokens * tokens * HEAD_DIM,
        nbytes=3 * MIB,
    )
    near = [exchange(part, d) for d, part in enumerate(near)]

    space = pltpu.VMEM((RANKS, SPAN * tokens + STAT_ROWS, HEAD_DIM), BF16)
    far, logs, wo, own = call(
        reorder_kernel,
        (back, in_hbm(w_out), in_hbm(own)),
        [whole()] + [anywhere()] * 2,
        (
            pltpu.VMEM((frames, tokens, inner), BF16),
            pltpu.VMEM((frames, tokens, HEAD_DIM), F32),
            pltpu.VMEM((inner, width), BF16),
            pltpu.VMEM((16, width), F32),
        ),
        (whole(),) * 4,
        scratch_shapes=[dma((2,))],
        flops=LONG,
        nbytes=MIB,
    )
    sent, first = call(
        first_kernel,
        (place, mark, *near, pinned(far), pinned(logs)),
        [scalar()] + [whole()] * (RANKS + 3),
        (sds((tokens, inner), BF16), pltpu.VMEM((tokens, inner), BF16)),
        (whole(), whole()),
        nbytes=2 * MIB,
        scratch_shapes=[space],
    )
    next_first = lax.ppermute(sent, "tm", back_perm)
    velocity, following, base = call(
        project_kernel,
        (
            place,
            sizes,
            *near,
            pinned(far),
            pinned(logs),
            pinned(first),
            pinned(wo),
            pinned(own),
            next_latents,
            in_hbm(latents),
            in_hbm(fresh_noise),
        ),
        [scalar()] * 2 + [whole()] * (RANKS + 6) + [anywhere()] * 2,
        (
            pltpu.HBM((frames, tokens, width), BF16),
            pltpu.HBM((frames, tokens, width), BF16),
            pltpu.VMEM((tokens, width), BF16),
        ),
        (anywhere(), anywhere(), whole()),
        flops=project_flops,
        nbytes=6 * MIB,
        scratch_shapes=[
            space,
            pltpu.VMEM((tokens, inner), BF16),
            pltpu.VMEM((frames, tokens, width), BF16),
            pltpu.VMEM((tokens, width), BF16),
            pltpu.VMEM((frames, tokens, width), BF16),
            pltpu.VMEM((frames - 1, tokens, width), BF16),
            dma((2,)),
            *[dma((3,))] * 2,
        ],
    )
    following = call(
        last_kernel,
        (sizes, next_first, pinned(wo), pinned(own), pinned(base), following),
        [scalar()] + [whole()] * 4 + [anywhere()],
        sds((frames, tokens, width), BF16),
        anywhere(),
        flops=project_flops // 2,
        nbytes=4 * MIB,
        scratch_shapes=[pltpu.VMEM((tokens, width), BF16), dma((3,))],
        input_output_aliases={5: 0},
    )
    return velocity, following


def solution(mesh):
    in_specs = (P("tm", "tok", None), P("tok", None), P(), P(), P(), P(), P(), P(), P(), P(), P())
    out_specs = (P("tm", "tok", None), P("tm", "tok", None))
    return jax.shard_map(body, mesh=mesh, in_specs=in_specs, out_specs=out_specs, check_vma=False)
```

```python
import math

import jax
import jax.numpy as jnp
from jax import lax
from jax.experimental import pallas as pl
from jax.experimental.pallas import tpu as pltpu
from jax.sharding import PartitionSpec as P

HEAD_DIM = 128
HEADS = 6
SPAN = 3
RANKS = 4
BASE2 = HEAD_DIM ** (-0.5) * math.log2(math.e)
MASKED = -1e30
FLOOR = -1e29
MIB = 1 << 20
STAT_ROWS = 16
PAUSE = 3_500_000_000
LONG = 60_000_000_000
BF16 = jnp.bfloat16
F32 = jnp.float32


def normalise(x, scale1, shift):
    values = x.astype(F32)
    center = jnp.mean(values, axis=-1, keepdims=True)
    values = values - center
    spread = jnp.mean(values * values, axis=-1, keepdims=True)
    return (values * lax.rsqrt(spread + 1e-06) * scale1 + shift).astype(BF16)


def matmul(a, b):
    return jnp.dot(a, b, preferred_element_type=F32)


def softmax_parts(q, k, bias=None):
    scores = lax.dot_general(q, k, (((1,), (1,)), ((), ())), preferred_element_type=F32)
    if bias is not None:
        scores = scores + bias
    top = jnp.max(scores, axis=-1, keepdims=True)
    if bias is not None:
        top = jnp.maximum(top, FLOOR)
    weights = jnp.exp2((scores - top) * BASE2)
    return weights.astype(BF16), jnp.sum(weights, axis=-1, keepdims=True), top


def finish(weights, total, top, v, may_be_empty):
    mixed = matmul(weights, v)
    if not may_be_empty:
        return mixed * (1.0 / total), top * BASE2 + jnp.log2(total)
    some = total > 0.0
    safe = jnp.where(some, total, 1.0)
    return mixed * (1.0 / safe), jnp.where(some, top * BASE2 + jnp.log2(safe), MASKED)


def attend(q, k, v):
    return finish(*softmax_parts(q, k), v, False)


def split3(x):
    one = x.astype(BF16).astype(F32)
    rest = x - one
    two = rest.astype(BF16).astype(F32)
    return one, two, rest - two


def packed(tile, step):
    one, two, three = split3(tile)
    return one + pltpu.roll(two, step, 1) + pltpu.roll(three, 2 * step, 1)


def swap_halves(even, odd):
    low = lax.broadcasted_iota(jnp.int32, even.shape, 1) < 4
    return jnp.where(low, even, pltpu.roll(odd, 4, 1)), jnp.where(low, pltpu.roll(even, 4, 1), odd)


def shuffle_kernel(x_hbm, out_hbm, first_hbm, x_ref, mixed_ref, in_sems, out_sems, first_sem):
    _, tokens, width = x_ref.shape
    chunks = in_sems.shape[0]
    rows = tokens // chunks
    pairs = rows // 8
    ins, outs = [], []
    for c in range(chunks):
        r = pl.ds(c * rows, rows)
        ins.append(pltpu.make_async_copy(x_hbm.at[:, r], x_ref.at[:, r], in_sems.at[c]))
        ins[c].start()
    for c in range(chunks):
        ins[c].wait()
        first, second = [
            x_ref[f, c * rows : (c + 1) * rows].astype(F32).reshape(pairs, 8, width) for f in range(2)
        ]
        even, odd = swap_halves(first, second)
        mixed_ref[c * pairs : (c + 1) * pairs, 0] = even.astype(BF16)
        mixed_ref[c * pairs : (c + 1) * pairs, 1] = odd.astype(BF16)
        r = pl.ds(c * pairs, pairs)
        outs.append(pltpu.make_async_copy(mixed_ref.at[r], out_hbm.at[r], out_sems.at[c]))
        outs[c].start()
    outs.append(pltpu.make_async_copy(x_ref.at[0], first_hbm, first_sem))
    outs[-1].start()
    for copy in outs:
        copy.wait()


def home_kernel(
    noise_ref,
    offset_ref,
    step_ref,
    blocks_ref,
    place_ref,
    x_ref,
    table_hbm,
    wq_hbm,
    wk_hbm,
    wv_hbm,
    size_ref,
    own_hbm,
    shift_hbm,
    scale_hbm,
    bias_hbm,
    *refs,
):
    outs = refs[:RANKS]
    table_ref, q_ref, k_ref, v_ref, wq_ref, wk_ref, wv_ref, *refs = refs[RANKS:]
    own_ref, shift_ref, scale_ref, bias_ref, sems, store_sems = refs
    loads = []
    for n, (src, dst) in enumerate(
        ((table_hbm, table_ref), (wq_hbm, wq_ref), (wk_hbm, wk_ref), (wv_hbm, wv_ref))
    ):
        loads.append(pltpu.make_async_copy(src, dst, sems.at[n]))
        loads[n].start()
    frames, tokens, _ = x_ref.shape
    total = noise_ref.shape[0]
    loads[0].wait()
    for n in range(frames + 1):
        frame = jnp.minimum(place_ref[0] * frames + n, total - 1)
        level = noise_ref[lax.rem(frame + offset_ref[0], total)]
        size_ref[n] = step_ref[level]
        own_ref[n : n + 1, :] = table_ref[0, pl.ds(level, 1), :]
        own_ref[n + 3 : n + 4, :] = table_ref[1, pl.ds(level, 1), :] + 1.0
        own_ref[n + 6 : n + 7, :] = table_ref[2, pl.ds(level, 1), :]
    stores = [
        pltpu.make_async_copy(src, dst, store_sems.at[n])
        for n, (src, dst) in enumerate(
            ((own_ref, own_hbm), (shift_ref, shift_hbm), (scale_ref, scale_hbm), (bias_ref, bias_hbm))
        )
    ]
    stores[0].start()
    share = bias_ref.shape[0] // total
    for f in range(total):
        level = noise_ref[lax.rem(f + offset_ref[0], total)]
        shift_ref[f // frames, f % frames : f % frames + 1, :] = table_ref[0, pl.ds(level, 1), :]
        scale_ref[f // frames, f % frames : f % frames + 1, :] = table_ref[1, pl.ds(level, 1), :] + 1.0
    stores[1].start()
    stores[2].start()
    wide = (8, total * share)
    lane = lax.broadcasted_iota(jnp.int32, wide, 1) // share
    block = jnp.zeros(wide, F32)
    for f in range(total):
        block = jnp.where(lane == f, blocks_ref[f].astype(F32), block)
    block = jnp.broadcast_to(block[0:1], bias_ref.shape)
    down = lax.broadcasted_iota(jnp.int32, bias_ref.shape, 0)
    along = lax.broadcasted_iota(jnp.int32, bias_ref.shape, 1)
    allowed = (down % share == along % share) & (down != along) & (block <= jnp.transpose(block))
    bias_ref[...] = jnp.where(allowed, 0.0, MASKED)
    stores[3].start()
    normed = []
    for f in range(frames):
        normed.append(normalise(x_ref[f], own_ref[f + 3 : f + 4, :], own_ref[f : f + 1, :]))
    normed = jnp.concatenate(normed, axis=0)
    for n, (ref, w) in enumerate(((q_ref, wq_ref), (k_ref, wk_ref), (v_ref, wv_ref))):
        loads[1 + n].wait()
        ref[...] = matmul(normed, w[...]).astype(BF16)
    for d in range(RANKS):
        other = place_ref[1] ^ d
        r = pl.ds(pl.multiple_of((other // 2) * tokens, tokens), tokens)
        for u in range(SPAN):
            c = pl.ds(pl.multiple_of((other % 2) * SPAN * HEAD_DIM + u * HEAD_DIM, HEAD_DIM), HEAD_DIM)
            for n, ref in enumerate((k_ref, v_ref, q_ref)):
                block = slice((n * SPAN + u) * tokens, (n * SPAN + u + 1) * tokens)
                outs[d][block] = ref[r, c]
    for store in stores:
        store.wait()


def pass_kernel(in_ref, out_ref):
    out_ref[...] = in_ref[...]


def spatial_kernel(*refs):
    kvs, qs, outs = refs[: 2 * RANKS], refs[:RANKS], refs[2 * RANKS :]
    tokens = HEAD_DIM
    lane = lax.broadcasted_iota(jnp.int32, (tokens, HEAD_DIM), 1)
    stats = [jnp.zeros((tokens, HEAD_DIM), F32)] * RANKS
    for u in range(SPAN):
        r = slice(u * tokens, (u + 1) * tokens)
        block = slice((2 * SPAN + u) * tokens, (2 * SPAN + u + 1) * tokens)
        keys = jnp.concatenate([ref[u * tokens : (u + 1) * tokens] for ref in kvs], axis=0)
        vals = jnp.concatenate([ref[(SPAN + u) * tokens : (SPAN + u + 1) * tokens] for ref in kvs], axis=0)
        for s in range(0, RANKS, 2):
            q = jnp.concatenate([qs[s][block], qs[s + 1][block]], axis=0)
            mixed, logs = attend(q, keys, vals)
            mixed = mixed.astype(BF16)
            for d in range(2):
                half = slice(d * tokens, (d + 1) * tokens)
                outs[s + d][r] = mixed[half]
                stats[s + d] = jnp.where(lane == u, logs[half], stats[s + d])
    for d in range(RANKS):
        turned = jnp.transpose(packed(stats[d], 4))[0:STAT_ROWS]
        outs[d][SPAN * tokens : SPAN * tokens + STAT_ROWS] = turned.astype(BF16)


def temporal_kernel(x_ref, *refs):
    scale_hbm, shift_hbm, wq_hbm, wk_hbm, bias_hbm, wv_hbm, out_hbm = refs[:7]
    scale_ref, shift_ref, wq_ref, wk_ref, bias_ref, wv_ref, out_ref, sems, out_sems = refs[7:]
    held = (scale_ref, shift_ref, wq_ref, wk_ref, bias_ref, wv_ref)
    loads = []
    for n, (src, dst) in enumerate(zip(refs[:6], held)):
        loads.append(pltpu.make_async_copy(src, dst, sems.at[n]))
        loads[n].start()
    groups, rows, width = x_ref.shape
    low = lax.broadcasted_iota(jnp.int32, (groups, rows, width), 1) < rows // 2

    def spread(ref):
        first = jnp.broadcast_to(ref[:, 0:1, :], low.shape)
        return jnp.where(low, first, jnp.broadcast_to(ref[:, 1:2, :], low.shape))

    loads[0].wait()
    loads[1].wait()
    normed = normalise(x_ref[...].astype(F32), spread(scale_ref), spread(shift_ref))
    normed = normed.reshape(groups * rows, width)
    loads[2].wait()
    q = matmul(normed, wq_ref[...]).astype(BF16)
    loads[3].wait()
    k = matmul(normed, wk_ref[...]).astype(BF16)
    loads[4].wait()
    lane = lax.broadcasted_iota(jnp.int32, (groups * rows, HEAD_DIM), 1)
    stats = jnp.zeros((groups * rows, HEAD_DIM), F32)
    heads = [slice(h * HEAD_DIM, (h + 1) * HEAD_DIM) for h in range(HEADS)]
    loads[5].wait()
    v = matmul(normed, wv_ref[...]).astype(BF16)
    parts = [softmax_parts(q[:, own], k[:, own], bias_ref[...]) for own in heads]
    copies = []

    def send(n):
        c = pl.ds(n * HEAD_DIM, HEAD_DIM)
        copies.append(pltpu.make_async_copy(out_ref.at[:, c], out_hbm.at[:, c], out_sems.at[n]))
        copies[n].start()

    for h, (own, (weights, total, top)) in enumerate(zip(heads, parts)):
        mixed, logs = finish(weights, total, top, v[:, own], True)
        out_ref[:, own] = mixed.astype(BF16)
        send(h)
        stats = jnp.where(lane == h, logs, stats)
    out_ref[:, HEADS * HEAD_DIM :] = packed(stats, 8).astype(BF16)
    send(HEADS)
    for copy in copies:
        copy.wait()


def reorder_kernel(time_ref, wo_hbm, own_hbm, far_ref, logs_ref, wo_ref, own_ref, sems):
    loads = []
    for n, (src, dst) in enumerate(((wo_hbm, wo_ref), (own_hbm, own_ref))):
        loads.append(pltpu.make_async_copy(src, dst, sems.at[n]))
        loads[n].start()
    frames, tokens, inner = far_ref.shape
    width = time_ref.shape[1]
    turned = time_ref[...].astype(F32).reshape(tokens // 8, 2, 8, width)
    for f, rows in enumerate(swap_halves(turned[:, 0], turned[:, 1])):
        rows = rows.reshape(tokens, width)
        far_ref[f] = rows[:, :inner].astype(BF16)
        stats = rows[:, inner:]
        logs_ref[f, :, 0:8] = stats[:, 0:8] + stats[:, 8:16] + stats[:, 16:24]
    for load in loads:
        load.wait()


def merged(f, rank, near_refs, far_ref, logs_ref, space_ref, out_ref):
    for d, ref in enumerate(near_refs):
        space_ref[rank ^ d] = ref[...]
    tokens = out_ref.shape[0]
    time_log = logs_ref[f, :, 0:8]
    log_rows = []
    for h in range(HEADS):
        st = space_ref[2 * f + h // SPAN, SPAN * tokens : SPAN * tokens + STAT_ROWS].astype(F32)
        b = h % SPAN
        log_rows.append(st[b : b + 1] + st[b + 4 : b + 5] + st[b + 8 : b + 9])
    log_rows.append(jnp.zeros((8 - HEADS, HEAD_DIM), F32))
    space_log = jnp.transpose(jnp.concatenate(log_rows, axis=0))
    of_space = 1.0 / (1.0 + jnp.exp2(time_log - space_log))
    of_time = 1.0 / (1.0 + jnp.exp2(space_log - time_log))
    for h in range(HEADS):
        own = slice(h * HEAD_DIM, (h + 1) * HEAD_DIM)
        u = h % SPAN
        near = space_ref[2 * f + h // SPAN, u * tokens : (u + 1) * tokens].astype(F32)
        far = far_ref[f, :, own].astype(F32)
        mixed = of_space[:, h : h + 1] * near + of_time[:, h : h + 1] * far
        out_ref[:, own] = mixed.astype(BF16)


def first_kernel(place_ref, mark_ref, *refs):
    del mark_ref
    near_refs, (far_ref, logs_ref, sent_ref, first_ref, space_ref) = refs[:RANKS], refs[RANKS:]
    merged(0, place_ref[1], near_refs, far_ref, logs_ref, space_ref, first_ref)
    sent_ref[...] = first_ref[...]


def project_kernel(place_ref, size_ref, *refs):
    near_refs = refs[:RANKS]
    far_ref, logs_ref, first_ref, wo_ref, own_ref, in_ref, x_hbm, fresh_hbm = refs[RANKS : RANKS + 8]
    vel_hbm, next_hbm, base_ref = refs[RANKS + 8 : RANKS + 11]
    space_ref, second_ref, x_ref, fresh_ref, vel_ref, next_ref, sems, vel_sems, next_sems = refs[RANKS + 11 :]
    frames, tokens, _ = x_ref.shape
    loads = []
    for n, (src, dst) in enumerate(
        (
            (x_hbm, x_ref),
            (fresh_hbm, fresh_ref),
        )
    ):
        loads.append(pltpu.make_async_copy(src, dst, sems.at[n]))
        loads[n].start()

    merged(1, place_ref[1], near_refs, far_ref, logs_ref, space_ref, second_ref)
    attended = jnp.concatenate([first_ref[...], second_ref[...]], axis=0)
    for load in loads:
        load.wait()

    base_ref[...] = jnp.where(place_ref[0] == place_ref[2], fresh_ref[...], in_ref[...])
    chunks = vel_sems.shape[0]
    width = vel_ref.shape[2] // chunks
    copies = []
    for n in range(chunks):
        c, d = slice(n * width, (n + 1) * width), pl.ds(n * width, width)
        projected = matmul(attended, wo_ref[:, c])
        for f in range(frames):
            moving = projected[f * tokens : (f + 1) * tokens] * own_ref[6 + f : 7 + f, c]
            vel_ref[f, :, c] = moving.astype(BF16)
            if f > 0:
                advanced = x_ref[f, :, c].astype(F32) + size_ref[f] * moving
                next_ref[f - 1, :, c] = advanced.astype(BF16)
        copies.append(pltpu.make_async_copy(vel_ref.at[:, :, d], vel_hbm.at[:, :, d], vel_sems.at[n]))
        copies[-1].start()
        filled = next_hbm.at[pl.ds(0, frames - 1), :, d]
        copies.append(pltpu.make_async_copy(next_ref.at[:, :, d], filled, next_sems.at[n]))
        copies[-1].start()
    for copy in copies:
        copy.wait()


def last_kernel(size_ref, att_ref, wo_ref, own_ref, base_ref, kept_ref, next_ref, out_ref, sems):
    del kept_ref
    slot = next_ref.shape[0] - 1
    chunks = sems.shape[0]
    width = out_ref.shape[1] // chunks
    copies = []
    for n in range(chunks):
        c, d = slice(n * width, (n + 1) * width), pl.ds(n * width, width)
        moving = matmul(att_ref[...], wo_ref[:, c]) * own_ref[8:9, c]
        out_ref[:, c] = (base_ref[:, c].astype(F32) + size_ref[2] * moving).astype(BF16)
        copies.append(pltpu.make_async_copy(out_ref.at[:, d], next_ref.at[slot, :, d], sems.at[n]))
        copies[n].start()
    for copy in copies:
        copy.wait()


def whole():
    return pl.BlockSpec(memory_space=pltpu.VMEM)


def scalar():
    return pl.BlockSpec(memory_space=pltpu.SMEM)


def anywhere():
    return pl.BlockSpec(memory_space=pl.ANY)


def pinned(x):
    return pltpu.with_memory_space_constraint(x, pltpu.VMEM)


def in_hbm(x):
    return pltpu.with_memory_space_constraint(x, pltpu.HBM)


def call(kernel, args, in_specs, outs, out_specs, flops=0, nbytes=0, vmem=20, **more):
    return pl.pallas_call(
        kernel,
        out_shape=outs,
        in_specs=in_specs,
        out_specs=out_specs,
        compiler_params=pltpu.CompilerParams(vmem_limit_bytes=vmem * MIB),
        cost_estimate=pl.CostEstimate(flops=flops, bytes_accessed=nbytes, transcendentals=0),
        **more,
    )(*args)


def body(
    latents,
    fresh_noise,
    noise_levels,
    offset,
    block_ids,
    mod_table,
    step_sizes,
    w_query,
    w_key,
    w_value,
    w_out,
):
    frames, tokens, width = latents.shape
    times = lax.axis_size("tm")
    ranks = lax.axis_size("tok")
    share = tokens // times
    total = frames * times
    inner = HEADS * HEAD_DIM
    sds = jax.ShapeDtypeStruct
    dma = pltpu.SemaphoreType.DMA
    back_perm = [(i, i - 1) for i in range(1, times)]
    project_flops = 2 * frames * tokens * width * inner

    def exchange(x, d):
        pairs = []
        for tm in range(times):
            for tok in range(ranks):
                side, y, core = tok // RANKS, tok % RANKS, tm % 2
                pairs.append((tm * ranks + tok, (tm - core + side) * ranks + core * RANKS + (y ^ d)))
        return lax.ppermute(x, ("tm", "tok"), pairs)

    outgoing, incoming, x = call(
        shuffle_kernel,
        (in_hbm(latents),),
        [anywhere()],
        (
            pltpu.HBM((tokens // 8, 2, 8, width), BF16),
            pltpu.HBM((tokens, width), BF16),
            pltpu.VMEM((frames, tokens, width), BF16),
        ),
        (anywhere(), anywhere(), whole()),
        nbytes=2 * MIB,
        scratch_shapes=[pltpu.VMEM((tokens // 8, 2, 8, width), BF16), dma((8,)), dma((8,)), dma],
    )
    column = lax.all_to_all(outgoing.reshape(times, frames * share, width), "tm", 0, 0)

    place = lax.axis_index("tm").astype(jnp.int32)
    rank = lax.axis_index("tok").astype(jnp.int32) % RANKS
    place = jnp.stack([place, rank, jnp.int32(times - 1)])
    table = mod_table.transpose(1, 0, 2)
    small = (
        pltpu.VMEM((16, width), F32),
        pltpu.VMEM((times, frames, width), F32),
        pltpu.VMEM((times, frames, width), F32),
        pltpu.VMEM((total * share, total * share), F32),
    )
    sizes, own, shifts, scales, bias, *parts = call(
        home_kernel,
        (
            noise_levels,
            offset,
            step_sizes,
            block_ids,
            place,
            pinned(x),
            *[in_hbm(a) for a in (table, w_query, w_key, w_value)],
        ),
        [scalar()] * 5 + [whole()] + [anywhere()] * 4,
        (
            sds((frames + 1,), F32),
            *[pltpu.HBM(a.inner_aval.shape, F32) for a in small],
            *[sds((3 * SPAN * tokens, HEAD_DIM), BF16)] * RANKS,
        ),
        (scalar(), *[anywhere()] * 4, *[whole()] * RANKS),
        flops=LONG,
        nbytes=10 * MIB,
        scratch_shapes=[
            pltpu.VMEM(table.shape, F32),
            *[pltpu.VMEM((frames * tokens, inner), BF16)] * 3,
            *[pltpu.VMEM((width, inner), BF16)] * 3,
            *small,
            dma((4,)),
            dma((4,)),
        ],
    )
    units = [exchange(part, d) for d, part in enumerate(parts)]

    incoming, sizes = lax.optimization_barrier((incoming, sizes))
    next_latents = lax.ppermute(incoming, "tm", back_perm)

    back = call(
        temporal_kernel,
        (column, *[in_hbm(a) for a in (scales, shifts, w_query, w_key, bias, w_value)]),
        [whole()] + [anywhere()] * 6,
        pltpu.HBM((total * share, inner + HEAD_DIM), BF16),
        anywhere(),
        flops=LONG,
        nbytes=10 * MIB,
        scratch_shapes=[
            *small[1:3],
            *[pltpu.VMEM((width, inner), BF16)] * 2,
            small[3],
            pltpu.VMEM((width, inner), BF16),
            pltpu.VMEM((total * share, inner + HEAD_DIM), BF16),
            dma((6,)),
            dma((HEADS + 1,)),
        ],
    )
    mark = step_sizes.reshape(1, -1)
    _, next_latents, mark, *units = lax.optimization_barrier((back, next_latents, mark, *units))
    mark = call(pass_kernel, (mark,), [whole()], sds(mark.shape, F32), whole(), flops=PAUSE)
    mark, *units = lax.optimization_barrier((mark, *units))
    sibling = [lax.ppermute(part, "tm", [(i, i ^ 1) for i in range(times)]) for part in units]
    back = lax.all_to_all(back.reshape(times, frames * share, inner + HEAD_DIM), "tm", 0, 0)
    back = back.reshape(times * frames * share, inner + HEAD_DIM)

    near = call(
        spatial_kernel,
        (*units, *sibling),
        [whole()] * (2 * RANKS),
        [sds((SPAN * tokens + STAT_ROWS, HEAD_DIM), BF16)] * RANKS,
        [whole()] * RANKS,
        flops=4 * SPAN * RANKS * ranks * tokens * tokens * HEAD_DIM,
        nbytes=3 * MIB,
    )
    near = [exchange(part, d) for d, part in enumerate(near)]

    space = pltpu.VMEM((RANKS, SPAN * tokens + STAT_ROWS, HEAD_DIM), BF16)
    far, logs, wo, own = call(
        reorder_kernel,
        (back, in_hbm(w_out), in_hbm(own)),
        [whole()] + [anywhere()] * 2,
        (
            pltpu.VMEM((frames, tokens, inner), BF16),
            pltpu.VMEM((frames, tokens, HEAD_DIM), F32),
            pltpu.VMEM((inner, width), BF16),
            pltpu.VMEM((16, width), F32),
        ),
        (whole(),) * 4,
        scratch_shapes=[dma((2,))],
        flops=LONG,
        nbytes=MIB,
    )
    sent, first = call(
        first_kernel,
        (place, mark, *near, pinned(far), pinned(logs)),
        [scalar()] + [whole()] * (RANKS + 3),
        (sds((tokens, inner), BF16), pltpu.VMEM((tokens, inner), BF16)),
        (whole(), whole()),
        nbytes=2 * MIB,
        scratch_shapes=[space],
    )
    next_first = lax.ppermute(sent, "tm", back_perm)
    velocity, following, base = call(
        project_kernel,
        (
            place,
            sizes,
            *near,
            pinned(far),
            pinned(logs),
            pinned(first),
            pinned(wo),
            pinned(own),
            next_latents,
            in_hbm(latents),
            in_hbm(fresh_noise),
        ),
        [scalar()] * 2 + [whole()] * (RANKS + 6) + [anywhere()] * 2,
        (
            pltpu.HBM((frames, tokens, width), BF16),
            pltpu.HBM((frames, tokens, width), BF16),
            pltpu.VMEM((tokens, width), BF16),
        ),
        (anywhere(), anywhere(), whole()),
        flops=project_flops,
        nbytes=6 * MIB,
        scratch_shapes=[
            space,
            pltpu.VMEM((tokens, inner), BF16),
            pltpu.VMEM((frames, tokens, width), BF16),
            pltpu.VMEM((tokens, width), BF16),
            pltpu.VMEM((frames, tokens, width), BF16),
            pltpu.VMEM((frames - 1, tokens, width), BF16),
            dma((2,)),
            *[dma((6,))] * 2,
        ],
    )
    following = call(
        last_kernel,
        (sizes, next_first, pinned(wo), pinned(own), pinned(base), following),
        [scalar()] + [whole()] * 4 + [anywhere()],
        sds((frames, tokens, width), BF16),
        anywhere(),
        flops=project_flops // 2,
        nbytes=4 * MIB,
        scratch_shapes=[pltpu.VMEM((tokens, width), BF16), dma((6,))],
        input_output_aliases={5: 0},
    )
    return velocity, following


def solution(mesh):
    in_specs = (P("tm", "tok", None), P("tok", None), P(), P(), P(), P(), P(), P(), P(), P(), P())
    out_specs = (P("tm", "tok", None), P("tm", "tok", None))
    return jax.shard_map(body, mesh=mesh, in_specs=in_specs, out_specs=out_specs, check_vma=False)
```
